32 devices in a mesh: groups: 2 (over x), pool: 2 (over core), tensor: 8 (over z, y).
Axes of the slice: x: 2, y: 2, z: 4, core: 2. Of those that a mesh axis runs over, the one named last changes fastest.
Arguments:
- hidden: bfloat16 [64, 5120], P(('groups', 'pool', 'tensor')), parts along dimension 0, may hold values from -1.5 to 1.5
- input_gain: float32 [5120], replicated, may hold values from 0.1 to 1.9
- query_weight: bfloat16 [5120, 4096], P(None, ('pool', 'tensor')), may hold values from -0.078125 to 0.078125
- key_weight: bfloat16 [5120, 512], P(None, ('pool', 'tensor')), may hold values from -0.078125 to 0.078125
- value_weight: bfloat16 [5120, 512], P(None, ('pool', 'tensor')), may hold values from -0.078125 to 0.078125
- query_gain: float32 [128], replicated, may hold values from 2 to 6
- key_gain: float32 [128], replicated, may hold values from 1 to 4
- output_weight: bfloat16 [4096, 5120], P(('pool', 'tensor')), may hold values from -0.09375 to 0.09375
- post_gain: float32 [5120], replicated, may hold values from 0.1 to 1.9
- gate_weight: bfloat16 [5120, 12800], P(None, ('pool', 'tensor')), may hold values from -0.078125 to 0.078125
- up_weight: bfloat16 [5120, 12800], P(None, ('pool', 'tensor')), may hold values from -0.078125 to 0.078125
- down_weight: bfloat16 [12800, 5120], P(('pool', 'tensor')), may hold values from -0.0546875 to 0.0546875
- key_cache: bfloat16 [65536, 512], P(('groups', 'pool', 'tensor')), parts along dimension 0, may hold values from -45 to 45
- value_cache: bfloat16 [65536, 512], P(('groups', 'pool', 'tensor')), parts along dimension 0, may hold values from -6 to 6
- lengths: int32 [64], P('groups'), parts along dimension 0, may hold values from 128 to 2048, as said below
- request_slot: int32 [64], P('groups'), parts along dimension 0, may hold values from 0 to 63, as said below
Outputs:
- mixed: bfloat16 [64, 5120], P(('groups', 'pool', 'tensor')), parts along dimension 0
- final: bfloat16 [64, 5120], P(('groups', 'pool', 'tensor')), parts along dimension 0
The draws below stay inside these ranges and needn't reach their ends.
There are 2 independent parts, one for each index of `groups`. The reference program is written for one: setup_inputs(seed, part) draws one part's arguments, and reference() takes and returns one part's arrays. A program takes and returns all parts, laid end to end along the dimension named above; an argument that names none is the same for every part. Nothing has to cross between parts.
Inputs may be any that keep to these rules, and one draw needn't show every extreme that they name: `request_slot`: each owner holds at most 4 requests and some owner holds exactly 4; no two requests share a slot. The lengths of one owner's requests sum to at most 2048; some request has exactly 2048 and some exactly 128.
All inputs are finite; a program needn't handle non-finite values.
Results may differ from the reference program's by a relative error of at most 0.03.
The reference program's roundings to bfloat16 on the way count: a program that leaves them out, or rounds other values in their place, can miss the bound.
Values may be sent and summed in bfloat16 or wider, within the bound.
No kernel may reach another device: no remote copies, remote signals or barrier semaphores. Data moves between devices by JAX's collectives and lax.ppermute only.
A program may use at most 64 MiB of HBM per device.

```python
import math
import jax
import jax.numpy as jnp
from jax import lax

D = 5120
HEADS = 32
KV_HEADS = 4
HD = 128
FF = 12800
SLOTS = 4
MAXLEN = 2048
MINLEN = 128
OWNERS = 16
REQ = 32
QD = 4096
KD = 512


def request_layout(key):
    folded = jax.random.fold_in(key, 7)
    key_owner, key_length, key_order = jax.random.split(folded, 3)
    pattern = jnp.tile(jnp.array([4, 1, 2, 1], jnp.int32), OWNERS // 4)
    owner_order = jax.random.permutation(key_owner, OWNERS)
    counts = jnp.zeros((OWNERS,), jnp.int32).at[owner_order].set(pattern)
    slot_ids = jnp.arange(OWNERS * SLOTS, dtype=jnp.int32)
    usable = slot_ids % SLOTS < counts[slot_ids // SLOTS]
    ranked = jnp.sort(jnp.where(usable, slot_ids, slot_ids + OWNERS * SLOTS))[:REQ]
    chosen = ranked[jax.random.permutation(key_order, REQ)]
    holders = counts[chosen // SLOTS]
    ceiling = MAXLEN // holders
    length_draw = jax.random.randint(key_length, (REQ,), MINLEN, ceiling + 1)
    length_draw = jnp.where(chosen == owner_order[1] * SLOTS, MAXLEN, length_draw)
    length_draw = jnp.where(chosen == owner_order[0] * SLOTS, MINLEN, length_draw)
    return (chosen.astype(jnp.int32), length_draw.astype(jnp.int32))


def draw_request_slot(key, part):
    return request_layout(key)[0]


def draw_lengths(key, part):
    return request_layout(key)[1]


def draw_key_cache(key, part):
    row_total = OWNERS * MAXLEN
    drawn = jnp.clip(jax.random.normal(jax.random.fold_in(key, 13), (row_total, KV_HEADS * HD), jnp.float32), -6.0, 6.0)
    return drawn.astype(jnp.bfloat16)


def level_of(key, extent, cuts, least, top_value):
    level, own = 1.0, jax.random.fold_in(key, 6)
    for dim, shards_of in cuts:
        steps = jnp.exp(jax.random.uniform(jax.random.fold_in(own, dim), (shards_of,), jnp.float32, least / len(cuts), top_value / len(cuts)))
        level = level * jnp.repeat(steps, extent[dim] // shards_of).reshape([-1 if axis == dim else 1 for axis in range(len(extent))])
    return level


def scatter_about(key, dims, deviation, limit, pieces=(), kind=jnp.bfloat16):
    result = deviation * jax.random.normal(key, dims, jnp.float32)
    if pieces:
        result = result * level_of(key, dims, pieces, -0.22, 0.18)
    return jnp.clip(result, -limit, limit).astype(kind)


def setup_inputs(seed: int = 0, part: int = 0) -> dict:
    splits = jax.random.split(jax.random.key(seed), 17)
    part_splits = jax.random.split(jax.random.fold_in(splits[16], part), 17)
    return {
        "hidden": scatter_about(part_splits[0], (REQ, D), 0.25, 1.5, ((0, 16),)),
        "input_gain": jnp.clip(1.0 + 0.18 * jax.random.normal(splits[1], (D,), jnp.float32), 0.1, 1.9),
        "query_weight": scatter_about(splits[2], (D, QD), D ** -0.5, 0.078125, ((1, 16),)),
        "key_weight": scatter_about(splits[3], (D, KD), D ** -0.5, 0.078125, ((1, 16),)),
        "value_weight": scatter_about(splits[4], (D, KD), D ** -0.5, 0.078125, ((1, 16),)),
        "query_gain": jnp.clip(jnp.exp(jax.random.uniform(splits[5], (HD,), jnp.float32, math.log(2.0), math.log(6.0))), 2.0, 6.0),
        "key_gain": jnp.clip(jnp.exp(jax.random.uniform(splits[6], (HD,), jnp.float32, math.log(1.0), math.log(4.0))), 1.0, 4.0),
        "output_weight": scatter_about(splits[7], (QD, D), QD ** -0.5, 0.09375, ((0, 16),)),
        "post_gain": jnp.clip(1.0 + 0.18 * jax.random.normal(splits[8], (D,), jnp.float32), 0.1, 1.9),
        "gate_weight": scatter_about(splits[9], (D, FF), D ** -0.5, 0.078125, ((1, 16),)),
        "up_weight": scatter_about(splits[10], (D, FF), D ** -0.5, 0.078125, ((1, 16),)),
        "down_weight": scatter_about(splits[11], (FF, D), FF ** -0.5, 0.0546875, ((0, 16),)),
        "key_cache": draw_key_cache(jax.random.fold_in(jax.random.fold_in(splits[16], part), 71), part),
        "value_cache": scatter_about(part_splits[13], (OWNERS * MAXLEN, KD), 1.0, 6.0, ((0, 16),)),
        "lengths": draw_lengths(jax.random.fold_in(jax.random.fold_in(splits[16], part), 71), part),
        "request_slot": draw_request_slot(jax.random.fold_in(jax.random.fold_in(splits[16], part), 71), part),
    }


eps = 1e-06
theta = 1000000.0

def rms_scale(values, scales):
    values = values.astype(jnp.float32)
    return values * lax.rsqrt(lax.optimization_barrier(jnp.mean(values * values, axis=-1, keepdims=True)) + eps) * scales

def rotate(values, position):
    half_width = values.shape[-1] // 2
    frequency = theta ** (-jnp.arange(half_width, dtype=jnp.float32) * 2.0 / values.shape[-1])
    angles = position * frequency
    cosine = jnp.cos(angles)
    sine_part = jnp.sin(angles)
    front_half = values[..., :half_width]
    back_half = values[..., half_width:]
    return jnp.concatenate([front_half * cosine - back_half * sine_part, back_half * cosine + front_half * sine_part], axis=-1)

def reference(hidden, input_gain, query_weight, key_weight, value_weight, query_gain, key_gain, output_weight, post_gain, gate_weight, up_weight, down_weight, key_cache, value_cache, lengths, request_slot):
    requests = hidden.shape[0]
    group_size = HEADS // KV_HEADS
    normed = rms_scale(hidden, input_gain).astype(jnp.bfloat16)
    query_rows = jnp.dot(normed, query_weight, preferred_element_type=jnp.float32).astype(jnp.bfloat16)
    key_rows = jnp.dot(normed, key_weight, preferred_element_type=jnp.float32).astype(jnp.bfloat16)
    value_rows = jnp.dot(normed, value_weight, preferred_element_type=jnp.float32).astype(jnp.bfloat16)
    position = lengths.astype(jnp.float32)[:, None, None]
    query_heads = rotate(rms_scale(query_rows.reshape(requests, HEADS, HD), query_gain), position).astype(jnp.bfloat16)
    query_heads = query_heads.reshape(requests, KV_HEADS, group_size, HD)
    key_new = rotate(rms_scale(key_rows.reshape(requests, KV_HEADS, HD), key_gain), position).astype(jnp.bfloat16)
    value_new = value_rows.reshape(requests, KV_HEADS, HD)
    owner_of = (request_slot // SLOTS).astype(jnp.int32)
    within = request_slot % SLOTS
    earlier = (owner_of[None, :] == owner_of[:, None]) & (within[None, :] < within[:, None])
    offsets = lax.optimization_barrier(jnp.sum(jnp.where(earlier, lengths[None, :], 0), axis=1)).astype(jnp.int32)
    pooled_keys = key_cache.reshape(OWNERS, MAXLEN, KV_HEADS, HD)
    pooled_values = value_cache.reshape(OWNERS, MAXLEN, KV_HEADS, HD)
    token_pos = jnp.arange(MAXLEN, dtype=jnp.int32)
    scale_factor = 1.0 / math.sqrt(HD)

    def attend(items):
        query_one, key_one, value_one, owner_one, offset_one, length_one = items
        keys_here = lax.dynamic_index_in_dim(pooled_keys, owner_one, 0, keepdims=False).astype(jnp.float32)
        values_here = lax.dynamic_index_in_dim(pooled_values, owner_one, 0, keepdims=False).astype(jnp.float32)
        query_float = query_one.astype(jnp.float32)
        scores = jnp.einsum('kgd,tkd->kgt', query_float, keys_here) * scale_factor
        own_score = jnp.einsum('kgd,kd->kg', query_float, key_one.astype(jnp.float32)) * scale_factor
        inside = ((token_pos >= offset_one) & (token_pos < offset_one + length_one))[None, None, :]
        largest = jnp.maximum(lax.optimization_barrier(jnp.max(jnp.where(inside, scores, -1e+30), axis=2)), own_score)
        weights = jnp.where(inside, jnp.exp(scores - largest[..., None]), 0.0)
        own_weight = jnp.exp(own_score - largest)
        denominator = lax.optimization_barrier(jnp.sum(weights, axis=2)) + own_weight
        weights_low = weights.astype(jnp.bfloat16).astype(jnp.float32)
        own_low = own_weight.astype(jnp.bfloat16).astype(jnp.float32)
        summed = jnp.einsum('kgt,tkd->kgd', weights_low, values_here)
        summed = summed + own_low[..., None] * value_one.astype(jnp.float32)[:, None, :]
        return (summed / denominator[..., None]).astype(jnp.bfloat16).reshape(HEADS * HD)
    head_rows = lax.map(attend, (query_heads, key_new, value_new, owner_of, offsets, lengths.astype(jnp.int32)))
    attended = jnp.dot(head_rows, output_weight, preferred_element_type=jnp.float32)
    mixed = (hidden.astype(jnp.float32) + attended).astype(jnp.bfloat16)
    post_normed = rms_scale(mixed, post_gain).astype(jnp.bfloat16)
    gate_part = jnp.dot(post_normed, gate_weight, preferred_element_type=jnp.float32)
    up_part = jnp.dot(post_normed, up_weight, preferred_element_type=jnp.float32)
    activated = (jax.nn.silu(gate_part) * up_part).astype(jnp.bfloat16)
    lowered = jnp.dot(activated, down_weight, preferred_element_type=jnp.float32)
    final = (mixed.astype(jnp.float32) + lowered).astype(jnp.bfloat16)
    return (mixed, final)
```

```python
import math

import jax
import jax.numpy as jnp
from jax import lax
from jax.sharding import PartitionSpec as P

SLOTS = 4


eps = 1e-06
theta = 1000000.0


def rms_scale(values, scales):
    values = values.astype(jnp.float32)
    return values * lax.rsqrt(jnp.mean(values * values, axis=-1, keepdims=True) + eps) * scales


def rotate(values, position):
    half_width = values.shape[-1] // 2
    frequency = theta ** (-jnp.arange(half_width, dtype=jnp.float32) * 2.0 / values.shape[-1])
    angles = position * frequency
    cosine = jnp.cos(angles)
    sine_part = jnp.sin(angles)
    front_half = values[..., :half_width]
    back_half = values[..., half_width:]
    return jnp.concatenate(
        [front_half * cosine - back_half * sine_part, back_half * cosine + front_half * sine_part],
        axis=-1,
    )


def gather_rows(rows, devices):
    copies = jnp.broadcast_to(rows[None], (devices,) + rows.shape)
    arrived = lax.all_to_all(copies, ("pool", "tensor"), split_axis=0, concat_axis=0, tiled=True)
    return arrived.reshape(devices * rows.shape[0], rows.shape[1])


def scatter_sum(partial, devices):
    blocks = partial.astype(jnp.bfloat16).reshape(devices, -1, partial.shape[1])
    arrived = lax.all_to_all(blocks, ("pool", "tensor"), split_axis=0, concat_axis=0, tiled=True)
    return jnp.sum(arrived.astype(jnp.float32), axis=0)


def on_device(
    hidden,
    input_gain,
    query_weight,
    key_weight,
    value_weight,
    query_gain,
    key_gain,
    output_weight,
    post_gain,
    gate_weight,
    up_weight,
    down_weight,
    key_cache,
    value_cache,
    lengths,
    request_slot,
):
    devices = lax.axis_size(("pool", "tensor"))
    device_index = lax.axis_index(("pool", "tensor"))
    local_rows = hidden.shape[0]
    query_cols = query_weight.shape[1]
    key_cols = key_weight.shape[1]
    width_sent = query_cols + 2 * key_cols
    head_dim = query_gain.shape[0]
    slot_count = SLOTS
    head_count = devices * query_cols // head_dim
    kv_count = devices * key_cols // head_dim
    group_size = head_count // kv_count
    normed = rms_scale(hidden, input_gain).astype(jnp.bfloat16)
    shard_rows = gather_rows(normed, devices)
    query_part = jnp.dot(shard_rows, query_weight, preferred_element_type=jnp.float32)
    key_part = jnp.dot(shard_rows, key_weight, preferred_element_type=jnp.float32)
    value_part = jnp.dot(shard_rows, value_weight, preferred_element_type=jnp.float32)
    projected = jnp.concatenate([query_part, key_part, value_part], axis=1).astype(jnp.bfloat16)
    outgoing = (
        jnp.zeros((devices * slot_count, width_sent), jnp.bfloat16).at[request_slot].set(projected)
    )
    outgoing = outgoing.reshape(devices, slot_count, width_sent)
    arrived = lax.all_to_all(
        outgoing, ("pool", "tensor"), split_axis=0, concat_axis=2, tiled=True
    ).reshape(slot_count, devices, width_sent)
    query_full = arrived[:, :, :query_cols].reshape(slot_count, head_count, head_dim)
    key_full = arrived[:, :, query_cols : query_cols + key_cols].reshape(
        slot_count, kv_count, head_dim
    )
    value_new = arrived[:, :, query_cols + key_cols :].reshape(slot_count, kv_count, head_dim)
    slot_ids = device_index * slot_count + jnp.arange(slot_count, dtype=jnp.int32)
    matches = request_slot[None, :] == slot_ids[:, None]
    slot_length = jnp.sum(jnp.where(matches, lengths[None, :], 0), axis=1)
    owner_of = request_slot // slot_count
    within = request_slot % slot_count
    earlier = (owner_of[None, :] == device_index) & (
        within[None, :] < jnp.arange(slot_count, dtype=jnp.int32)[:, None]
    )
    slot_offset = jnp.sum(jnp.where(earlier, lengths[None, :], 0), axis=1)
    position = slot_length.astype(jnp.float32)[:, None, None]
    query_heads = rotate(rms_scale(query_full, query_gain), position).astype(jnp.bfloat16)
    query_heads = query_heads.reshape(slot_count, kv_count, group_size, head_dim)
    key_new = rotate(rms_scale(key_full, key_gain), position).astype(jnp.bfloat16)
    pool_tokens = key_cache.shape[0]
    scale_factor = 1.0 / math.sqrt(head_dim)
    scores = jnp.stack(
        [
            jnp.einsum(
                "sgd,td->sgt",
                query_heads[:, kv],
                key_cache[:, kv * head_dim : (kv + 1) * head_dim],
                preferred_element_type=jnp.float32,
            )
            for kv in range(kv_count)
        ],
        axis=1,
    ) * scale_factor
    own_score = (
        jnp.einsum("skgd,skd->skg", query_heads, key_new, preferred_element_type=jnp.float32)
        * scale_factor
    )
    token_pos = jnp.arange(pool_tokens, dtype=jnp.int32)
    inside = (token_pos[None, :] >= slot_offset[:, None]) & (
        token_pos[None, :] < (slot_offset + slot_length)[:, None]
    )
    inside = inside[:, None, None, :]
    largest = jnp.maximum(jnp.max(jnp.where(inside, scores, -1e30), axis=3), own_score)
    weights = jnp.where(inside, jnp.exp(scores - largest[..., None]), 0.0)
    own_weight = jnp.exp(own_score - largest)
    denominator = jnp.sum(weights, axis=3) + own_weight
    weights_low = weights.astype(jnp.bfloat16)
    summed = jnp.stack(
        [
            jnp.einsum(
                "sgt,td->sgd",
                weights_low[:, kv],
                value_cache[:, kv * head_dim : (kv + 1) * head_dim],
                preferred_element_type=jnp.float32,
            )
            for kv in range(kv_count)
        ],
        axis=1,
    )
    own_low = own_weight.astype(jnp.bfloat16).astype(jnp.float32)
    summed = summed + own_low[..., None] * value_new.astype(jnp.float32)[:, :, None, :]
    head_out = (
        (summed / denominator[..., None])
        .astype(jnp.bfloat16)
        .reshape(slot_count, devices, query_cols)
    )
    returned = lax.all_to_all(head_out, ("pool", "tensor"), split_axis=1, concat_axis=0, tiled=True)
    head_rows = returned.reshape(devices * slot_count, query_cols)[request_slot]
    partial_value = jnp.dot(head_rows, output_weight, preferred_element_type=jnp.float32)
    mixed_rows = (hidden.astype(jnp.float32) + scatter_sum(partial_value, devices)).astype(jnp.bfloat16)
    post_normed = gather_rows(rms_scale(mixed_rows, post_gain).astype(jnp.bfloat16), devices)
    gate_part = jnp.dot(post_normed, gate_weight, preferred_element_type=jnp.float32)
    up_part = jnp.dot(post_normed, up_weight, preferred_element_type=jnp.float32)
    activated = (jax.nn.silu(gate_part) * up_part).astype(jnp.bfloat16)
    lowered = scatter_sum(
        jnp.dot(activated, down_weight, preferred_element_type=jnp.float32), devices
    )
    final_rows = (mixed_rows.astype(jnp.float32) + lowered).astype(jnp.bfloat16)
    return (mixed_rows, final_rows)


def solution(mesh):
    placed = (
        P(("groups", "pool", "tensor"), None),
        P(),
        P(None, ("pool", "tensor")),
        P(None, ("pool", "tensor")),
        P(None, ("pool", "tensor")),
        P(),
        P(),
        P(("pool", "tensor"), None),
        P(),
        P(None, ("pool", "tensor")),
        P(None, ("pool", "tensor")),
        P(("pool", "tensor"), None),
        P(("groups", "pool", "tensor"), None),
        P(("groups", "pool", "tensor"), None),
        P("groups"),
        P("groups"),
    )
    return jax.shard_map(
        on_device,
        mesh=mesh,
        in_specs=placed,
        out_specs=(P(("groups", "pool", "tensor"), None), P(("groups", "pool", "tensor"), None)),
        check_vma=False,
    )
```

```python
import functools
import math

import jax
import jax.numpy as jnp
from jax import lax
from jax.experimental import pallas as pl
from jax.experimental.pallas import tpu as pltpu
from jax.sharding import PartitionSpec as P

SLOTS = 4
LANES = 128
MIB = 2**20


eps = 1e-06
theta = 1000000.0


def rms_scale(values, scales):
    values = values.astype(jnp.float32)
    return values * lax.rsqrt(jnp.mean(values * values, axis=-1, keepdims=True) + eps) * scales


def rotate(values, position):
    half_width = values.shape[-1] // 2
    frequency = theta ** (-jnp.arange(half_width, dtype=jnp.float32) * 2.0 / values.shape[-1])
    angles = position * frequency
    cosine = jnp.cos(angles)
    sine_part = jnp.sin(angles)
    front_half = values[..., :half_width]
    back_half = values[..., half_width:]
    return jnp.concatenate(
        [front_half * cosine - back_half * sine_part, back_half * cosine + front_half * sine_part],
        axis=-1,
    )


def swap_cores(block):
    return lax.ppermute(block, "pool", [(0, 1), (1, 0)])


def gather_halves(rows, chips):
    copies = jnp.broadcast_to(rows[None], (chips,) + rows.shape)
    own = lax.all_to_all(copies, "tensor", split_axis=0, concat_axis=0, tiled=True)
    own = own.reshape(chips * rows.shape[0], rows.shape[1])
    return own, swap_cores(own)


def scatter_halves(own_half, other_half, chips):
    added = own_half.astype(jnp.float32) + swap_cores(other_half).astype(jnp.float32)
    blocks = added.astype(jnp.bfloat16).reshape(chips, -1, own_half.shape[1])
    arrived = lax.all_to_all(blocks, "tensor", split_axis=0, concat_axis=0, tiled=True)
    return jnp.sum(arrived.astype(jnp.float32), axis=0)


def dot_rows(left, right):
    return lax.dot_general(
        left, right, (((1,), (0,)), ((), ())), preferred_element_type=jnp.float32
    )


def dot_columns(left, right):
    return lax.dot_general(
        left, right, (((1,), (1,)), ((), ())), preferred_element_type=jnp.float32
    )


def pieces(extent, step):
    return [(start, min(step, extent - start)) for start in range(0, extent, step)]


def copy_rows(source, target, sems, parts):
    copies = [
        pltpu.make_async_copy(
            source.at[pl.ds(start, size)], target.at[pl.ds(start, size)], sems.at[index]
        )
        for index, (start, size) in enumerate(parts)
    ]
    for copy in copies:
        copy.start()
    return copies


IN_VMEM = pl.BlockSpec(memory_space=pltpu.VMEM)
IN_SMEM = pl.BlockSpec(memory_space=pltpu.SMEM)
IN_HBM = pl.BlockSpec(memory_space=pl.ANY)


def keep_in_hbm(array):
    return pltpu.with_memory_space_constraint(array, pltpu.HBM)


def project_kernel(
    slot_count, own, other, gain, slots, q_hbm, k_hbm, v_hbm, out, normed, q_vm, k_vm, v_vm, sems
):
    half, width = own.shape
    parts = pieces(width, width // 4)
    q_copies = copy_rows(q_hbm, q_vm, sems.at[0], parts)
    k_copy = copy_rows(k_hbm, k_vm, sems.at[1], [(0, k_vm.shape[0])])[0]
    v_copy = copy_rows(v_hbm, v_vm, sems.at[2], [(0, v_vm.shape[0])])[0]
    for index, source in enumerate((own, other)):
        rows = source[...].astype(jnp.float32)
        scale = lax.rsqrt(jnp.mean(rows * rows, axis=-1, keepdims=True) + eps)
        normed[pl.ds(index * half, half), :] = (rows * scale * gain[...]).astype(jnp.bfloat16)
    total = jnp.zeros((2 * half, q_vm.shape[1]), jnp.float32)
    for copy, (start, size) in zip(q_copies, parts):
        copy.wait()
        total = total + dot_rows(normed[:, start : start + size], q_vm[start : start + size, :])
    k_copy.wait()
    v_copy.wait()
    key_part = dot_columns(normed[...], k_vm[...])
    value_part = dot_columns(normed[...], v_vm[...])
    projected = jnp.concatenate([total, key_part, value_part], axis=1).astype(jnp.bfloat16)
    places = lax.broadcasted_iota(jnp.int32, (out.shape[0] * slot_count, 2 * half), 0)
    chosen = jnp.where(slots[...] == places, 1.0, 0.0).astype(jnp.bfloat16)
    packed = dot_rows(chosen, projected)
    for owner in range(out.shape[0]):
        out[owner] = packed[owner * slot_count : (owner + 1) * slot_count, :].astype(jnp.bfloat16)


def project(own, other, gain, slots, query_weight, key_weight, value_weight, devices, slot_count):
    depth, query_cols = query_weight.shape
    key_cols = key_weight.shape[1]
    width = query_cols + 2 * key_cols
    return pl.pallas_call(
        functools.partial(project_kernel, slot_count),
        out_shape=jax.ShapeDtypeStruct((devices, slot_count, width), jnp.bfloat16),
        in_specs=[IN_VMEM] * 4 + [IN_HBM] * 3,
        out_specs=IN_VMEM,
        scratch_shapes=[
            pltpu.VMEM((2 * own.shape[0], depth), jnp.bfloat16),
            pltpu.VMEM((depth, query_cols), jnp.bfloat16),
            pltpu.VMEM((key_cols, depth), jnp.bfloat16),
            pltpu.VMEM((key_cols, depth), jnp.bfloat16),
            pltpu.SemaphoreType.DMA((3, 4)),
        ],
        compiler_params=pltpu.CompilerParams(vmem_limit_bytes=16 * MIB),
        name="project",
    )(
        own,
        other,
        gain.reshape(1, depth),
        slots.reshape(1, -1),
        keep_in_hbm(query_weight),
        keep_in_hbm(key_weight.T),
        keep_in_hbm(value_weight.T),
    )


def attend_kernel(
    query_cols,
    key_cols,
    starts,
    ends,
    arrived,
    cosine,
    sine,
    query_gain,
    key_gain,
    key_hbm,
    value_hbm,
    out,
    key_vm,
    value_vm,
    sems,
):
    devices, slot_count, _ = arrived.shape
    tokens = key_vm.shape[0]
    head_dim = query_gain.shape[1]
    kv_count = devices * key_cols // head_dim
    sharers = devices // kv_count
    heads_here = query_cols // head_dim
    repeats = sharers * heads_here
    count = repeats * slot_count
    parts = pieces(tokens, tokens // 2)
    key_copies = copy_rows(key_hbm, key_vm, sems.at[0], parts)
    value_copies = copy_rows(value_hbm, value_vm, sems.at[1], parts)
    scale_factor = 1.0 / math.sqrt(head_dim)
    slot_of = lax.rem(lax.broadcasted_iota(jnp.int32, (count, 1), 0), slot_count)
    first = jnp.zeros((count, 1), jnp.int32)
    last = jnp.zeros((count, 1), jnp.int32)
    for slot in range(slot_count):
        first = jnp.where(slot_of == slot, starts[slot], first)
        last = jnp.where(slot_of == slot, ends[slot], last)
    cos_new = cosine[...]
    sin_new = sine[...]

    def prepare(rows, gain, cos_rows, sin_rows):
        rows = rows * lax.rsqrt(jnp.mean(rows * rows, axis=-1, keepdims=True) + eps) * gain[...]
        turned = pltpu.roll(rows, head_dim // 2, 1)
        return (rows * cos_rows + turned * sin_rows).astype(jnp.bfloat16)

    def tile(rows):
        return jnp.concatenate([rows] * repeats, axis=0)

    cos_all = tile(cos_new)
    sin_all = tile(sin_new)
    queries, own_scores, own_values = [], [], []
    for kv in range(kv_count):
        holders = range(kv * sharers, (kv + 1) * sharers)
        rows = jnp.concatenate(
            [
                arrived[holder, :, head * head_dim : (head + 1) * head_dim].astype(jnp.float32)
                for head in range(heads_here)
                for holder in holders
            ],
            axis=0,
        )
        query = prepare(rows, query_gain, cos_all, sin_all)
        fresh = jnp.concatenate(
            [
                arrived[holder, :, query_cols : query_cols + key_cols].astype(jnp.float32)
                for holder in holders
            ],
            axis=1,
        )
        key_new = prepare(fresh, key_gain, cos_new, sin_new).astype(jnp.float32)
        value_new = jnp.concatenate(
            [
                arrived[holder, :, query_cols + key_cols :].astype(jnp.float32)
                for holder in holders
            ],
            axis=1,
        )
        queries.append(query)
        own_scores.append(
            jnp.sum(query.astype(jnp.float32) * tile(key_new), axis=-1, keepdims=True)
            * scale_factor
        )
        own_values.append(tile(value_new))
    positions = lax.broadcasted_iota(jnp.int32, (count, tokens), 1)
    inside = (positions >= first) & (positions < last)
    for copy in key_copies:
        copy.wait()
    for kv in range(kv_count):
        columns = slice(kv * head_dim, (kv + 1) * head_dim)
        scores = dot_columns(queries[kv], key_vm[:, columns]) * scale_factor
        own_score = own_scores[kv]
        largest = jnp.maximum(
            jnp.max(jnp.where(inside, scores, -1e30), axis=1, keepdims=True), own_score
        )
        weights = jnp.where(inside, jnp.exp(scores - largest), 0.0)
        own_weight = jnp.exp(own_score - largest)
        denominator = jnp.sum(weights, axis=1, keepdims=True) + own_weight
        if kv == 0:
            for copy in value_copies:
                copy.wait()
        summed = dot_rows(weights.astype(jnp.bfloat16), value_vm[:, columns])
        own_low = own_weight.astype(jnp.bfloat16).astype(jnp.float32)
        summed = (summed + own_low * own_values[kv]) / denominator
        for head in range(heads_here):
            for place in range(sharers):
                row = (head * sharers + place) * slot_count
                out[kv * sharers + place, :, head * head_dim : (head + 1) * head_dim] = summed[
                    row : row + slot_count, :
                ].astype(jnp.bfloat16)


def attend(arrived, starts, ends, cosine, sine, query_gain, key_gain, key_cache, value_cache, query_cols):
    devices, slot_count, width = arrived.shape
    key_cols = (width - query_cols) // 2
    head_dim = query_gain.shape[0]
    return pl.pallas_call(
        functools.partial(attend_kernel, query_cols, key_cols),
        out_shape=jax.ShapeDtypeStruct((devices, slot_count, query_cols), jnp.bfloat16),
        in_specs=[IN_SMEM] * 2 + [IN_VMEM] * 5 + [IN_HBM] * 2,
        out_specs=IN_VMEM,
        scratch_shapes=[
            pltpu.VMEM(key_cache.shape, jnp.bfloat16),
            pltpu.VMEM(value_cache.shape, jnp.bfloat16),
            pltpu.SemaphoreType.DMA((2, 2)),
        ],
        compiler_params=pltpu.CompilerParams(vmem_limit_bytes=24 * MIB),
        name="attend",
    )(
        starts,
        ends,
        arrived,
        cosine,
        sine,
        query_gain.reshape(1, head_dim),
        key_gain.reshape(1, head_dim),
        keep_in_hbm(key_cache),
        keep_in_hbm(value_cache),
    )


def mix_kernel(returned, slots, weight_hbm, own_out, other_out, weight_vm, sems):
    owners, slot_count, depth = returned.shape
    half, width = own_out.shape
    parts = pieces(depth, depth // 2)
    copies = copy_rows(weight_hbm, weight_vm, sems, parts)
    by_slot = jnp.concatenate(
        [returned[owner].astype(jnp.float32) for owner in range(owners)], axis=0
    ).astype(jnp.bfloat16)
    places = lax.broadcasted_iota(jnp.int32, (2 * half, owners * slot_count), 1)
    chosen = jnp.where(slots[...] == places, 1.0, 0.0).astype(jnp.bfloat16)
    rows = dot_rows(chosen, by_slot).astype(jnp.bfloat16)
    for copy in copies:
        copy.wait()
    for start, size in pieces(width, 1024):
        total = dot_rows(rows, weight_vm[:, start : start + size])
        own_out[:, start : start + size] = total[:half].astype(own_out.dtype)
        other_out[:, start : start + size] = total[half:].astype(other_out.dtype)


def mix(returned, slots, output_weight, requests):
    depth, width = output_weight.shape
    half = requests // 2
    return pl.pallas_call(
        mix_kernel,
        out_shape=(
            jax.ShapeDtypeStruct((half, width), jnp.float32),
            jax.ShapeDtypeStruct((half, width), jnp.bfloat16),
        ),
        in_specs=[IN_VMEM] * 2 + [IN_HBM],
        out_specs=(IN_VMEM, IN_VMEM),
        scratch_shapes=[
            pltpu.VMEM((depth, width), jnp.bfloat16),
            pltpu.SemaphoreType.DMA((2,)),
        ],
        compiler_params=pltpu.CompilerParams(vmem_limit_bytes=16 * MIB),
        name="mix",
    )(returned, slots.reshape(-1, 1), keep_in_hbm(output_weight))


def feed_kernel(
    own, other, gate_hbm, up_hbm, down_hbm, own_out, other_out, rows, gate_vm, up_vm, down_vm, acts, sems
):
    half, width = own.shape
    units = gate_vm.shape[0]
    parts = pieces(units, 256)
    gate_copies, up_copies = [], []
    for index, part in enumerate(parts):
        gate_copies += copy_rows(gate_hbm, gate_vm, sems.at[0, pl.ds(index, 1)], [part])
        up_copies += copy_rows(up_hbm, up_vm, sems.at[1, pl.ds(index, 1)], [part])
    down_copies = copy_rows(down_hbm, down_vm, sems.at[2], parts)
    rows[:half, :] = own[...]
    rows[half:, :] = other[...]
    for index, (start, size) in enumerate(parts):
        gate_copies[index].wait()
        gate_part = dot_columns(rows[...], gate_vm[start : start + size, :])
        up_copies[index].wait()
        up_part = dot_columns(rows[...], up_vm[start : start + size, :])
        silu = gate_part / (1.0 + jnp.exp(-gate_part))
        acts[:, start : start + size] = (silu * up_part).astype(jnp.bfloat16)
    for copy in down_copies:
        copy.wait()
    for start, size in pieces(width, 1024):
        total = dot_rows(acts[...], down_vm[:, start : start + size])
        own_out[:, start : start + size] = total[:half].astype(own_out.dtype)
        other_out[:, start : start + size] = total[half:].astype(other_out.dtype)


def feed(own, other, gate_weight, up_weight, down_weight):
    half, width = own.shape
    units = gate_weight.shape[1]
    return pl.pallas_call(
        feed_kernel,
        out_shape=(
            jax.ShapeDtypeStruct((half, width), jnp.float32),
            jax.ShapeDtypeStruct((half, width), jnp.bfloat16),
        ),
        in_specs=[IN_VMEM] * 2 + [IN_HBM] * 3,
        out_specs=(IN_VMEM, IN_VMEM),
        scratch_shapes=[
            pltpu.VMEM((2 * half, width), jnp.bfloat16),
            pltpu.VMEM((units, width), jnp.bfloat16),
            pltpu.VMEM((units, width), jnp.bfloat16),
            pltpu.VMEM((units, width), jnp.bfloat16),
            pltpu.VMEM((2 * half, units), jnp.bfloat16),
            pltpu.SemaphoreType.DMA((3, len(pieces(units, 256)))),
        ],
        compiler_params=pltpu.CompilerParams(vmem_limit_bytes=48 * MIB),
        name="feed",
    )(
        own,
        other,
        keep_in_hbm(gate_weight.T),
        keep_in_hbm(up_weight.T),
        keep_in_hbm(down_weight),
    )


def halves_first(values, half):
    swapped = jnp.concatenate([values[half:], values[:half]])
    return jnp.where(lax.axis_index("pool") == 0, values, swapped)


def on_device_kernels(
    hidden,
    input_gain,
    query_weight,
    key_weight,
    value_weight,
    query_gain,
    key_gain,
    output_weight,
    post_gain,
    gate_weight,
    up_weight,
    down_weight,
    key_cache,
    value_cache,
    lengths,
    request_slot,
):
    devices = lax.axis_size(("pool", "tensor"))
    chips = lax.axis_size("tensor")
    device_index = lax.axis_index(("pool", "tensor"))
    requests = lengths.shape[0]
    half = requests // 2
    slot_count = SLOTS
    query_cols = query_weight.shape[1]
    head_dim = query_gain.shape[0]
    own, other = gather_halves(hidden, chips)
    slots = halves_first(request_slot, half)
    outgoing = project(
        own, other, input_gain, slots, query_weight, key_weight, value_weight, devices, slot_count
    )
    arrived = lax.all_to_all(
        outgoing, ("pool", "tensor"), split_axis=0, concat_axis=0, tiled=True
    )
    slot_ids = device_index * slot_count + jnp.arange(slot_count, dtype=jnp.int32)
    matches = request_slot[None, :] == slot_ids[:, None]
    slot_length = jnp.sum(jnp.where(matches, lengths[None, :], 0), axis=1)
    owner_of = request_slot // slot_count
    within = request_slot % slot_count
    earlier = (owner_of[None, :] == device_index) & (
        within[None, :] < jnp.arange(slot_count, dtype=jnp.int32)[:, None]
    )
    slot_offset = jnp.sum(jnp.where(earlier, lengths[None, :], 0), axis=1)
    frequency = theta ** (-jnp.arange(head_dim // 2, dtype=jnp.float32) * 2.0 / head_dim)
    angles = slot_length.astype(jnp.float32)[:, None] * frequency[None, :]
    cosine = jnp.cos(angles)
    sine = jnp.sin(angles)
    head_out = attend(
        arrived,
        slot_offset,
        slot_offset + slot_length,
        jnp.concatenate([cosine, cosine], axis=1),
        jnp.concatenate([-sine, sine], axis=1),
        query_gain,
        key_gain,
        key_cache,
        value_cache,
        query_cols,
    )
    returned = lax.all_to_all(
        head_out, ("pool", "tensor"), split_axis=0, concat_axis=0, tiled=True
    )
    own_sum, other_sum = mix(returned, slots, output_weight, requests)
    mixed_rows = (
        hidden.astype(jnp.float32) + scatter_halves(own_sum, other_sum, chips)
    ).astype(jnp.bfloat16)
    post_normed = rms_scale(mixed_rows, post_gain).astype(jnp.bfloat16)
    own, other = gather_halves(post_normed, chips)
    own_sum, other_sum = feed(own, other, gate_weight, up_weight, down_weight)
    lowered = scatter_halves(own_sum, other_sum, chips)
    final_rows = (mixed_rows.astype(jnp.float32) + lowered).astype(jnp.bfloat16)
    return (mixed_rows, final_rows)


def gather_rows(rows, devices):
    copies = jnp.broadcast_to(rows[None], (devices,) + rows.shape)
    arrived = lax.all_to_all(copies, ("pool", "tensor"), split_axis=0, concat_axis=0, tiled=True)
    return arrived.reshape(devices * rows.shape[0], rows.shape[1])


def scatter_sum(partial, devices):
    blocks = partial.astype(jnp.bfloat16).reshape(devices, -1, partial.shape[1])
    arrived = lax.all_to_all(blocks, ("pool", "tensor"), split_axis=0, concat_axis=0, tiled=True)
    return jnp.sum(arrived.astype(jnp.float32), axis=0)


def on_device_general(
    hidden,
    input_gain,
    query_weight,
    key_weight,
    value_weight,
    query_gain,
    key_gain,
    output_weight,
    post_gain,
    gate_weight,
    up_weight,
    down_weight,
    key_cache,
    value_cache,
    lengths,
    request_slot,
):
    devices = lax.axis_size(("pool", "tensor"))
    device_index = lax.axis_index(("pool", "tensor"))
    local_rows = hidden.shape[0]
    query_cols = query_weight.shape[1]
    key_cols = key_weight.shape[1]
    width_sent = query_cols + 2 * key_cols
    head_dim = query_gain.shape[0]
    slot_count = SLOTS
    head_count = devices * query_cols // head_dim
    kv_count = devices * key_cols // head_dim
    group_size = head_count // kv_count
    normed = rms_scale(hidden, input_gain).astype(jnp.bfloat16)
    shard_rows = gather_rows(normed, devices)
    query_part = jnp.dot(shard_rows, query_weight, preferred_element_type=jnp.float32)
    key_part = jnp.dot(shard_rows, key_weight, preferred_element_type=jnp.float32)
    value_part = jnp.dot(shard_rows, value_weight, preferred_element_type=jnp.float32)
    projected = jnp.concatenate([query_part, key_part, value_part], axis=1).astype(jnp.bfloat16)
    outgoing = (
        jnp.zeros((devices * slot_count, width_sent), jnp.bfloat16).at[request_slot].set(projected)
    )
    outgoing = outgoing.reshape(devices, slot_count, width_sent)
    arrived = lax.all_to_all(
        outgoing, ("pool", "tensor"), split_axis=0, concat_axis=2, tiled=True
    ).reshape(slot_count, devices, width_sent)
    query_full = arrived[:, :, :query_cols].reshape(slot_count, head_count, head_dim)
    key_full = arrived[:, :, query_cols : query_cols + key_cols].reshape(
        slot_count, kv_count, head_dim
    )
    value_new = arrived[:, :, query_cols + key_cols :].reshape(slot_count, kv_count, head_dim)
    slot_ids = device_index * slot_count + jnp.arange(slot_count, dtype=jnp.int32)
    matches = request_slot[None, :] == slot_ids[:, None]
    slot_length = jnp.sum(jnp.where(matches, lengths[None, :], 0), axis=1)
    owner_of = request_slot // slot_count
    within = request_slot % slot_count
    earlier = (owner_of[None, :] == device_index) & (
        within[None, :] < jnp.arange(slot_count, dtype=jnp.int32)[:, None]
    )
    slot_offset = jnp.sum(jnp.where(earlier, lengths[None, :], 0), axis=1)
    position = slot_length.astype(jnp.float32)[:, None, None]
    query_heads = rotate(rms_scale(query_full, query_gain), position).astype(jnp.bfloat16)
    query_heads = query_heads.reshape(slot_count, kv_count, group_size, head_dim)
    key_new = rotate(rms_scale(key_full, key_gain), position).astype(jnp.bfloat16)
    pool_tokens = key_cache.shape[0]
    scale_factor = 1.0 / math.sqrt(head_dim)
    scores = jnp.stack(
        [
            jnp.einsum(
                "sgd,td->sgt",
                query_heads[:, kv],
                key_cache[:, kv * head_dim : (kv + 1) * head_dim],
                preferred_element_type=jnp.float32,
            )
            for kv in range(kv_count)
        ],
        axis=1,
    ) * scale_factor
    own_score = (
        jnp.einsum("skgd,skd->skg", query_heads, key_new, preferred_element_type=jnp.float32)
        * scale_factor
    )
    token_pos = jnp.arange(pool_tokens, dtype=jnp.int32)
    inside = (token_pos[None, :] >= slot_offset[:, None]) & (
        token_pos[None, :] < (slot_offset + slot_length)[:, None]
    )
    inside = inside[:, None, None, :]
    largest = jnp.maximum(jnp.max(jnp.where(inside, scores, -1e30), axis=3), own_score)
    weights = jnp.where(inside, jnp.exp(scores - largest[..., None]), 0.0)
    own_weight = jnp.exp(own_score - largest)
    denominator = jnp.sum(weights, axis=3) + own_weight
    weights_low = weights.astype(jnp.bfloat16)
    summed = jnp.stack(
        [
            jnp.einsum(
                "sgt,td->sgd",
                weights_low[:, kv],
                value_cache[:, kv * head_dim : (kv + 1) * head_dim],
                preferred_element_type=jnp.float32,
            )
            for kv in range(kv_count)
        ],
        axis=1,
    )
    own_low = own_weight.astype(jnp.bfloat16).astype(jnp.float32)
    summed = summed + own_low[..., None] * value_new.astype(jnp.float32)[:, :, None, :]
    head_out = (
        (summed / denominator[..., None])
        .astype(jnp.bfloat16)
        .reshape(slot_count, devices, query_cols)
    )
    returned = lax.all_to_all(head_out, ("pool", "tensor"), split_axis=1, concat_axis=0, tiled=True)
    head_rows = returned.reshape(devices * slot_count, query_cols)[request_slot]
    partial_value = jnp.dot(head_rows, output_weight, preferred_element_type=jnp.float32)
    mixed_rows = (hidden.astype(jnp.float32) + scatter_sum(partial_value, devices)).astype(jnp.bfloat16)
    post_normed = gather_rows(rms_scale(mixed_rows, post_gain).astype(jnp.bfloat16), devices)
    gate_part = jnp.dot(post_normed, gate_weight, preferred_element_type=jnp.float32)
    up_part = jnp.dot(post_normed, up_weight, preferred_element_type=jnp.float32)
    activated = (jax.nn.silu(gate_part) * up_part).astype(jnp.bfloat16)
    lowered = scatter_sum(
        jnp.dot(activated, down_weight, preferred_element_type=jnp.float32), devices
    )
    final_rows = (mixed_rows.astype(jnp.float32) + lowered).astype(jnp.bfloat16)
    return (mixed_rows, final_rows)


def on_device(*arrays):
    query_cols, key_cols = arrays[2].shape[1], arrays[3].shape[1]
    head_dim = arrays[5].shape[0]
    devices = lax.axis_size(("pool", "tensor"))
    kv_count = devices * key_cols // head_dim
    whole_heads = query_cols % head_dim == 0 and head_dim % LANES == 0
    shared = kv_count > 0 and devices % kv_count == 0
    pairs = lax.axis_size("pool") == 2 and arrays[14].shape[0] % 16 == 0
    if whole_heads and shared and pairs:
        return on_device_kernels(*arrays)
    return on_device_general(*arrays)


def solution(mesh):
    placed = (
        P(("groups", "pool", "tensor"), None),
        P(),
        P(None, ("pool", "tensor")),
        P(None, ("pool", "tensor")),
        P(None, ("pool", "tensor")),
        P(),
        P(),
        P(("pool", "tensor"), None),
        P(),
        P(None, ("pool", "tensor")),
        P(None, ("pool", "tensor")),
        P(("pool", "tensor"), None),
        P(("groups", "pool", "tensor"), None),
        P(("groups", "pool", "tensor"), None),
        P("groups"),
        P("groups"),
    )
    return jax.shard_map(
        on_device,
        mesh=mesh,
        in_specs=placed,
        out_specs=(P(("groups", "pool", "tensor"), None), P(("groups", "pool", "tensor"), None)),
        check_vma=False,
    )
```

```python
import functools
import math

import jax
import jax.numpy as jnp
from jax import lax
from jax.experimental import pallas as pl
from jax.experimental.pallas import tpu as pltpu
from jax.sharding import PartitionSpec as P

SLOTS = 4
LANES = 128
MIB = 2**20
FETCHED = 13 * MIB // 4


eps = 1e-06
theta = 1000000.0


def rms_scale(values, scales):
    values = values.astype(jnp.float32)
    return values * lax.rsqrt(jnp.mean(values * values, axis=-1, keepdims=True) + eps) * scales


def rotate(values, position):
    half_width = values.shape[-1] // 2
    frequency = theta ** (-jnp.arange(half_width, dtype=jnp.float32) * 2.0 / values.shape[-1])
    angles = position * frequency
    cosine = jnp.cos(angles)
    sine_part = jnp.sin(angles)
    front_half = values[..., :half_width]
    back_half = values[..., half_width:]
    return jnp.concatenate(
        [front_half * cosine - back_half * sine_part, back_half * cosine + front_half * sine_part],
        axis=-1,
    )


def swap_cores(block):
    return lax.ppermute(block, "pool", [(0, 1), (1, 0)])


def beside(exchange, blocks, work, *arrays):
    blocks, arrays = lax.optimization_barrier((blocks, arrays))
    return lax.optimization_barrier((exchange(blocks), work(*arrays)))


def swap_chips(blocks):
    return lax.all_to_all(blocks, "tensor", split_axis=0, concat_axis=0, tiled=True)


def swap_all(blocks):
    return lax.all_to_all(blocks, ("pool", "tensor"), split_axis=0, concat_axis=0, tiled=True)


def gather_halves(rows, chips, work, *arrays):
    copies = jnp.broadcast_to(rows[None], (chips,) + rows.shape)
    own, done = beside(swap_chips, copies, work, *arrays)
    own = own.reshape(chips * rows.shape[0], rows.shape[1])
    return own, swap_cores(own), done


def scatter_halves(own_half, other_half, chips):
    added = own_half.astype(jnp.float32) + swap_cores(other_half).astype(jnp.float32)
    blocks = added.astype(jnp.bfloat16).reshape(chips, -1, own_half.shape[1])
    return jnp.sum(swap_chips(blocks).astype(jnp.float32), axis=0)


def dot_rows(left, right):
    return lax.dot_general(
        left, right, (((1,), (0,)), ((), ())), preferred_element_type=jnp.float32
    )


def dot_columns(left, right):
    return lax.dot_general(
        left, right, (((1,), (1,)), ((), ())), preferred_element_type=jnp.float32
    )


def pieces(extent, step):
    return [(start, min(step, extent - start)) for start in range(0, extent, step)]


IN_VMEM = pl.BlockSpec(memory_space=pltpu.VMEM)
IN_SMEM = pl.BlockSpec(memory_space=pltpu.SMEM)
IN_HBM = pl.BlockSpec(memory_space=pl.ANY)


def keep_in_hbm(array):
    return pltpu.with_memory_space_constraint(array, pltpu.HBM)


def keep_in_vmem(array):
    return pltpu.with_memory_space_constraint(array, pltpu.VMEM)


def fetch_kernel(count, *refs):
    sources, targets, sems = refs[:count], refs[count : 2 * count], refs[2 * count]
    copies = []
    for index, (source, target) in enumerate(zip(sources, targets)):
        rows, columns = target.shape
        copies.append(
            pltpu.make_async_copy(
                source.at[pl.ds(0, rows), pl.ds(0, columns)], target, sems.at[index]
            )
        )
    for copy in copies:
        copy.start()
    for copy in copies:
        copy.wait()


def fetch(arrays, shapes):
    size = sum(2 * rows * columns for rows, columns in shapes)
    return pl.pallas_call(
        functools.partial(fetch_kernel, len(arrays)),
        out_shape=tuple(
            pltpu.VMEM(shape, array.dtype) for array, shape in zip(arrays, shapes)
        ),
        in_specs=[IN_HBM] * len(arrays),
        out_specs=tuple([IN_VMEM] * len(arrays)),
        scratch_shapes=[pltpu.SemaphoreType.DMA((len(arrays),))],
        compiler_params=pltpu.CompilerParams(vmem_limit_bytes=MIB),
        cost_estimate=pl.CostEstimate(flops=0, bytes_accessed=size, transcendentals=0),
        name="fetch",
    )(*[keep_in_hbm(array) for array in arrays])


def project_kernel(slot_count, own, other, gain, slots, q_vm, k_vm, v_vm, out, normed):
    half = own.shape[0]
    for index, source in enumerate((own, other)):
        rows = source[...].astype(jnp.float32)
        scale = lax.rsqrt(jnp.mean(rows * rows, axis=-1, keepdims=True) + eps)
        normed[pl.ds(index * half, half), :] = (rows * scale * gain[...]).astype(jnp.bfloat16)
    query_part = dot_rows(normed[...], q_vm[...])
    key_part = dot_columns(normed[...], k_vm[...])
    value_part = dot_columns(normed[...], v_vm[...])
    projected = jnp.concatenate([query_part, key_part, value_part], axis=1).astype(jnp.bfloat16)
    places = lax.broadcasted_iota(jnp.int32, (out.shape[0] * slot_count, 2 * half), 0)
    chosen = jnp.where(slots[...] == places, 1.0, 0.0).astype(jnp.bfloat16)
    packed = dot_rows(chosen, projected)
    for owner in range(out.shape[0]):
        out[owner] = packed[owner * slot_count : (owner + 1) * slot_count, :].astype(jnp.bfloat16)


def project(own, other, gain, slots, weights, devices, slot_count):
    depth, query_cols = weights[0].shape
    width = query_cols + weights[1].shape[0] + weights[2].shape[0]
    return pl.pallas_call(
        functools.partial(project_kernel, slot_count),
        out_shape=jax.ShapeDtypeStruct((devices, slot_count, width), jnp.bfloat16),
        in_specs=[IN_VMEM] * 7,
        out_specs=IN_VMEM,
        scratch_shapes=[pltpu.VMEM((2 * own.shape[0], depth), jnp.bfloat16)],
        compiler_params=pltpu.CompilerParams(vmem_limit_bytes=8 * MIB),
        name="project",
    )(
        own,
        other,
        gain.reshape(1, depth),
        slots.reshape(1, -1),
        *[keep_in_vmem(weight) for weight in weights],
    )


def plan_kernel(
    slot_count,
    index,
    lengths,
    slots,
    frequency,
    key_hbm,
    value_hbm,
    first,
    last,
    cosine,
    sine,
    key_vm,
    value_vm,
    sems,
):
    copies = [
        pltpu.make_async_copy(key_hbm.at[pl.ds(0, key_vm.shape[0])], key_vm, sems.at[0]),
        pltpu.make_async_copy(value_hbm.at[pl.ds(0, value_vm.shape[0])], value_vm, sems.at[1]),
    ]
    for copy in copies:
        copy.start()
    start = index[0] * slot_count
    requests = slots.shape[1]
    place = slots[...] - start
    rows = lax.broadcasted_iota(jnp.int32, (slot_count, requests), 0)
    amounts = lengths[...].astype(jnp.float32)
    length = jnp.sum(jnp.where(place == rows, amounts, 0.0), axis=1, keepdims=True)
    offset = jnp.sum(
        jnp.where((place >= 0) & (place < rows), amounts, 0.0), axis=1, keepdims=True
    )
    angles = length * frequency[...]
    turn = jnp.sin(angles)
    lean = jnp.cos(angles)
    cosine[...] = jnp.concatenate([lean, lean], axis=1)
    sine[...] = jnp.concatenate([-turn, turn], axis=1)
    first[...] = jnp.broadcast_to(offset.astype(jnp.int32), first.shape)
    last[...] = jnp.broadcast_to((offset + length).astype(jnp.int32), last.shape)
    for copy in copies:
        copy.wait()


def plan(index, lengths, slots, head_dim, key_cache, value_cache, slot_count):
    tokens, width = key_cache.shape
    key_rows = min(tokens, FETCHED // (2 * width) // 256 * 256)
    value_rows = min(tokens, max(256, FETCHED // (2 * width) // 256 * 256 - key_rows))
    frequency = theta ** (-jnp.arange(head_dim // 2, dtype=jnp.float32) * 2.0 / head_dim)
    table = jax.ShapeDtypeStruct((slot_count, head_dim), jnp.float32)
    bound = jax.ShapeDtypeStruct((slot_count, head_dim), jnp.int32)
    return pl.pallas_call(
        functools.partial(plan_kernel, slot_count),
        out_shape=(
            bound,
            bound,
            table,
            table,
            pltpu.VMEM((key_rows, width), jnp.bfloat16),
            pltpu.VMEM((value_rows, width), jnp.bfloat16),
        ),
        in_specs=[IN_SMEM] + [IN_VMEM] * 3 + [IN_HBM] * 2,
        out_specs=tuple([IN_VMEM] * 6),
        scratch_shapes=[pltpu.SemaphoreType.DMA((2,))],
        compiler_params=pltpu.CompilerParams(vmem_limit_bytes=MIB),
        cost_estimate=pl.CostEstimate(
            flops=0, bytes_accessed=2 * width * (key_rows + value_rows), transcendentals=0
        ),
        name="plan",
    )(
        index,
        lengths.reshape(1, -1),
        slots.reshape(1, -1),
        frequency.reshape(1, -1),
        keep_in_hbm(key_cache),
        keep_in_hbm(value_cache),
    )


def attend_kernel(
    query_cols,
    key_cols,
    arrived,
    first,
    last,
    cosine,
    sine,
    query_gain,
    key_gain,
    key_near,
    value_near,
    key_hbm,
    value_hbm,
    out,
    key_far,
    value_far,
    queries,
    scores,
    sems,
):
    devices, slot_count, _ = arrived.shape
    tokens, width = key_hbm.shape
    head_dim = query_gain.shape[1]
    kv_count = devices * key_cols // head_dim
    sharers = devices // kv_count
    heads_here = query_cols // head_dim
    repeats = sharers * heads_here
    count = repeats * slot_count
    key_rows, value_rows = key_near.shape[0], value_near.shape[0]
    copies = []
    for source, target, start, sem in (
        (key_hbm, key_far, key_rows, 0),
        (value_hbm, value_far, value_rows, 1),
    ):
        if start < tokens:
            copies.append(
                pltpu.make_async_copy(
                    source.at[pl.ds(start, tokens - start)],
                    target.at[pl.ds(0, tokens - start)],
                    sems.at[sem],
                )
            )
    for copy in copies:
        copy.start()
    scale_factor = 1.0 / math.sqrt(head_dim)

    def tile(rows, times):
        return jnp.concatenate([rows] * times, axis=0)

    def prepare(rows, gain, times):
        rows = rows * lax.rsqrt(jnp.mean(rows * rows, axis=-1, keepdims=True) + eps) * gain[...]
        turned = pltpu.roll(rows, head_dim // 2, 1)
        return (rows * tile(cosine[...], times) + turned * tile(sine[...], times)).astype(
            jnp.bfloat16
        )

    blocks = [arrived[device].astype(jnp.float32) for device in range(devices)]
    rows = jnp.concatenate(
        [
            blocks[kv * sharers + place][:, head * head_dim : (head + 1) * head_dim]
            for kv in range(kv_count)
            for head in range(heads_here)
            for place in range(sharers)
        ],
        axis=0,
    )
    query = prepare(rows, query_gain, kv_count * repeats)

    def whole(begin):
        return [
            jnp.concatenate(
                [
                    blocks[kv * sharers + place][:, begin : begin + key_cols]
                    for place in range(sharers)
                ],
                axis=1,
            )
            for kv in range(kv_count)
        ]

    fresh = prepare(jnp.concatenate(whole(query_cols), axis=0), key_gain, kv_count)
    fresh = fresh.astype(jnp.float32)
    key_new = jnp.concatenate(
        [
            tile(fresh[kv * slot_count : (kv + 1) * slot_count, :], repeats)
            for kv in range(kv_count)
        ],
        axis=0,
    )
    value_new = [tile(rows, repeats) for rows in whole(query_cols + key_cols)]
    own_score = (
        jnp.sum(query.astype(jnp.float32) * key_new, axis=-1, keepdims=True) * scale_factor
    )
    queries[...] = jnp.zeros(queries.shape, queries.dtype)
    for kv in range(kv_count):
        queries[kv * count : (kv + 1) * count, kv * head_dim : (kv + 1) * head_dim] = query[
            kv * count : (kv + 1) * count, :
        ]
    start = tile(first[:, :1], kv_count * repeats)
    end = tile(last[:, :1], kv_count * repeats)
    step = 256
    largest = own_score
    for begin in range(0, tokens, step):
        if begin == key_rows:
            copies[0].wait()
        if begin < key_rows:
            keys = key_near[begin : begin + step, :]
        else:
            keys = key_far[begin - key_rows : begin - key_rows + step, :]
        positions = lax.broadcasted_iota(jnp.int32, (kv_count * count, step), 1) + begin
        inside = (positions >= start) & (positions < end)
        part = jnp.where(inside, dot_columns(queries[...], keys) * scale_factor, -1e30)
        scores[:, begin : begin + step] = part
        largest = jnp.maximum(largest, jnp.max(part, axis=1, keepdims=True))
    own_weight = jnp.exp(own_score - largest)
    denominator = own_weight
    summed = jnp.zeros((kv_count * count, width), jnp.float32)
    for begin in range(0, tokens, step):
        if begin == value_rows:
            copies[-1].wait()
        if begin < value_rows:
            values = value_near[begin : begin + step, :]
        else:
            values = value_far[begin - value_rows : begin - value_rows + step, :]
        weights = jnp.exp(scores[:, begin : begin + step] - largest)
        denominator = denominator + jnp.sum(weights, axis=1, keepdims=True)
        summed = summed + dot_rows(weights.astype(jnp.bfloat16), values)
    own_low = own_weight.astype(jnp.bfloat16).astype(jnp.float32)
    for kv in range(kv_count):
        span = slice(kv * count, (kv + 1) * count)
        mine = summed[span, kv * head_dim : (kv + 1) * head_dim]
        mine = (mine + own_low[span, :] * value_new[kv]) / denominator[span, :]
        for head in range(heads_here):
            for place in range(sharers):
                row = (head * sharers + place) * slot_count
                out[kv * sharers + place, :, head * head_dim : (head + 1) * head_dim] = mine[
                    row : row + slot_count, :
                ].astype(jnp.bfloat16)


def attend(arrived, planned, query_gain, key_gain, key_cache, value_cache, query_cols):
    first, last, cosine, sine, key_near, value_near = planned
    devices, slot_count, width = arrived.shape
    key_cols = (width - query_cols) // 2
    head_dim = query_gain.shape[0]
    tokens, cache_width = key_cache.shape
    rows = devices * query_cols // head_dim * slot_count
    return pl.pallas_call(
        functools.partial(attend_kernel, query_cols, key_cols),
        out_shape=jax.ShapeDtypeStruct((devices, slot_count, query_cols), jnp.bfloat16),
        in_specs=[IN_VMEM] * 9 + [IN_HBM] * 2,
        out_specs=IN_VMEM,
        scratch_shapes=[
            pltpu.VMEM((max(16, tokens - key_near.shape[0]), cache_width), jnp.bfloat16),
            pltpu.VMEM((max(16, tokens - value_near.shape[0]), cache_width), jnp.bfloat16),
            pltpu.VMEM((rows, cache_width), jnp.bfloat16),
            pltpu.VMEM((rows, tokens), jnp.float32),
            pltpu.SemaphoreType.DMA((2,)),
        ],
        compiler_params=pltpu.CompilerParams(vmem_limit_bytes=24 * MIB),
        name="attend",
    )(
        arrived,
        first,
        last,
        cosine,
        sine,
        query_gain.reshape(1, head_dim),
        key_gain.reshape(1, head_dim),
        keep_in_vmem(key_near),
        keep_in_vmem(value_near),
        keep_in_hbm(key_cache),
        keep_in_hbm(value_cache),
    )


def mix_kernel(returned, slots, weight, own_out, other_out):
    owners, slot_count, _ = returned.shape
    half, width = own_out.shape
    by_slot = jnp.concatenate(
        [returned[owner].astype(jnp.float32) for owner in range(owners)], axis=0
    ).astype(jnp.bfloat16)
    places = lax.broadcasted_iota(jnp.int32, (2 * half, owners * slot_count), 1)
    chosen = jnp.where(slots[...] == places, 1.0, 0.0).astype(jnp.bfloat16)
    rows = dot_rows(chosen, by_slot).astype(jnp.bfloat16)
    for start, size in pieces(width, 1024):
        total = dot_rows(rows, weight[:, start : start + size])
        own_out[:, start : start + size] = total[:half].astype(own_out.dtype)
        other_out[:, start : start + size] = total[half:].astype(other_out.dtype)


def mix(returned, slots, output_weight, requests):
    half, width = requests // 2, output_weight.shape[1]
    return pl.pallas_call(
        mix_kernel,
        out_shape=(
            jax.ShapeDtypeStruct((half, width), jnp.float32),
            jax.ShapeDtypeStruct((half, width), jnp.bfloat16),
        ),
        in_specs=[IN_VMEM] * 3,
        out_specs=(IN_VMEM, IN_VMEM),
        compiler_params=pltpu.CompilerParams(vmem_limit_bytes=8 * MIB),
        name="mix",
    )(returned, slots.reshape(-1, 1), keep_in_vmem(output_weight))


def feed_kernel(
    own,
    other,
    gate_near,
    up_near,
    gate_hbm,
    up_hbm,
    down_hbm,
    own_out,
    other_out,
    rows,
    gate_vm,
    up_vm,
    down_vm,
    sems,
):
    half, width = own.shape
    near = gate_near.shape[1]
    step = 512

    def copy_columns(source, target, row, parts):
        copies = [
            pltpu.make_async_copy(
                source.at[:, pl.ds(start, size)],
                target.at[:, pl.ds(start, size)],
                sems.at[row, index],
            )
            for index, (start, size) in enumerate(parts)
        ]
        return copies

    far = pieces(width, step)[near // step :]
    gate_copies = copy_columns(gate_hbm, gate_vm, 0, far)
    up_copies = copy_columns(up_hbm, up_vm, 1, far)
    parts = pieces(width, step)
    down_copies = copy_columns(down_hbm, down_vm, 2, parts)
    for gate_copy, up_copy in zip(gate_copies, up_copies):
        gate_copy.start()
        up_copy.start()
    for copy in down_copies:
        copy.start()
    rows[:half, :] = own[...]
    rows[half:, :] = other[...]
    gate_part = dot_columns(rows[:, :near], gate_near[...])
    up_part = dot_columns(rows[:, :near], up_near[...])
    for index, (start, size) in enumerate(far):
        some = rows[:, start : start + size]
        gate_copies[index].wait()
        gate_part = gate_part + dot_columns(some, gate_vm[:, start : start + size])
        up_copies[index].wait()
        up_part = up_part + dot_columns(some, up_vm[:, start : start + size])
    active = (gate_part / (1.0 + jnp.exp(-gate_part)) * up_part).astype(jnp.bfloat16)
    for index, (start, size) in enumerate(parts):
        down_copies[index].wait()
        total = dot_rows(active, down_vm[:, start : start + size])
        own_out[:, start : start + size] = total[:half].astype(own_out.dtype)
        other_out[:, start : start + size] = total[half:].astype(other_out.dtype)


def feed(own, other, near, gate_weight, up_weight, down_weight):
    half, width = own.shape
    units = down_weight.shape[0]
    return pl.pallas_call(
        feed_kernel,
        out_shape=(
            jax.ShapeDtypeStruct((half, width), jnp.float32),
            jax.ShapeDtypeStruct((half, width), jnp.bfloat16),
        ),
        in_specs=[IN_VMEM] * 4 + [IN_HBM] * 3,
        out_specs=(IN_VMEM, IN_VMEM),
        scratch_shapes=[
            pltpu.VMEM((2 * half, width), jnp.bfloat16),
            pltpu.VMEM((units, width), jnp.bfloat16),
            pltpu.VMEM((units, width), jnp.bfloat16),
            pltpu.VMEM((units, width), jnp.bfloat16),
            pltpu.SemaphoreType.DMA((3, len(pieces(width, 512)))),
        ],
        compiler_params=pltpu.CompilerParams(vmem_limit_bytes=40 * MIB),
        name="feed",
    )(
        own,
        other,
        *[keep_in_vmem(array) for array in near],
        keep_in_hbm(gate_weight),
        keep_in_hbm(up_weight),
        keep_in_hbm(down_weight),
    )


def halves_first(values, half):
    swapped = jnp.concatenate([values[half:], values[:half]])
    return jnp.where(lax.axis_index("pool") == 0, values, swapped)


def on_device_kernels(
    hidden,
    input_gain,
    query_weight,
    key_weight,
    value_weight,
    query_gain,
    key_gain,
    output_weight,
    post_gain,
    gate_weight,
    up_weight,
    down_weight,
    key_cache,
    value_cache,
    lengths,
    request_slot,
):
    devices = lax.axis_size(("pool", "tensor"))
    chips = lax.axis_size("tensor")
    device_index = lax.axis_index(("pool", "tensor"))
    requests = lengths.shape[0]
    half = requests // 2
    slot_count = SLOTS
    query_cols = query_weight.shape[1]
    head_dim = query_gain.shape[0]
    width = hidden.shape[1]
    index = device_index.astype(jnp.int32).reshape(1)

    def fetch_whole(*arrays):
        return fetch(arrays, [array.shape for array in arrays])

    def fetch_columns(*arrays):
        columns = FETCHED // sum(2 * array.shape[0] for array in arrays) // 512 * 512
        return fetch(arrays, [(array.shape[0], min(columns, width // 2)) for array in arrays])

    def plan_here(*arrays):
        return plan(*arrays[:3], head_dim, *arrays[3:], slot_count)

    own, other, weights = gather_halves(
        hidden, chips, fetch_whole, query_weight, key_weight.T, value_weight.T
    )
    slots = halves_first(request_slot, half)
    outgoing = project(own, other, input_gain, slots, weights, devices, slot_count)
    arrived, planned = beside(
        swap_all, outgoing, plan_here, index, lengths, request_slot, key_cache, value_cache
    )
    head_out = attend(
        arrived, planned, query_gain, key_gain, key_cache, value_cache, query_cols
    )
    returned, weights = beside(swap_all, head_out, fetch_whole, output_weight)
    own_sum, other_sum = mix(returned, slots, weights[0], requests)
    mixed_rows = (
        hidden.astype(jnp.float32) + scatter_halves(own_sum, other_sum, chips)
    ).astype(jnp.bfloat16)
    post_normed = rms_scale(mixed_rows, post_gain).astype(jnp.bfloat16)
    gate_rows, up_rows = gate_weight.T, up_weight.T
    own, other, near = gather_halves(post_normed, chips, fetch_columns, gate_rows, up_rows)
    own_sum, other_sum = feed(own, other, near, gate_rows, up_rows, down_weight)
    lowered = scatter_halves(own_sum, other_sum, chips)
    final_rows = (mixed_rows.astype(jnp.float32) + lowered).astype(jnp.bfloat16)
    return (mixed_rows, final_rows)


def gather_rows(rows, devices):
    copies = jnp.broadcast_to(rows[None], (devices,) + rows.shape)
    arrived = lax.all_to_all(copies, ("pool", "tensor"), split_axis=0, concat_axis=0, tiled=True)
    return arrived.reshape(devices * rows.shape[0], rows.shape[1])


def scatter_sum(partial, devices):
    blocks = partial.astype(jnp.bfloat16).reshape(devices, -1, partial.shape[1])
    arrived = lax.all_to_all(blocks, ("pool", "tensor"), split_axis=0, concat_axis=0, tiled=True)
    return jnp.sum(arrived.astype(jnp.float32), axis=0)


def on_device_general(
    hidden,
    input_gain,
    query_weight,
    key_weight,
    value_weight,
    query_gain,
    key_gain,
    output_weight,
    post_gain,
    gate_weight,
    up_weight,
    down_weight,
    key_cache,
    value_cache,
    lengths,
    request_slot,
):
    devices = lax.axis_size(("pool", "tensor"))
    device_index = lax.axis_index(("pool", "tensor"))
    local_rows = hidden.shape[0]
    query_cols = query_weight.shape[1]
    key_cols = key_weight.shape[1]
    width_sent = query_cols + 2 * key_cols
    head_dim = query_gain.shape[0]
    slot_count = SLOTS
    head_count = devices * query_cols // head_dim
    kv_count = devices * key_cols // head_dim
    group_size = head_count // kv_count
    normed = rms_scale(hidden, input_gain).astype(jnp.bfloat16)
    shard_rows = gather_rows(normed, devices)
    query_part = jnp.dot(shard_rows, query_weight, preferred_element_type=jnp.float32)
    key_part = jnp.dot(shard_rows, key_weight, preferred_element_type=jnp.float32)
    value_part = jnp.dot(shard_rows, value_weight, preferred_element_type=jnp.float32)
    projected = jnp.concatenate([query_part, key_part, value_part], axis=1).astype(jnp.bfloat16)
    outgoing = (
        jnp.zeros((devices * slot_count, width_sent), jnp.bfloat16).at[request_slot].set(projected)
    )
    outgoing = outgoing.reshape(devices, slot_count, width_sent)
    arrived = lax.all_to_all(
        outgoing, ("pool", "tensor"), split_axis=0, concat_axis=2, tiled=True
    ).reshape(slot_count, devices, width_sent)
    query_full = arrived[:, :, :query_cols].reshape(slot_count, head_count, head_dim)
    key_full = arrived[:, :, query_cols : query_cols + key_cols].reshape(
        slot_count, kv_count, head_dim
    )
    value_new = arrived[:, :, query_cols + key_cols :].reshape(slot_count, kv_count, head_dim)
    slot_ids = device_index * slot_count + jnp.arange(slot_count, dtype=jnp.int32)
    matches = request_slot[None, :] == slot_ids[:, None]
    slot_length = jnp.sum(jnp.where(matches, lengths[None, :], 0), axis=1)
    owner_of = request_slot // slot_count
    within = request_slot % slot_count
    earlier = (owner_of[None, :] == device_index) & (
        within[None, :] < jnp.arange(slot_count, dtype=jnp.int32)[:, None]
    )
    slot_offset = jnp.sum(jnp.where(earlier, lengths[None, :], 0), axis=1)
    position = slot_length.astype(jnp.float32)[:, None, None]
    query_heads = rotate(rms_scale(query_full, query_gain), position).astype(jnp.bfloat16)
    query_heads = query_heads.reshape(slot_count, kv_count, group_size, head_dim)
    key_new = rotate(rms_scale(key_full, key_gain), position).astype(jnp.bfloat16)
    pool_tokens = key_cache.shape[0]
    scale_factor = 1.0 / math.sqrt(head_dim)
    scores = jnp.stack(
        [
            jnp.einsum(
                "sgd,td->sgt",
                query_heads[:, kv],
                key_cache[:, kv * head_dim : (kv + 1) * head_dim],
                preferred_element_type=jnp.float32,
            )
            for kv in range(kv_count)
        ],
        axis=1,
    ) * scale_factor
    own_score = (
        jnp.einsum("skgd,skd->skg", query_heads, key_new, preferred_element_type=jnp.float32)
        * scale_factor
    )
    token_pos = jnp.arange(pool_tokens, dtype=jnp.int32)
    inside = (token_pos[None, :] >= slot_offset[:, None]) & (
        token_pos[None, :] < (slot_offset + slot_length)[:, None]
    )
    inside = inside[:, None, None, :]
    largest = jnp.maximum(jnp.max(jnp.where(inside, scores, -1e30), axis=3), own_score)
    weights = jnp.where(inside, jnp.exp(scores - largest[..., None]), 0.0)
    own_weight = jnp.exp(own_score - largest)
    denominator = jnp.sum(weights, axis=3) + own_weight
    weights_low = weights.astype(jnp.bfloat16)
    summed = jnp.stack(
        [
            jnp.einsum(
                "sgt,td->sgd",
                weights_low[:, kv],
                value_cache[:, kv * head_dim : (kv + 1) * head_dim],
                preferred_element_type=jnp.float32,
            )
            for kv in range(kv_count)
        ],
        axis=1,
    )
    own_low = own_weight.astype(jnp.bfloat16).astype(jnp.float32)
    summed = summed + own_low[..., None] * value_new.astype(jnp.float32)[:, :, None, :]
    head_out = (
        (summed / denominator[..., None])
        .astype(jnp.bfloat16)
        .reshape(slot_count, devices, query_cols)
    )
    returned = lax.all_to_all(head_out, ("pool", "tensor"), split_axis=1, concat_axis=0, tiled=True)
    head_rows = returned.reshape(devices * slot_count, query_cols)[request_slot]
    partial_value = jnp.dot(head_rows, output_weight, preferred_element_type=jnp.float32)
    mixed_rows = (hidden.astype(jnp.float32) + scatter_sum(partial_value, devices)).astype(jnp.bfloat16)
    post_normed = gather_rows(rms_scale(mixed_rows, post_gain).astype(jnp.bfloat16), devices)
    gate_part = jnp.dot(post_normed, gate_weight, preferred_element_type=jnp.float32)
    up_part = jnp.dot(post_normed, up_weight, preferred_element_type=jnp.float32)
    activated = (jax.nn.silu(gate_part) * up_part).astype(jnp.bfloat16)
    lowered = scatter_sum(
        jnp.dot(activated, down_weight, preferred_element_type=jnp.float32), devices
    )
    final_rows = (mixed_rows.astype(jnp.float32) + lowered).astype(jnp.bfloat16)
    return (mixed_rows, final_rows)


def on_device(*arrays):
    query_cols, key_cols = arrays[2].shape[1], arrays[3].shape[1]
    head_dim = arrays[5].shape[0]
    devices = lax.axis_size(("pool", "tensor"))
    kv_count = devices * key_cols // head_dim
    whole_heads = query_cols % head_dim == 0 and head_dim % LANES == 0
    shared = kv_count > 0 and devices % kv_count == 0
    pairs = lax.axis_size("pool") == 2 and arrays[14].shape[0] % 16 == 0
    if whole_heads and shared and pairs:
        return on_device_kernels(*arrays)
    return on_device_general(*arrays)


def solution(mesh):
    placed = (
        P(("groups", "pool", "tensor"), None),
        P(),
        P(None, ("pool", "tensor")),
        P(None, ("pool", "tensor")),
        P(None, ("pool", "tensor")),
        P(),
        P(),
        P(("pool", "tensor"), None),
        P(),
        P(None, ("pool", "tensor")),
        P(None, ("pool", "tensor")),
        P(("pool", "tensor"), None),
        P(("groups", "pool", "tensor"), None),
        P(("groups", "pool", "tensor"), None),
        P("groups"),
        P("groups"),
    )
    return jax.shard_map(
        on_device,
        mesh=mesh,
        in_specs=placed,
        out_specs=(P(("groups", "pool", "tensor"), None), P(("groups", "pool", "tensor"), None)),
        check_vma=False,
    )
```

```python
import functools
import math

import jax
import jax.numpy as jnp
from jax import lax
from jax.experimental import pallas as pl
from jax.experimental.pallas import tpu as pltpu
from jax.sharding import PartitionSpec as P

SLOTS = 4
LANES = 128
MIB = 2**20
FETCHED = 13 * MIB // 4
FEED_STEP = 512


eps = 1e-06
theta = 1000000.0


def rms_scale(values, scales):
    values = values.astype(jnp.float32)
    return values * lax.rsqrt(jnp.mean(values * values, axis=-1, keepdims=True) + eps) * scales


def rotate(values, position):
    half_width = values.shape[-1] // 2
    frequency = theta ** (-jnp.arange(half_width, dtype=jnp.float32) * 2.0 / values.shape[-1])
    angles = position * frequency
    cosine = jnp.cos(angles)
    sine_part = jnp.sin(angles)
    front_half = values[..., :half_width]
    back_half = values[..., half_width:]
    return jnp.concatenate(
        [front_half * cosine - back_half * sine_part, back_half * cosine + front_half * sine_part],
        axis=-1,
    )


def swap_cores(block):
    return lax.ppermute(block, "pool", [(0, 1), (1, 0)])


def beside(exchange, blocks, work, *arrays):
    blocks, arrays = lax.optimization_barrier((blocks, arrays))
    return lax.optimization_barrier((exchange(blocks), work(*arrays)))


def swap_chips(blocks):
    return lax.all_to_all(blocks, "tensor", split_axis=0, concat_axis=0, tiled=True)


def swap_all(blocks):
    return lax.all_to_all(blocks, ("pool", "tensor"), split_axis=0, concat_axis=0, tiled=True)


def gather_half(rows, chips, work, *arrays):
    copies = jnp.broadcast_to(rows[None], (chips,) + rows.shape)
    return beside(swap_chips, copies, work, *arrays)


def scatter_halves(own_half, other_half, chips):
    added = own_half.astype(jnp.float32) + swap_cores(other_half).astype(jnp.float32)
    blocks = added.astype(jnp.bfloat16).reshape(chips, -1, own_half.shape[1])
    return jnp.sum(swap_chips(blocks).astype(jnp.float32), axis=0)


def dot_rows(left, right):
    return lax.dot_general(
        left, right, (((1,), (0,)), ((), ())), preferred_element_type=jnp.float32
    )


def dot_columns(left, right):
    return lax.dot_general(
        left, right, (((1,), (1,)), ((), ())), preferred_element_type=jnp.float32
    )


def pieces(extent, step):
    return [(start, min(step, extent - start)) for start in range(0, extent, step)]


IN_VMEM = pl.BlockSpec(memory_space=pltpu.VMEM)
IN_SMEM = pl.BlockSpec(memory_space=pltpu.SMEM)
IN_HBM = pl.BlockSpec(memory_space=pl.ANY)


def keep_in_hbm(array):
    return pltpu.with_memory_space_constraint(array, pltpu.HBM)


def keep_in_vmem(array):
    return pltpu.with_memory_space_constraint(array, pltpu.VMEM)


def fetch_kernel(begin, *refs):
    count = len(refs) // 2
    sources, targets, sems = refs[:count], refs[count : 2 * count], refs[2 * count]
    copies = [
        pltpu.make_async_copy(
            source.at[:, pl.ds(begin, target.shape[1])], target, sems.at[index]
        )
        for index, (source, target) in enumerate(zip(sources, targets))
    ]
    for copy in copies:
        copy.start()
    for copy in copies:
        copy.wait()


def fetch(arrays, begin, end):
    shapes = [(array.shape[0], min(array.shape[1], end) - begin) for array in arrays]
    size = sum(2 * rows * columns for rows, columns in shapes)
    return pl.pallas_call(
        functools.partial(fetch_kernel, begin),
        out_shape=tuple(
            pltpu.VMEM(shape, array.dtype) for array, shape in zip(arrays, shapes)
        ),
        in_specs=[IN_HBM] * len(arrays),
        out_specs=tuple([IN_VMEM] * len(arrays)),
        scratch_shapes=[pltpu.SemaphoreType.DMA((len(arrays),))],
        compiler_params=pltpu.CompilerParams(vmem_limit_bytes=MIB),
        cost_estimate=pl.CostEstimate(flops=0, bytes_accessed=size, transcendentals=0),
        name="fetch",
    )(*[keep_in_hbm(array) for array in arrays])


def flat_rows(blocks):
    return jnp.concatenate(
        [blocks[chip].astype(jnp.float32) for chip in range(blocks.shape[0])], axis=0
    )


def project_kernel(slot_count, own, other, gain, slots, q_vm, k_vm, v_vm, out, normed):
    half = own.shape[0] * own.shape[1]
    for index, source in enumerate((own, other)):
        rows = flat_rows(source)
        scale = lax.rsqrt(jnp.mean(rows * rows, axis=-1, keepdims=True) + eps)
        normed[pl.ds(index * half, half), :] = (rows * scale * gain[...]).astype(jnp.bfloat16)
    query_part = dot_rows(normed[...], q_vm[...])
    key_part = dot_columns(normed[...], k_vm[...])
    value_part = dot_columns(normed[...], v_vm[...])
    projected = jnp.concatenate([query_part, key_part, value_part], axis=1).astype(jnp.bfloat16)
    places = lax.broadcasted_iota(jnp.int32, (out.shape[0] * slot_count, 2 * half), 0)
    chosen = jnp.where(slots[...] == places, 1.0, 0.0).astype(jnp.bfloat16)
    packed = dot_rows(chosen, projected)
    for owner in range(out.shape[0]):
        out[owner] = packed[owner * slot_count : (owner + 1) * slot_count, :].astype(jnp.bfloat16)


def project(own, other, gain, slots, weights, devices, slot_count):
    depth, query_cols = weights[0].shape
    width = query_cols + weights[1].shape[0] + weights[2].shape[0]
    return pl.pallas_call(
        functools.partial(project_kernel, slot_count),
        out_shape=jax.ShapeDtypeStruct((devices, slot_count, width), jnp.bfloat16),
        in_specs=[IN_VMEM] * 7,
        out_specs=IN_VMEM,
        scratch_shapes=[pltpu.VMEM((slots.shape[0], depth), jnp.bfloat16)],
        compiler_params=pltpu.CompilerParams(vmem_limit_bytes=8 * MIB),
        name="project",
    )(
        own,
        other,
        gain.reshape(1, depth),
        slots.reshape(1, -1),
        *[keep_in_vmem(weight) for weight in weights],
    )


def plan_kernel(
    slot_count,
    index,
    lengths,
    slots,
    frequency,
    key_hbm,
    value_hbm,
    first,
    last,
    cosine,
    sine,
    key_vm,
    value_vm,
    sems,
):
    copies = [
        pltpu.make_async_copy(key_hbm.at[pl.ds(0, key_vm.shape[0])], key_vm, sems.at[0]),
        pltpu.make_async_copy(value_hbm.at[pl.ds(0, value_vm.shape[0])], value_vm, sems.at[1]),
    ]
    for copy in copies:
        copy.start()
    start = index[0] * slot_count
    requests = slots.shape[1]
    place = slots[...] - start
    rows = lax.broadcasted_iota(jnp.int32, (slot_count, requests), 0)
    amounts = lengths[...].astype(jnp.float32)
    length = jnp.sum(jnp.where(place == rows, amounts, 0.0), axis=1, keepdims=True)
    offset = jnp.sum(
        jnp.where((place >= 0) & (place < rows), amounts, 0.0), axis=1, keepdims=True
    )
    angles = length * frequency[...]
    turn = jnp.sin(angles)
    lean = jnp.cos(angles)
    cosine[...] = jnp.concatenate([lean, lean], axis=1)
    sine[...] = jnp.concatenate([-turn, turn], axis=1)
    first[...] = jnp.broadcast_to(offset.astype(jnp.int32), first.shape)
    last[...] = jnp.broadcast_to((offset + length).astype(jnp.int32), last.shape)
    for copy in copies:
        copy.wait()


def plan(index, lengths, slots, head_dim, key_cache, value_cache, slot_count):
    tokens, width = key_cache.shape
    key_rows = min(tokens, FETCHED // (2 * width) // 256 * 256)
    value_rows = min(tokens, max(256, FETCHED // (2 * width) // 256 * 256 - key_rows))
    frequency = theta ** (-jnp.arange(head_dim // 2, dtype=jnp.float32) * 2.0 / head_dim)
    table = jax.ShapeDtypeStruct((slot_count, head_dim), jnp.float32)
    bound = jax.ShapeDtypeStruct((slot_count, head_dim), jnp.int32)
    return pl.pallas_call(
        functools.partial(plan_kernel, slot_count),
        out_shape=(
            bound,
            bound,
            table,
            table,
            pltpu.VMEM((key_rows, width), jnp.bfloat16),
            pltpu.VMEM((value_rows, width), jnp.bfloat16),
        ),
        in_specs=[IN_SMEM] + [IN_VMEM] * 3 + [IN_HBM] * 2,
        out_specs=tuple([IN_VMEM] * 6),
        scratch_shapes=[pltpu.SemaphoreType.DMA((2,))],
        compiler_params=pltpu.CompilerParams(vmem_limit_bytes=MIB),
        cost_estimate=pl.CostEstimate(
            flops=0, bytes_accessed=2 * width * (key_rows + value_rows), transcendentals=0
        ),
        name="plan",
    )(
        index,
        lengths.reshape(1, -1),
        slots.reshape(1, -1),
        frequency.reshape(1, -1),
        keep_in_hbm(key_cache),
        keep_in_hbm(value_cache),
    )


def attend_kernel(
    query_cols,
    key_cols,
    arrived,
    first,
    last,
    cosine,
    sine,
    query_gain,
    key_gain,
    key_near,
    value_near,
    key_hbm,
    value_hbm,
    out,
    key_far,
    value_far,
    queries,
    scores,
    sems,
):
    devices, slot_count, _ = arrived.shape
    tokens, width = key_hbm.shape
    head_dim = query_gain.shape[1]
    kv_count = devices * key_cols // head_dim
    sharers = devices // kv_count
    heads_here = query_cols // head_dim
    repeats = sharers * heads_here
    count = repeats * slot_count
    key_rows, value_rows = key_near.shape[0], value_near.shape[0]
    copies = []
    for source, target, start, sem in (
        (key_hbm, key_far, key_rows, 0),
        (value_hbm, value_far, value_rows, 1),
    ):
        if start < tokens:
            copies.append(
                pltpu.make_async_copy(
                    source.at[pl.ds(start, tokens - start)],
                    target.at[pl.ds(0, tokens - start)],
                    sems.at[sem],
                )
            )
    for copy in copies:
        copy.start()
    scale_factor = 1.0 / math.sqrt(head_dim)

    def tile(rows, times):
        return jnp.concatenate([rows] * times, axis=0)

    def prepare(rows, gain, times):
        rows = rows * lax.rsqrt(jnp.mean(rows * rows, axis=-1, keepdims=True) + eps) * gain[...]
        turned = pltpu.roll(rows, head_dim // 2, 1)
        return (rows * tile(cosine[...], times) + turned * tile(sine[...], times)).astype(
            jnp.bfloat16
        )

    blocks = [arrived[device].astype(jnp.float32) for device in range(devices)]
    rows = jnp.concatenate(
        [
            blocks[kv * sharers + place][:, head * head_dim : (head + 1) * head_dim]
            for kv in range(kv_count)
            for head in range(heads_here)
            for place in range(sharers)
        ],
        axis=0,
    )
    query = prepare(rows, query_gain, kv_count * repeats)

    def whole(begin):
        return [
            jnp.concatenate(
                [
                    blocks[kv * sharers + place][:, begin : begin + key_cols]
                    for place in range(sharers)
                ],
                axis=1,
            )
            for kv in range(kv_count)
        ]

    fresh = prepare(jnp.concatenate(whole(query_cols), axis=0), key_gain, kv_count)
    fresh = fresh.astype(jnp.float32)
    key_new = jnp.concatenate(
        [
            tile(fresh[kv * slot_count : (kv + 1) * slot_count, :], repeats)
            for kv in range(kv_count)
        ],
        axis=0,
    )
    value_new = [tile(rows, repeats) for rows in whole(query_cols + key_cols)]
    own_score = (
        jnp.sum(query.astype(jnp.float32) * key_new, axis=-1, keepdims=True) * scale_factor
    )
    queries[...] = jnp.zeros(queries.shape, queries.dtype)
    for kv in range(kv_count):
        queries[kv * count : (kv + 1) * count, kv * head_dim : (kv + 1) * head_dim] = query[
            kv * count : (kv + 1) * count, :
        ]
    start = tile(first[:, :1], kv_count * repeats)
    end = tile(last[:, :1], kv_count * repeats)
    step = 256
    largest = own_score
    for begin in range(0, tokens, step):
        if begin == key_rows:
            copies[0].wait()
        if begin < key_rows:
            keys = key_near[begin : begin + step, :]
        else:
            keys = key_far[begin - key_rows : begin - key_rows + step, :]
        positions = lax.broadcasted_iota(jnp.int32, (kv_count * count, step), 1) + begin
        inside = (positions >= start) & (positions < end)
        part = jnp.where(inside, dot_columns(queries[...], keys) * scale_factor, -1e30)
        scores[:, begin : begin + step] = part
        largest = jnp.maximum(largest, jnp.max(part, axis=1, keepdims=True))
    own_weight = jnp.exp(own_score - largest)
    denominator = own_weight
    summed = jnp.zeros((kv_count * count, width), jnp.float32)
    for begin in range(0, tokens, step):
        if begin == value_rows:
            copies[-1].wait()
        if begin < value_rows:
            values = value_near[begin : begin + step, :]
        else:
            values = value_far[begin - value_rows : begin - value_rows + step, :]
        weights = jnp.exp(scores[:, begin : begin + step] - largest)
        denominator = denominator + jnp.sum(weights, axis=1, keepdims=True)
        summed = summed + dot_rows(weights.astype(jnp.bfloat16), values)
    own_low = own_weight.astype(jnp.bfloat16).astype(jnp.float32)
    for kv in range(kv_count):
        span = slice(kv * count, (kv + 1) * count)
        mine = summed[span, kv * head_dim : (kv + 1) * head_dim]
        mine = (mine + own_low[span, :] * value_new[kv]) / denominator[span, :]
        for head in range(heads_here):
            for place in range(sharers):
                row = (head * sharers + place) * slot_count
                out[kv * sharers + place, :, head * head_dim : (head + 1) * head_dim] = mine[
                    row : row + slot_count, :
                ].astype(jnp.bfloat16)


def attend(arrived, planned, query_gain, key_gain, key_cache, value_cache, query_cols):
    first, last, cosine, sine, key_near, value_near = planned
    devices, slot_count, width = arrived.shape
    key_cols = (width - query_cols) // 2
    head_dim = query_gain.shape[0]
    tokens, cache_width = key_cache.shape
    rows = devices * query_cols // head_dim * slot_count
    return pl.pallas_call(
        functools.partial(attend_kernel, query_cols, key_cols),
        out_shape=jax.ShapeDtypeStruct((devices, slot_count, query_cols), jnp.bfloat16),
        in_specs=[IN_VMEM] * 9 + [IN_HBM] * 2,
        out_specs=IN_VMEM,
        scratch_shapes=[
            pltpu.VMEM((max(16, tokens - key_near.shape[0]), cache_width), jnp.bfloat16),
            pltpu.VMEM((max(16, tokens - value_near.shape[0]), cache_width), jnp.bfloat16),
            pltpu.VMEM((rows, cache_width), jnp.bfloat16),
            pltpu.VMEM((rows, tokens), jnp.float32),
            pltpu.SemaphoreType.DMA((2,)),
        ],
        compiler_params=pltpu.CompilerParams(vmem_limit_bytes=24 * MIB),
        name="attend",
    )(
        arrived,
        first,
        last,
        cosine,
        sine,
        query_gain.reshape(1, head_dim),
        key_gain.reshape(1, head_dim),
        keep_in_vmem(key_near),
        keep_in_vmem(value_near),
        keep_in_hbm(key_cache),
        keep_in_hbm(value_cache),
    )


def mix_kernel(returned, slots, weight, own_out, other_out):
    owners, slot_count, _ = returned.shape
    half, width = own_out.shape
    by_slot = jnp.concatenate(
        [returned[owner].astype(jnp.float32) for owner in range(owners)], axis=0
    ).astype(jnp.bfloat16)
    places = lax.broadcasted_iota(jnp.int32, (2 * half, owners * slot_count), 1)
    chosen = jnp.where(slots[...] == places, 1.0, 0.0).astype(jnp.bfloat16)
    rows = dot_rows(chosen, by_slot).astype(jnp.bfloat16)
    for start, size in pieces(width, 1024):
        total = dot_rows(rows, weight[:, start : start + size])
        own_out[:, start : start + size] = total[:half].astype(own_out.dtype)
        other_out[:, start : start + size] = total[half:].astype(other_out.dtype)


def mix(returned, slots, output_weight, requests):
    half, width = requests // 2, output_weight.shape[1]
    return pl.pallas_call(
        mix_kernel,
        out_shape=(
            jax.ShapeDtypeStruct((half, width), jnp.float32),
            jax.ShapeDtypeStruct((half, width), jnp.bfloat16),
        ),
        in_specs=[IN_VMEM] * 3,
        out_specs=(IN_VMEM, IN_VMEM),
        compiler_params=pltpu.CompilerParams(vmem_limit_bytes=8 * MIB),
        name="mix",
    )(returned, slots.reshape(-1, 1), keep_in_vmem(output_weight))


def feed_kernel(
    own,
    other,
    gate_near,
    up_near,
    gate_hbm,
    up_hbm,
    down_hbm,
    own_out,
    other_out,
    rows,
    gate_vm,
    up_vm,
    down_vm,
    sems,
):
    half, width = own_out.shape
    reach = gate_near.shape[1]

    near = reach // FEED_STEP
    parts = pieces(width, FEED_STEP)

    def copy_columns(source, target, row, index):
        start, size = parts[index]
        copy = pltpu.make_async_copy(
            source.at[:, pl.ds(start, size)], target.at[:, pl.ds(start, size)], sems.at[row, index]
        )
        copy.start()
        return copy

    unit_copies = [
        [copy_columns(gate_hbm, gate_vm, 0, index), copy_columns(up_hbm, up_vm, 1, index)]
        for index in range(near, len(parts))
    ]
    down_copies = [copy_columns(down_hbm, down_vm, 2, index) for index in range(len(parts))]
    rows[:half, :] = flat_rows(own).astype(jnp.bfloat16)
    rows[half:, :] = flat_rows(other).astype(jnp.bfloat16)
    gate_part = up_part = 0.0
    for index, (start, size) in enumerate(parts):
        gate, up = (gate_near, up_near) if index < near else (gate_vm, up_vm)
        if index >= near and (index - near) % 2 == 0:
            for copies in unit_copies[index - near : index - near + 2]:
                for copy in copies:
                    copy.wait()
        some = rows[:, start : start + size]
        gate_part = gate_part + dot_columns(some, gate[:, start : start + size])
        up_part = up_part + dot_columns(some, up[:, start : start + size])
    active = (gate_part / (1.0 + jnp.exp(-gate_part)) * up_part).astype(jnp.bfloat16)
    for index, (start, size) in enumerate(parts):
        if index % 2 == 0:
            for copy in down_copies[index : index + 2]:
                copy.wait()
        total = dot_rows(active, down_vm[:, start : start + size])
        own_out[:, start : start + size] = total[:half].astype(own_out.dtype)
        other_out[:, start : start + size] = total[half:].astype(other_out.dtype)


def feed(own, other, near, gate_weight, up_weight, down_weight):
    chips, local, width = own.shape
    half = chips * local
    units = down_weight.shape[0]
    return pl.pallas_call(
        feed_kernel,
        out_shape=(
            jax.ShapeDtypeStruct((half, width), jnp.float32),
            jax.ShapeDtypeStruct((half, width), jnp.bfloat16),
        ),
        in_specs=[IN_VMEM] * 4 + [IN_HBM] * 3,
        out_specs=(IN_VMEM, IN_VMEM),
        scratch_shapes=[
            pltpu.VMEM((2 * half, width), jnp.bfloat16),
            pltpu.VMEM((units, width), jnp.bfloat16),
            pltpu.VMEM((units, width), jnp.bfloat16),
            pltpu.VMEM((units, width), jnp.bfloat16),
            pltpu.SemaphoreType.DMA((3, len(pieces(width, FEED_STEP)))),
        ],
        compiler_params=pltpu.CompilerParams(vmem_limit_bytes=32 * MIB),
        name="feed",
    )(
        own,
        other,
        *[keep_in_vmem(array) for array in near],
        keep_in_hbm(gate_weight),
        keep_in_hbm(up_weight),
        keep_in_hbm(down_weight),
    )


def halves_first(values, half):
    swapped = jnp.concatenate([values[half:], values[:half]])
    return jnp.where(lax.axis_index("pool") == 0, values, swapped)


def on_device_kernels(
    hidden,
    input_gain,
    query_weight,
    key_weight,
    value_weight,
    query_gain,
    key_gain,
    output_weight,
    post_gain,
    gate_weight,
    up_weight,
    down_weight,
    key_cache,
    value_cache,
    lengths,
    request_slot,
):
    devices = lax.axis_size(("pool", "tensor"))
    chips = lax.axis_size("tensor")
    device_index = lax.axis_index(("pool", "tensor"))
    requests = lengths.shape[0]
    half = requests // 2
    slot_count = SLOTS
    query_cols = query_weight.shape[1]
    head_dim = query_gain.shape[0]
    width = hidden.shape[1]
    index = device_index.astype(jnp.int32).reshape(1)

    def fetch_whole(*arrays):
        return fetch(arrays, 0, max(array.shape[1] for array in arrays))

    units = down_weight.shape[0]
    reach = min(FETCHED // (4 * units) // FEED_STEP * FEED_STEP, width // 2)

    def fetch_first(*arrays):
        return fetch(arrays, 0, reach)

    def plan_here(*arrays):
        return plan(*arrays[:3], head_dim, *arrays[3:], slot_count)

    own, weights = gather_half(
        hidden, chips, fetch_whole, query_weight, key_weight.T, value_weight.T
    )
    other = swap_cores(own)
    slots = halves_first(request_slot, half)
    outgoing = project(own, other, input_gain, slots, weights, devices, slot_count)
    arrived, planned = beside(
        swap_all, outgoing, plan_here, index, lengths, request_slot, key_cache, value_cache
    )
    head_out = attend(
        arrived, planned, query_gain, key_gain, key_cache, value_cache, query_cols
    )
    returned, weights = beside(swap_all, head_out, fetch_whole, output_weight)
    own_sum, other_sum = mix(returned, slots, weights[0], requests)
    attended = scatter_halves(own_sum, other_sum, chips)
    mixed_rows = (hidden.astype(jnp.float32) + attended).astype(jnp.bfloat16)
    post_normed = rms_scale(mixed_rows, post_gain).astype(jnp.bfloat16)
    gate_rows, up_rows = gate_weight.T, up_weight.T
    own, near = gather_half(post_normed, chips, fetch_first, gate_rows, up_rows)
    other = swap_cores(own)
    own_sum, other_sum = feed(own, other, near, gate_rows, up_rows, down_weight)
    lowered = scatter_halves(own_sum, other_sum, chips)
    final_rows = (mixed_rows.astype(jnp.float32) + lowered).astype(jnp.bfloat16)
    return (mixed_rows, final_rows)


def gather_rows(rows, devices):
    copies = jnp.broadcast_to(rows[None], (devices,) + rows.shape)
    arrived = lax.all_to_all(copies, ("pool", "tensor"), split_axis=0, concat_axis=0, tiled=True)
    return arrived.reshape(devices * rows.shape[0], rows.shape[1])


def scatter_sum(partial, devices):
    blocks = partial.astype(jnp.bfloat16).reshape(devices, -1, partial.shape[1])
    arrived = lax.all_to_all(blocks, ("pool", "tensor"), split_axis=0, concat_axis=0, tiled=True)
    return jnp.sum(arrived.astype(jnp.float32), axis=0)


def on_device_general(
    hidden,
    input_gain,
    query_weight,
    key_weight,
    value_weight,
    query_gain,
    key_gain,
    output_weight,
    post_gain,
    gate_weight,
    up_weight,
    down_weight,
    key_cache,
    value_cache,
    lengths,
    request_slot,
):
    devices = lax.axis_size(("pool", "tensor"))
    device_index = lax.axis_index(("pool", "tensor"))
    local_rows = hidden.shape[0]
    query_cols = query_weight.shape[1]
    key_cols = key_weight.shape[1]
    width_sent = query_cols + 2 * key_cols
    head_dim = query_gain.shape[0]
    slot_count = SLOTS
    head_count = devices * query_cols // head_dim
    kv_count = devices * key_cols // head_dim
    group_size = head_count // kv_count
    normed = rms_scale(hidden, input_gain).astype(jnp.bfloat16)
    shard_rows = gather_rows(normed, devices)
    query_part = jnp.dot(shard_rows, query_weight, preferred_element_type=jnp.float32)
    key_part = jnp.dot(shard_rows, key_weight, preferred_element_type=jnp.float32)
    value_part = jnp.dot(shard_rows, value_weight, preferred_element_type=jnp.float32)
    projected = jnp.concatenate([query_part, key_part, value_part], axis=1).astype(jnp.bfloat16)
    outgoing = (
        jnp.zeros((devices * slot_count, width_sent), jnp.bfloat16).at[request_slot].set(projected)
    )
    outgoing = outgoing.reshape(devices, slot_count, width_sent)
    arrived = lax.all_to_all(
        outgoing, ("pool", "tensor"), split_axis=0, concat_axis=2, tiled=True
    ).reshape(slot_count, devices, width_sent)
    query_full = arrived[:, :, :query_cols].reshape(slot_count, head_count, head_dim)
    key_full = arrived[:, :, query_cols : query_cols + key_cols].reshape(
        slot_count, kv_count, head_dim
    )
    value_new = arrived[:, :, query_cols + key_cols :].reshape(slot_count, kv_count, head_dim)
    slot_ids = device_index * slot_count + jnp.arange(slot_count, dtype=jnp.int32)
    matches = request_slot[None, :] == slot_ids[:, None]
    slot_length = jnp.sum(jnp.where(matches, lengths[None, :], 0), axis=1)
    owner_of = request_slot // slot_count
    within = request_slot % slot_count
    earlier = (owner_of[None, :] == device_index) & (
        within[None, :] < jnp.arange(slot_count, dtype=jnp.int32)[:, None]
    )
    slot_offset = jnp.sum(jnp.where(earlier, lengths[None, :], 0), axis=1)
    position = slot_length.astype(jnp.float32)[:, None, None]
    query_heads = rotate(rms_scale(query_full, query_gain), position).astype(jnp.bfloat16)
    query_heads = query_heads.reshape(slot_count, kv_count, group_size, head_dim)
    key_new = rotate(rms_scale(key_full, key_gain), position).astype(jnp.bfloat16)
    pool_tokens = key_cache.shape[0]
    scale_factor = 1.0 / math.sqrt(head_dim)
    scores = jnp.stack(
        [
            jnp.einsum(
                "sgd,td->sgt",
                query_heads[:, kv],
                key_cache[:, kv * head_dim : (kv + 1) * head_dim],
                preferred_element_type=jnp.float32,
            )
            for kv in range(kv_count)
        ],
        axis=1,
    ) * scale_factor
    own_score = (
        jnp.einsum("skgd,skd->skg", query_heads, key_new, preferred_element_type=jnp.float32)
        * scale_factor
    )
    token_pos = jnp.arange(pool_tokens, dtype=jnp.int32)
    inside = (token_pos[None, :] >= slot_offset[:, None]) & (
        token_pos[None, :] < (slot_offset + slot_length)[:, None]
    )
    inside = inside[:, None, None, :]
    largest = jnp.maximum(jnp.max(jnp.where(inside, scores, -1e30), axis=3), own_score)
    weights = jnp.where(inside, jnp.exp(scores - largest[..., None]), 0.0)
    own_weight = jnp.exp(own_score - largest)
    denominator = jnp.sum(weights, axis=3) + own_weight
    weights_low = weights.astype(jnp.bfloat16)
    summed = jnp.stack(
        [
            jnp.einsum(
                "sgt,td->sgd",
                weights_low[:, kv],
                value_cache[:, kv * head_dim : (kv + 1) * head_dim],
                preferred_element_type=jnp.float32,
            )
            for kv in range(kv_count)
        ],
        axis=1,
    )
    own_low = own_weight.astype(jnp.bfloat16).astype(jnp.float32)
    summed = summed + own_low[..., None] * value_new.astype(jnp.float32)[:, :, None, :]
    head_out = (
        (summed / denominator[..., None])
        .astype(jnp.bfloat16)
        .reshape(slot_count, devices, query_cols)
    )
    returned = lax.all_to_all(head_out, ("pool", "tensor"), split_axis=1, concat_axis=0, tiled=True)
    head_rows = returned.reshape(devices * slot_count, query_cols)[request_slot]
    partial_value = jnp.dot(head_rows, output_weight, preferred_element_type=jnp.float32)
    mixed_rows = (hidden.astype(jnp.float32) + scatter_sum(partial_value, devices)).astype(jnp.bfloat16)
    post_normed = gather_rows(rms_scale(mixed_rows, post_gain).astype(jnp.bfloat16), devices)
    gate_part = jnp.dot(post_normed, gate_weight, preferred_element_type=jnp.float32)
    up_part = jnp.dot(post_normed, up_weight, preferred_element_type=jnp.float32)
    activated = (jax.nn.silu(gate_part) * up_part).astype(jnp.bfloat16)
    lowered = scatter_sum(
        jnp.dot(activated, down_weight, preferred_element_type=jnp.float32), devices
    )
    final_rows = (mixed_rows.astype(jnp.float32) + lowered).astype(jnp.bfloat16)
    return (mixed_rows, final_rows)


def on_device(*arrays):
    query_cols, key_cols = arrays[2].shape[1], arrays[3].shape[1]
    head_dim = arrays[5].shape[0]
    devices = lax.axis_size(("pool", "tensor"))
    kv_count = devices * key_cols // head_dim
    whole_heads = query_cols % head_dim == 0 and head_dim % LANES == 0
    shared = kv_count > 0 and devices % kv_count == 0
    pairs = lax.axis_size("pool") == 2 and arrays[14].shape[0] % 16 == 0
    if whole_heads and shared and pairs:
        return on_device_kernels(*arrays)
    return on_device_general(*arrays)


def solution(mesh):
    placed = (
        P(("groups", "pool", "tensor"), None),
        P(),
        P(None, ("pool", "tensor")),
        P(None, ("pool", "tensor")),
        P(None, ("pool", "tensor")),
        P(),
        P(),
        P(("pool", "tensor"), None),
        P(),
        P(None, ("pool", "tensor")),
        P(None, ("pool", "tensor")),
        P(("pool", "tensor"), None),
        P(("groups", "pool", "tensor"), None),
        P(("groups", "pool", "tensor"), None),
        P("groups"),
        P("groups"),
    )
    return jax.shard_map(
        on_device,
        mesh=mesh,
        in_specs=placed,
        out_specs=(P(("groups", "pool", "tensor"), None), P(("groups", "pool", "tensor"), None)),
        check_vma=False,
    )
```

```python
import functools
import math

import jax
import jax.numpy as jnp
from jax import lax
from jax.experimental import pallas as pl
from jax.experimental.pallas import tpu as pltpu
from jax.sharding import PartitionSpec as P

SLOTS = 4
LANES = 128
MIB = 2**20
FETCHED = 3 * MIB
STEP = 512


eps = 1e-06
theta = 1000000.0


def rms_scale(values, scales):
    values = values.astype(jnp.float32)
    return values * lax.rsqrt(jnp.mean(values * values, axis=-1, keepdims=True) + eps) * scales


def rotate(values, position):
    half_width = values.shape[-1] // 2
    frequency = theta ** (-jnp.arange(half_width, dtype=jnp.float32) * 2.0 / values.shape[-1])
    angles = position * frequency
    cosine = jnp.cos(angles)
    sine_part = jnp.sin(angles)
    front_half = values[..., :half_width]
    back_half = values[..., half_width:]
    return jnp.concatenate(
        [front_half * cosine - back_half * sine_part, back_half * cosine + front_half * sine_part],
        axis=-1,
    )


def swap_cores(block):
    return lax.ppermute(block, "pool", [(0, 1), (1, 0)])


def beside(exchange, blocks, work, *arrays):
    blocks, arrays = lax.optimization_barrier((blocks, arrays))
    return lax.optimization_barrier((exchange(blocks), work(*arrays)))


def swap_partners(block, mask):
    chips = lax.axis_size("tensor")
    return lax.ppermute(block, "tensor", [(chip, chip ^ mask) for chip in range(chips)])


def swap_chips(blocks):
    return lax.all_to_all(blocks, "tensor", split_axis=0, concat_axis=0, tiled=True)


def swap_all(blocks):
    return lax.all_to_all(blocks, ("pool", "tensor"), split_axis=0, concat_axis=0, tiled=True)


def gather_half(rows, chips, work, *arrays):
    copies = jnp.broadcast_to(rows[None], (chips,) + rows.shape)
    return beside(swap_chips, copies, work, *arrays)


def scatter_halves(own_half, other_half, chips):
    added = own_half.astype(jnp.float32) + swap_cores(other_half).astype(jnp.float32)
    blocks = added.astype(jnp.bfloat16).reshape(chips, -1, own_half.shape[1])
    return jnp.sum(swap_chips(blocks).astype(jnp.float32), axis=0)


def dot_rows(left, right):
    return lax.dot_general(
        left, right, (((1,), (0,)), ((), ())), preferred_element_type=jnp.float32
    )


def dot_columns(left, right):
    return lax.dot_general(
        left, right, (((1,), (1,)), ((), ())), preferred_element_type=jnp.float32
    )


def pieces(extent, step):
    return [(start, min(step, extent - start)) for start in range(0, extent, step)]


IN_VMEM = pl.BlockSpec(memory_space=pltpu.VMEM)
IN_HBM = pl.BlockSpec(memory_space=pl.ANY)


def keep_in_hbm(array):
    return pltpu.with_memory_space_constraint(array, pltpu.HBM)


def keep_in_vmem(array):
    return pltpu.with_memory_space_constraint(array, pltpu.VMEM)


def fetch_kernel(ranges, *refs):
    count = len(ranges)
    sources, targets, sems = refs[:count], refs[count : 2 * count], refs[2 * count]
    copies = [
        pltpu.make_async_copy(source.at[:, pl.ds(begin, end - begin)], target, sems.at[index])
        for index, (source, target, (begin, end)) in enumerate(zip(sources, targets, ranges))
    ]
    for copy in copies:
        copy.start()
    for copy in copies:
        copy.wait()


def fetch(ranges, *arrays):
    shapes = [(array.shape[0], end - begin) for array, (begin, end) in zip(arrays, ranges)]
    size = sum(2 * rows * columns for rows, columns in shapes)
    return pl.pallas_call(
        functools.partial(fetch_kernel, ranges),
        out_shape=tuple(
            pltpu.VMEM(shape, array.dtype) for array, shape in zip(arrays, shapes)
        ),
        in_specs=[IN_HBM] * len(arrays),
        out_specs=tuple([IN_VMEM] * len(arrays)),
        scratch_shapes=[pltpu.SemaphoreType.DMA((len(arrays),))],
        compiler_params=pltpu.CompilerParams(vmem_limit_bytes=MIB),
        cost_estimate=pl.CostEstimate(flops=0, bytes_accessed=size, transcendentals=0),
        name="fetch",
    )(*[keep_in_hbm(array) for array in arrays])


def split_columns(count, width, shares):
    blocks = [(array, start, size) for array in range(count) for start, size in pieces(width, STEP)]
    result = []
    done = 0
    for index in range(len(shares)):
        upto = len(blocks) * sum(shares[: index + 1]) // sum(shares)
        part = blocks[done:upto]
        done = upto
        spans = []
        for array in range(count):
            mine = [(start, size) for which, start, size in part if which == array]
            if mine:
                spans.append((array, mine[0][0], mine[-1][0] + mine[-1][1]))
        result.append(spans)
    return result


def flat_rows(blocks):
    return jnp.concatenate(
        [blocks[chip].astype(jnp.float32) for chip in range(blocks.shape[0])], axis=0
    )


def one_hot(rows, columns):
    return jnp.where(rows == columns, 1.0, 0.0).astype(jnp.bfloat16)


def slot_matrix(slots, places):
    return one_hot(lax.broadcasted_iota(jnp.int32, (places, slots.shape[1]), 0), slots[...])


def prepare_kernel(
    slot_count, slots, q_hbm, k_hbm, v_hbm, packing, unpacking, q_vm, k_vm, v_vm, sems
):
    copies = [
        pltpu.make_async_copy(source, target, sems.at[index])
        for index, (source, target) in enumerate(
            zip((q_hbm, k_hbm, v_hbm), (q_vm, k_vm, v_vm))
        )
    ]
    for copy in copies:
        copy.start()
    places, requests = packing.shape
    owners = places // slot_count
    core, parity = lax.axis_index("pool"), lax.rem(lax.axis_index("tensor"), 2)
    natural = slot_matrix(slots, places)
    row = lax.broadcasted_iota(jnp.int32, (requests, requests), 0)
    column = lax.broadcasted_iota(jnp.int32, (requests, requests), 1)
    half_first = one_hot(lax.rem(column + core * (requests // 2), requests), row)
    packing[...] = dot_rows(natural, half_first).astype(jnp.bfloat16)
    half, quarter, local = requests // 2, requests // 4, requests // owners
    half_of = lax.rem(row // half + core, 2)
    side_of = lax.rem(row // quarter + parity, 2)
    pair, inner = lax.rem(row, quarter) // local, lax.rem(row, local)
    source = half_of * half + (pair * 2 + side_of) * local + inner
    unpacking[...] = dot_columns(one_hot(source, column), natural).astype(jnp.bfloat16)
    for copy in copies:
        copy.wait()


def prepare(slot_count, devices, slots, *weights):
    requests = slots.shape[0]
    places = devices * slot_count
    size = sum(2 * weight.size for weight in weights)
    return pl.pallas_call(
        functools.partial(prepare_kernel, slot_count),
        out_shape=(
            jax.ShapeDtypeStruct((places, requests), jnp.bfloat16),
            jax.ShapeDtypeStruct((requests, places), jnp.bfloat16),
        )
        + tuple(pltpu.VMEM(weight.shape, weight.dtype) for weight in weights),
        in_specs=[IN_VMEM] + [IN_HBM] * len(weights),
        out_specs=tuple([IN_VMEM] * (2 + len(weights))),
        scratch_shapes=[pltpu.SemaphoreType.DMA((len(weights),))],
        compiler_params=pltpu.CompilerParams(vmem_limit_bytes=MIB),
        cost_estimate=pl.CostEstimate(flops=0, bytes_accessed=size, transcendentals=0),
        name="prepare",
    )(slots.reshape(1, -1), *[keep_in_hbm(weight) for weight in weights])


def project_kernel(slot_count, own, other, gain, packing, q_vm, k_vm, v_vm, out, normed):
    half = own.shape[0] * own.shape[1]
    for index, source in enumerate((own, other)):
        rows = flat_rows(source)
        scale = lax.rsqrt(jnp.mean(rows * rows, axis=-1, keepdims=True) + eps)
        normed[pl.ds(index * half, half), :] = (rows * scale * gain[...]).astype(jnp.bfloat16)
    query_part = dot_rows(normed[...], q_vm[...])
    key_part = dot_columns(normed[...], k_vm[...])
    value_part = dot_columns(normed[...], v_vm[...])
    projected = jnp.concatenate([query_part, key_part, value_part], axis=1).astype(jnp.bfloat16)
    packed = dot_rows(packing[...], projected)
    for owner in range(out.shape[0]):
        out[owner] = packed[owner * slot_count : (owner + 1) * slot_count, :].astype(jnp.bfloat16)


def project(slot_count, own, other, gain, packing, weights):
    depth, query_cols = weights[0].shape
    width = query_cols + weights[1].shape[0] + weights[2].shape[0]
    places, requests = packing.shape
    return pl.pallas_call(
        functools.partial(project_kernel, slot_count),
        out_shape=jax.ShapeDtypeStruct((places // slot_count, slot_count, width), jnp.bfloat16),
        in_specs=[IN_VMEM] * 7,
        out_specs=IN_VMEM,
        scratch_shapes=[pltpu.VMEM((requests, depth), jnp.bfloat16)],
        compiler_params=pltpu.CompilerParams(vmem_limit_bytes=8 * MIB),
        name="project",
    )(
        own,
        other,
        gain.reshape(1, depth),
        packing,
        *[keep_in_vmem(weight) for weight in weights],
    )


def plan_kernel(
    slot_count,
    lengths,
    slots,
    frequency,
    key_hbm,
    value_hbm,
    first,
    last,
    cosine,
    sine,
    key_vm,
    value_vm,
    sems,
):
    copies = [
        pltpu.make_async_copy(key_hbm.at[pl.ds(0, key_vm.shape[0])], key_vm, sems.at[0]),
        pltpu.make_async_copy(value_hbm.at[pl.ds(0, value_vm.shape[0])], value_vm, sems.at[1]),
    ]
    for copy in copies:
        copy.start()
    start = lax.axis_index(("pool", "tensor")) * slot_count
    requests = slots.shape[1]
    place = slots[...] - start
    rows = lax.broadcasted_iota(jnp.int32, (slot_count, requests), 0)
    amounts = lengths[...].astype(jnp.float32)
    length = jnp.sum(jnp.where(place == rows, amounts, 0.0), axis=1, keepdims=True)
    offset = jnp.sum(
        jnp.where((place >= 0) & (place < rows), amounts, 0.0), axis=1, keepdims=True
    )
    angles = length * frequency[...]
    turn = jnp.sin(angles)
    lean = jnp.cos(angles)
    cosine[...] = jnp.concatenate([lean, lean], axis=1)
    sine[...] = jnp.concatenate([-turn, turn], axis=1)
    first[...] = jnp.broadcast_to(offset.astype(jnp.int32), first.shape)
    last[...] = jnp.broadcast_to((offset + length).astype(jnp.int32), last.shape)
    for copy in copies:
        copy.wait()


def plan(slot_count, head_dim, lengths, slots, key_cache, value_cache):
    tokens, width = key_cache.shape
    key_rows = min(tokens, FETCHED // (2 * width) // 256 * 256)
    value_rows = min(tokens, max(256, FETCHED // (2 * width) // 256 * 256 - key_rows))
    frequency = theta ** (-jnp.arange(head_dim // 2, dtype=jnp.float32) * 2.0 / head_dim)
    table = jax.ShapeDtypeStruct((slot_count, head_dim), jnp.float32)
    bound = jax.ShapeDtypeStruct((slot_count, head_dim), jnp.int32)
    return pl.pallas_call(
        functools.partial(plan_kernel, slot_count),
        out_shape=(
            bound,
            bound,
            table,
            table,
            pltpu.VMEM((key_rows, width), jnp.bfloat16),
            pltpu.VMEM((value_rows, width), jnp.bfloat16),
        ),
        in_specs=[IN_VMEM] * 3 + [IN_HBM] * 2,
        out_specs=tuple([IN_VMEM] * 6),
        scratch_shapes=[pltpu.SemaphoreType.DMA((2,))],
        compiler_params=pltpu.CompilerParams(vmem_limit_bytes=MIB),
        cost_estimate=pl.CostEstimate(
            flops=0, bytes_accessed=2 * width * (key_rows + value_rows), transcendentals=0
        ),
        name="plan",
    )(
        lengths.reshape(1, -1),
        slots.reshape(1, -1),
        frequency.reshape(1, -1),
        keep_in_hbm(key_cache),
        keep_in_hbm(value_cache),
    )


def attend_kernel(
    query_cols,
    key_cols,
    arrived,
    first,
    last,
    cosine,
    sine,
    query_gain,
    key_gain,
    key_near,
    value_near,
    key_hbm,
    value_hbm,
    out,
    key_far,
    value_far,
    queries,
    scores,
    sems,
):
    devices, slot_count, _ = arrived.shape
    tokens, width = key_hbm.shape
    head_dim = query_gain.shape[1]
    kv_count = devices * key_cols // head_dim
    sharers = devices // kv_count
    heads_here = query_cols // head_dim
    repeats = sharers * heads_here
    count = repeats * slot_count
    key_rows, value_rows = key_near.shape[0], value_near.shape[0]
    copies = []
    for source, target, start, sem in (
        (key_hbm, key_far, key_rows, 0),
        (value_hbm, value_far, value_rows, 1),
    ):
        if start < tokens:
            copies.append(
                pltpu.make_async_copy(
                    source.at[pl.ds(start, tokens - start)],
                    target.at[pl.ds(0, tokens - start)],
                    sems.at[sem],
                )
            )
    for copy in copies:
        copy.start()
    scale_factor = 1.0 / math.sqrt(head_dim)

    def tile(rows, times):
        return jnp.concatenate([rows] * times, axis=0)

    def prepare(rows, gain, times):
        rows = rows * lax.rsqrt(jnp.mean(rows * rows, axis=-1, keepdims=True) + eps) * gain[...]
        turned = pltpu.roll(rows, head_dim // 2, 1)
        return (rows * tile(cosine[...], times) + turned * tile(sine[...], times)).astype(
            jnp.bfloat16
        )

    blocks = [arrived[device].astype(jnp.float32) for device in range(devices)]
    rows = jnp.concatenate(
        [
            blocks[kv * sharers + place][:, head * head_dim : (head + 1) * head_dim]
            for kv in range(kv_count)
            for head in range(heads_here)
            for place in range(sharers)
        ],
        axis=0,
    )
    query = prepare(rows, query_gain, kv_count * repeats)

    def whole(begin):
        return [
            jnp.concatenate(
                [
                    blocks[kv * sharers + place][:, begin : begin + key_cols]
                    for place in range(sharers)
                ],
                axis=1,
            )
            for kv in range(kv_count)
        ]

    fresh = prepare(jnp.concatenate(whole(query_cols), axis=0), key_gain, kv_count)
    fresh = fresh.astype(jnp.float32)
    key_new = jnp.concatenate(
        [
            tile(fresh[kv * slot_count : (kv + 1) * slot_count, :], repeats)
            for kv in range(kv_count)
        ],
        axis=0,
    )
    value_new = [tile(rows, repeats) for rows in whole(query_cols + key_cols)]
    own_score = (
        jnp.sum(query.astype(jnp.float32) * key_new, axis=-1, keepdims=True) * scale_factor
    )
    queries[...] = jnp.zeros(queries.shape, queries.dtype)
    for kv in range(kv_count):
        queries[kv * count : (kv + 1) * count, kv * head_dim : (kv + 1) * head_dim] = query[
            kv * count : (kv + 1) * count, :
        ]
    start = tile(first[:, :1], kv_count * repeats)
    end = tile(last[:, :1], kv_count * repeats)
    step = 256
    largest = own_score
    for begin in range(0, tokens, step):
        if begin == key_rows:
            copies[0].wait()
        if begin < key_rows:
            keys = key_near[begin : begin + step, :]
        else:
            keys = key_far[begin - key_rows : begin - key_rows + step, :]
        positions = lax.broadcasted_iota(jnp.int32, (kv_count * count, step), 1) + begin
        inside = (positions >= start) & (positions < end)
        part = jnp.where(inside, dot_columns(queries[...], keys) * scale_factor, -1e30)
        scores[:, begin : begin + step] = part
        largest = jnp.maximum(largest, jnp.max(part, axis=1, keepdims=True))
    own_weight = jnp.exp(own_score - largest)
    denominator = own_weight
    summed = jnp.zeros((kv_count * count, width), jnp.float32)
    for begin in range(0, tokens, step):
        if begin == value_rows:
            copies[-1].wait()
        if begin < value_rows:
            values = value_near[begin : begin + step, :]
        else:
            values = value_far[begin - value_rows : begin - value_rows + step, :]
        weights = jnp.exp(scores[:, begin : begin + step] - largest)
        denominator = denominator + jnp.sum(weights, axis=1, keepdims=True)
        summed = summed + dot_rows(weights.astype(jnp.bfloat16), values)
    own_low = own_weight.astype(jnp.bfloat16).astype(jnp.float32)
    for kv in range(kv_count):
        span = slice(kv * count, (kv + 1) * count)
        mine = summed[span, kv * head_dim : (kv + 1) * head_dim]
        mine = (mine + own_low[span, :] * value_new[kv]) / denominator[span, :]
        for head in range(heads_here):
            for place in range(sharers):
                row = (head * sharers + place) * slot_count
                out[kv * sharers + place, :, head * head_dim : (head + 1) * head_dim] = mine[
                    row : row + slot_count, :
                ].astype(jnp.bfloat16)


def attend(arrived, planned, query_gain, key_gain, key_cache, value_cache, query_cols):
    first, last, cosine, sine, key_near, value_near = planned
    devices, slot_count, width = arrived.shape
    key_cols = (width - query_cols) // 2
    head_dim = query_gain.shape[0]
    tokens, cache_width = key_cache.shape
    rows = devices * query_cols // head_dim * slot_count
    return pl.pallas_call(
        functools.partial(attend_kernel, query_cols, key_cols),
        out_shape=jax.ShapeDtypeStruct((devices, slot_count, query_cols), jnp.bfloat16),
        in_specs=[IN_VMEM] * 9 + [IN_HBM] * 2,
        out_specs=IN_VMEM,
        scratch_shapes=[
            pltpu.VMEM((max(16, tokens - key_near.shape[0]), cache_width), jnp.bfloat16),
            pltpu.VMEM((max(16, tokens - value_near.shape[0]), cache_width), jnp.bfloat16),
            pltpu.VMEM((rows, cache_width), jnp.bfloat16),
            pltpu.VMEM((rows, tokens), jnp.float32),
            pltpu.SemaphoreType.DMA((2,)),
        ],
        compiler_params=pltpu.CompilerParams(vmem_limit_bytes=24 * MIB),
        name="attend",
    )(
        arrived,
        first,
        last,
        cosine,
        sine,
        query_gain.reshape(1, head_dim),
        key_gain.reshape(1, head_dim),
        keep_in_vmem(key_near),
        keep_in_vmem(value_near),
        keep_in_hbm(key_cache),
        keep_in_hbm(value_cache),
    )


def mix_kernel(returned, unpacking, weight, hidden, near_out, far_out, other_out):
    owners = returned.shape[0]
    quarter, width = near_out.shape
    local = hidden.shape[0]
    pair = lax.axis_index("tensor") // 2
    by_slot = jnp.concatenate(
        [returned[owner].astype(jnp.float32) for owner in range(owners)], axis=0
    ).astype(jnp.bfloat16)
    rows = dot_rows(unpacking[...], by_slot).astype(jnp.bfloat16)
    for start, size in pieces(width, 1024):
        columns = slice(start, start + size)
        total = dot_rows(rows, weight[:, columns])
        residual = hidden[:, columns].astype(jnp.float32)
        near_out[:, columns] = total[:quarter] + jnp.concatenate(
            [jnp.where(pair == index, residual, 0.0) for index in range(quarter // local)], axis=0
        )
        far_out[:, columns] = total[quarter : 2 * quarter]
        other_out[:, columns] = total[2 * quarter :].astype(other_out.dtype)


def mix(returned, unpacking, output_weight, hidden):
    quarter, width = unpacking.shape[0] // 4, output_weight.shape[1]
    return pl.pallas_call(
        mix_kernel,
        out_shape=(
            jax.ShapeDtypeStruct((quarter, width), jnp.float32),
            jax.ShapeDtypeStruct((quarter, width), jnp.float32),
            jax.ShapeDtypeStruct((2 * quarter, width), jnp.bfloat16),
        ),
        in_specs=[IN_VMEM] * 4,
        out_specs=(IN_VMEM, IN_VMEM, IN_VMEM),
        compiler_params=pltpu.CompilerParams(vmem_limit_bytes=8 * MIB),
        name="mix",
    )(returned, unpacking, keep_in_vmem(output_weight), hidden)


def renew_kernel(own, partner, gain, mixed, normed):
    local = mixed.shape[0]
    total = own[...].astype(jnp.float32) + partner[...].astype(jnp.float32)
    rows = total.astype(jnp.bfloat16).astype(jnp.float32)
    scale = lax.rsqrt(jnp.mean(rows * rows, axis=-1, keepdims=True) + eps)
    normed[...] = (rows * scale * gain[...]).astype(jnp.bfloat16)
    pair = lax.axis_index("tensor") // 2
    here = rows[:local]
    for index in range(1, rows.shape[0] // local):
        here = jnp.where(pair == index, rows[index * local : (index + 1) * local], here)
    mixed[...] = here.astype(jnp.bfloat16)


def renew(own, partner, gain, local):
    return pl.pallas_call(
        renew_kernel,
        out_shape=(
            jax.ShapeDtypeStruct((local, own.shape[1]), jnp.bfloat16),
            jax.ShapeDtypeStruct(own.shape, jnp.bfloat16),
        ),
        in_specs=[IN_VMEM] * 3,
        out_specs=(IN_VMEM, IN_VMEM),
        compiler_params=pltpu.CompilerParams(vmem_limit_bytes=4 * MIB),
        name="renew",
    )(own, partner, gain.reshape(1, -1))


def feed_kernel(spans, local, *refs):
    quarters, weights = refs[:4], refs[4 : 4 + len(spans)]
    own_out, other_out, rows = refs[4 + len(spans) :]
    half, width = own_out.shape
    quarter = half // 2

    def columns(array, start, size):
        for (index, begin, end), ref in zip(spans, weights):
            if index == array and begin <= start and start + size <= end:
                return ref[:, start - begin : start - begin + size]

    for index in range(2):
        rows[index * half : (index + 1) * half, :] = jnp.concatenate(
            [block[...].astype(jnp.float32) for block in quarters[2 * index : 2 * index + 2]],
            axis=0,
        ).astype(jnp.bfloat16)
    gate_part = up_part = 0.0
    for start, size in pieces(width, STEP):
        some = rows[:, start : start + size]
        gate_part = gate_part + dot_columns(some, columns(0, start, size))
        up_part = up_part + dot_columns(some, columns(1, start, size))
    active = (gate_part / (1.0 + jnp.exp(-gate_part)) * up_part).astype(jnp.bfloat16)
    parity = lax.rem(lax.axis_index("tensor"), 2)
    row = lax.broadcasted_iota(jnp.int32, (2 * half, 2 * half), 0)
    place = lax.rem(row, half)
    pair, inner = place // (2 * local), lax.rem(place, local)
    side_of = lax.rem(place // local + parity, 2)
    source = (row // half) * half + side_of * quarter + pair * local + inner
    order = one_hot(source, lax.broadcasted_iota(jnp.int32, (2 * half, 2 * half), 1))
    active = dot_rows(order, active).astype(jnp.bfloat16)
    for start, size in pieces(width, STEP):
        total = dot_rows(active, columns(2, start, size))
        own_out[:, start : start + size] = total[:half]
        other_out[:, start : start + size] = total[half:].astype(other_out.dtype)


def feed(quarters, spans, weights, local):
    quarter, width = quarters[0].shape
    half = 2 * quarter
    return pl.pallas_call(
        functools.partial(feed_kernel, spans, local),
        out_shape=(
            jax.ShapeDtypeStruct((half, width), jnp.float32),
            jax.ShapeDtypeStruct((half, width), jnp.bfloat16),
        ),
        in_specs=[IN_VMEM] * (4 + len(spans)),
        out_specs=(IN_VMEM, IN_VMEM),
        scratch_shapes=[pltpu.VMEM((2 * half, width), jnp.bfloat16)],
        compiler_params=pltpu.CompilerParams(vmem_limit_bytes=4 * MIB),
        name="feed",
    )(*quarters, *[keep_in_vmem(weight) for weight in weights])


def on_device_kernels(
    hidden,
    input_gain,
    query_weight,
    key_weight,
    value_weight,
    query_gain,
    key_gain,
    output_weight,
    post_gain,
    gate_weight,
    up_weight,
    down_weight,
    key_cache,
    value_cache,
    lengths,
    request_slot,
):
    devices = lax.axis_size(("pool", "tensor"))
    chips = lax.axis_size("tensor")
    local, width = hidden.shape
    quarter = lengths.shape[0] // 4
    slot_count = SLOTS
    query_cols = query_weight.shape[1]
    head_dim = query_gain.shape[0]
    own, (packing, unpacking, *weights) = gather_half(
        hidden,
        chips,
        functools.partial(prepare, slot_count, devices),
        request_slot,
        query_weight,
        key_weight.T,
        value_weight.T,
    )
    outgoing = project(slot_count, own, swap_cores(own), input_gain, packing, weights)
    arrived, planned = beside(
        swap_all,
        outgoing,
        functools.partial(plan, slot_count, head_dim),
        lengths,
        request_slot,
        key_cache,
        value_cache,
    )
    head_out = attend(
        arrived, planned, query_gain, key_gain, key_cache, value_cache, query_cols
    )
    returned, weights = beside(
        swap_all, head_out, functools.partial(fetch, [(0, width)]), output_weight
    )
    near_sum, far_sum, other_sum = mix(returned, unpacking, weights[0], hidden)

    layers = (gate_weight.T, up_weight.T, down_weight)
    shares = [2, 8] + [7] * (chips.bit_length() - 3) + [8, 5]
    groups = split_columns(len(layers), width, shares)
    spans, fetched = [], []

    def beside_fetch(exchange, block):
        group = groups[len(fetched)]
        work = functools.partial(fetch, [(begin, end) for _, begin, end in group])
        block, parts = beside(exchange, block, work, *[layers[index] for index, _, _ in group])
        spans.extend(group)
        fetched.append(parts)
        return block

    def plus(left, right):
        return left.astype(jnp.float32) + right.astype(jnp.float32)

    from_core = beside_fetch(swap_cores, other_sum)
    far_sum = plus(far_sum, from_core[quarter:]).astype(jnp.bfloat16)
    from_side = beside_fetch(lambda block: swap_partners(block, 1), far_sum)
    total = plus(plus(near_sum, from_core[:quarter]), from_side).astype(jnp.bfloat16)
    mask = 2
    while 2 * mask < chips:
        partner = beside_fetch(lambda block: swap_partners(block, mask), total)
        total = plus(total, partner).astype(jnp.bfloat16)
        mask *= 2
    partner = beside_fetch(lambda block: swap_partners(block, mask), total)
    mixed_rows, normed = renew(total, partner, post_gain, local)
    across = swap_cores(normed)
    beyond = beside_fetch(lambda block: swap_partners(block, 1), normed)
    quarters = (normed, beyond, across, swap_cores(beyond))
    own_sum, other_sum = feed(
        quarters, spans, [array for parts in fetched for array in parts], local
    )
    lowered = scatter_halves(own_sum, other_sum, chips)
    final_rows = (mixed_rows.astype(jnp.float32) + lowered).astype(jnp.bfloat16)
    return (mixed_rows, final_rows)


def gather_rows(rows, devices):
    copies = jnp.broadcast_to(rows[None], (devices,) + rows.shape)
    arrived = lax.all_to_all(copies, ("pool", "tensor"), split_axis=0, concat_axis=0, tiled=True)
    return arrived.reshape(devices * rows.shape[0], rows.shape[1])


def scatter_sum(partial, devices):
    blocks = partial.astype(jnp.bfloat16).reshape(devices, -1, partial.shape[1])
    arrived = lax.all_to_all(blocks, ("pool", "tensor"), split_axis=0, concat_axis=0, tiled=True)
    return jnp.sum(arrived.astype(jnp.float32), axis=0)


def on_device_general(
    hidden,
    input_gain,
    query_weight,
    key_weight,
    value_weight,
    query_gain,
    key_gain,
    output_weight,
    post_gain,
    gate_weight,
    up_weight,
    down_weight,
    key_cache,
    value_cache,
    lengths,
    request_slot,
):
    devices = lax.axis_size(("pool", "tensor"))
    device_index = lax.axis_index(("pool", "tensor"))
    local_rows = hidden.shape[0]
    query_cols = query_weight.shape[1]
    key_cols = key_weight.shape[1]
    width_sent = query_cols + 2 * key_cols
    head_dim = query_gain.shape[0]
    slot_count = SLOTS
    head_count = devices * query_cols // head_dim
    kv_count = devices * key_cols // head_dim
    group_size = head_count // kv_count
    normed = rms_scale(hidden, input_gain).astype(jnp.bfloat16)
    shard_rows = gather_rows(normed, devices)
    query_part = jnp.dot(shard_rows, query_weight, preferred_element_type=jnp.float32)
    key_part = jnp.dot(shard_rows, key_weight, preferred_element_type=jnp.float32)
    value_part = jnp.dot(shard_rows, value_weight, preferred_element_type=jnp.float32)
    projected = jnp.concatenate([query_part, key_part, value_part], axis=1).astype(jnp.bfloat16)
    outgoing = (
        jnp.zeros((devices * slot_count, width_sent), jnp.bfloat16).at[request_slot].set(projected)
    )
    outgoing = outgoing.reshape(devices, slot_count, width_sent)
    arrived = lax.all_to_all(
        outgoing, ("pool", "tensor"), split_axis=0, concat_axis=2, tiled=True
    ).reshape(slot_count, devices, width_sent)
    query_full = arrived[:, :, :query_cols].reshape(slot_count, head_count, head_dim)
    key_full = arrived[:, :, query_cols : query_cols + key_cols].reshape(
        slot_count, kv_count, head_dim
    )
    value_new = arrived[:, :, query_cols + key_cols :].reshape(slot_count, kv_count, head_dim)
    slot_ids = device_index * slot_count + jnp.arange(slot_count, dtype=jnp.int32)
    matches = request_slot[None, :] == slot_ids[:, None]
    slot_length = jnp.sum(jnp.where(matches, lengths[None, :], 0), axis=1)
    owner_of = request_slot // slot_count
    within = request_slot % slot_count
    earlier = (owner_of[None, :] == device_index) & (
        within[None, :] < jnp.arange(slot_count, dtype=jnp.int32)[:, None]
    )
    slot_offset = jnp.sum(jnp.where(earlier, lengths[None, :], 0), axis=1)
    position = slot_length.astype(jnp.float32)[:, None, None]
    query_heads = rotate(rms_scale(query_full, query_gain), position).astype(jnp.bfloat16)
    query_heads = query_heads.reshape(slot_count, kv_count, group_size, head_dim)
    key_new = rotate(rms_scale(key_full, key_gain), position).astype(jnp.bfloat16)
    pool_tokens = key_cache.shape[0]
    scale_factor = 1.0 / math.sqrt(head_dim)
    scores = jnp.stack(
        [
            jnp.einsum(
                "sgd,td->sgt",
                query_heads[:, kv],
                key_cache[:, kv * head_dim : (kv + 1) * head_dim],
                preferred_element_type=jnp.float32,
            )
            for kv in range(kv_count)
        ],
        axis=1,
    ) * scale_factor
    own_score = (
        jnp.einsum("skgd,skd->skg", query_heads, key_new, preferred_element_type=jnp.float32)
        * scale_factor
    )
    token_pos = jnp.arange(pool_tokens, dtype=jnp.int32)
    inside = (token_pos[None, :] >= slot_offset[:, None]) & (
        token_pos[None, :] < (slot_offset + slot_length)[:, None]
    )
    inside = inside[:, None, None, :]
    largest = jnp.maximum(jnp.max(jnp.where(inside, scores, -1e30), axis=3), own_score)
    weights = jnp.where(inside, jnp.exp(scores - largest[..., None]), 0.0)
    own_weight = jnp.exp(own_score - largest)
    denominator = jnp.sum(weights, axis=3) + own_weight
    weights_low = weights.astype(jnp.bfloat16)
    summed = jnp.stack(
        [
            jnp.einsum(
                "sgt,td->sgd",
                weights_low[:, kv],
                value_cache[:, kv * head_dim : (kv + 1) * head_dim],
                preferred_element_type=jnp.float32,
            )
            for kv in range(kv_count)
        ],
        axis=1,
    )
    own_low = own_weight.astype(jnp.bfloat16).astype(jnp.float32)
    summed = summed + own_low[..., None] * value_new.astype(jnp.float32)[:, :, None, :]
    head_out = (
        (summed / denominator[..., None])
        .astype(jnp.bfloat16)
        .reshape(slot_count, devices, query_cols)
    )
    returned = lax.all_to_all(head_out, ("pool", "tensor"), split_axis=1, concat_axis=0, tiled=True)
    head_rows = returned.reshape(devices * slot_count, query_cols)[request_slot]
    partial_value = jnp.dot(head_rows, output_weight, preferred_element_type=jnp.float32)
    mixed_rows = (hidden.astype(jnp.float32) + scatter_sum(partial_value, devices)).astype(jnp.bfloat16)
    post_normed = gather_rows(rms_scale(mixed_rows, post_gain).astype(jnp.bfloat16), devices)
    gate_part = jnp.dot(post_normed, gate_weight, preferred_element_type=jnp.float32)
    up_part = jnp.dot(post_normed, up_weight, preferred_element_type=jnp.float32)
    activated = (jax.nn.silu(gate_part) * up_part).astype(jnp.bfloat16)
    lowered = scatter_sum(
        jnp.dot(activated, down_weight, preferred_element_type=jnp.float32), devices
    )
    final_rows = (mixed_rows.astype(jnp.float32) + lowered).astype(jnp.bfloat16)
    return (mixed_rows, final_rows)


def on_device(*arrays):
    query_cols, key_cols = arrays[2].shape[1], arrays[3].shape[1]
    head_dim = arrays[5].shape[0]
    devices = lax.axis_size(("pool", "tensor"))
    kv_count = devices * key_cols // head_dim
    whole_heads = query_cols % head_dim == 0 and head_dim % LANES == 0
    shared = kv_count > 0 and devices % kv_count == 0
    chips = lax.axis_size("tensor")
    pairs = lax.axis_size("pool") == 2 and chips >= 4 and chips & (chips - 1) == 0
    pairs = pairs and arrays[14].shape[0] % 32 == 0
    if whole_heads and shared and pairs:
        return on_device_kernels(*arrays)
    return on_device_general(*arrays)


def solution(mesh):
    placed = (
        P(("groups", "pool", "tensor"), None),
        P(),
        P(None, ("pool", "tensor")),
        P(None, ("pool", "tensor")),
        P(None, ("pool", "tensor")),
        P(),
        P(),
        P(("pool", "tensor"), None),
        P(),
        P(None, ("pool", "tensor")),
        P(None, ("pool", "tensor")),
        P(("pool", "tensor"), None),
        P(("groups", "pool", "tensor"), None),
        P(("groups", "pool", "tensor"), None),
        P("groups"),
        P("groups"),
    )
    return jax.shard_map(
        on_device,
        mesh=mesh,
        in_specs=placed,
        out_specs=(P(("groups", "pool", "tensor"), None), P(("groups", "pool", "tensor"), None)),
        check_vma=False,
    )
```

```python
import functools
import math

import jax
import jax.numpy as jnp
from jax import lax
from jax.experimental import pallas as pl
from jax.experimental.pallas import tpu as pltpu
from jax.sharding import PartitionSpec as P

SLOTS = 4
LANES = 128
MIB = 2**20
FETCHED = 3 * MIB
STEP = 512


eps = 1e-06
theta = 1000000.0


def rms_scale(values, scales):
    values = values.astype(jnp.float32)
    return values * lax.rsqrt(jnp.mean(values * values, axis=-1, keepdims=True) + eps) * scales


def rotate(values, position):
    half_width = values.shape[-1] // 2
    frequency = theta ** (-jnp.arange(half_width, dtype=jnp.float32) * 2.0 / values.shape[-1])
    angles = position * frequency
    cosine = jnp.cos(angles)
    sine_part = jnp.sin(angles)
    front_half = values[..., :half_width]
    back_half = values[..., half_width:]
    return jnp.concatenate(
        [front_half * cosine - back_half * sine_part, back_half * cosine + front_half * sine_part],
        axis=-1,
    )


def swap_cores(block):
    return lax.ppermute(block, "pool", [(0, 1), (1, 0)])


def beside(exchange, blocks, work, *arrays):
    blocks, arrays = lax.optimization_barrier((blocks, arrays))
    return lax.optimization_barrier((exchange(blocks), work(*arrays)))


def swap_partners(block, mask):
    chips = lax.axis_size("tensor")
    return lax.ppermute(block, "tensor", [(chip, chip ^ mask) for chip in range(chips)])


def swap_chips(blocks):
    return lax.all_to_all(blocks, "tensor", split_axis=0, concat_axis=0, tiled=True)


def swap_all(blocks):
    return lax.all_to_all(blocks, ("pool", "tensor"), split_axis=0, concat_axis=0, tiled=True)


def gather_half(rows, chips, work, *arrays):
    copies = jnp.broadcast_to(rows[None], (chips,) + rows.shape)
    return beside(swap_chips, copies, work, *arrays)


def scatter_halves(own_half, other_half, chips):
    added = own_half.astype(jnp.float32) + swap_cores(other_half).astype(jnp.float32)
    blocks = added.astype(jnp.bfloat16).reshape(chips, -1, own_half.shape[1])
    return jnp.sum(swap_chips(blocks).astype(jnp.float32), axis=0)


def dot_rows(left, right):
    return lax.dot_general(
        left, right, (((1,), (0,)), ((), ())), preferred_element_type=jnp.float32
    )


def dot_columns(left, right):
    return lax.dot_general(
        left, right, (((1,), (1,)), ((), ())), preferred_element_type=jnp.float32
    )


def pieces(extent, step):
    return [(start, min(step, extent - start)) for start in range(0, extent, step)]


IN_VMEM = pl.BlockSpec(memory_space=pltpu.VMEM)
IN_HBM = pl.BlockSpec(memory_space=pl.ANY)


def keep_in_hbm(array):
    return pltpu.with_memory_space_constraint(array, pltpu.HBM)


def keep_in_vmem(array):
    return pltpu.with_memory_space_constraint(array, pltpu.VMEM)


def fetch_kernel(ranges, turned, *refs):
    count = len(ranges)
    sources, targets, stages = refs[:count], refs[count : 2 * count], list(refs[2 * count : -1])
    sems = refs[-1]
    copies, turns = [], []
    for index, (begin, end) in enumerate(ranges):
        if turned[index]:
            stage = stages.pop(0)
            for start, size in pieces(end - begin, STEP):
                turns.append((len(copies), stage, targets[index], start, size))
                copies.append(
                    pltpu.make_async_copy(
                        sources[index].at[:, pl.ds(begin + start, size)],
                        stage.at[:, pl.ds(start, size)],
                        sems.at[len(copies)],
                    )
                )
        else:
            copies.append(
                pltpu.make_async_copy(
                    sources[index].at[:, pl.ds(begin, end - begin)],
                    targets[index],
                    sems.at[len(copies)],
                )
            )
    for copy in copies:
        copy.start()
    for index, stage, target, start, size in turns:
        copies[index].wait()
        target[start : start + size, :] = stage[:, start : start + size].T
    turning = [index for index, *_ in turns]
    for index, copy in enumerate(copies):
        if index not in turning:
            copy.wait()


def fetch(ranges, turned, *arrays):
    shapes = [(array.shape[0], end - begin) for array, (begin, end) in zip(arrays, ranges)]
    size = sum(2 * rows * columns for rows, columns in shapes)
    stages = [pltpu.VMEM(shape, jnp.bfloat16) for shape, turn in zip(shapes, turned) if turn]
    count = sum(
        len(pieces(columns, STEP)) if turn else 1 for (_, columns), turn in zip(shapes, turned)
    )
    staged = sum(2 * rows * columns for (rows, columns), turn in zip(shapes, turned) if turn)
    return pl.pallas_call(
        functools.partial(fetch_kernel, ranges, turned),
        out_shape=tuple(
            pltpu.VMEM(shape[::-1] if turn else shape, array.dtype)
            for array, shape, turn in zip(arrays, shapes, turned)
        ),
        in_specs=[IN_HBM] * len(arrays),
        out_specs=tuple([IN_VMEM] * len(arrays)),
        scratch_shapes=stages + [pltpu.SemaphoreType.DMA((count,))],
        compiler_params=pltpu.CompilerParams(vmem_limit_bytes=2 * MIB + staged),
        cost_estimate=pl.CostEstimate(flops=0, bytes_accessed=size, transcendentals=0),
        name="fetch",
    )(*[keep_in_hbm(array) for array in arrays])


def split_columns(arrays, width, shares):
    blocks = [(array, start, size) for array in arrays for start, size in pieces(width, STEP)]
    result = []
    done = 0
    for index in range(len(shares)):
        upto = len(blocks) * sum(shares[: index + 1]) // sum(shares)
        part = blocks[done:upto]
        done = upto
        spans = []
        for array in arrays:
            mine = [(start, size) for which, start, size in part if which == array]
            if mine:
                spans.append((array, mine[0][0], mine[-1][0] + mine[-1][1]))
        result.append(spans)
    return result


def flat_rows(blocks):
    return jnp.concatenate(
        [blocks[chip].astype(jnp.float32) for chip in range(blocks.shape[0])], axis=0
    )


def one_hot(rows, columns):
    return jnp.where(rows == columns, 1.0, 0.0).astype(jnp.bfloat16)


def slot_matrix(slots, places):
    return one_hot(lax.broadcasted_iota(jnp.int32, (places, slots.shape[1]), 0), slots[...])


def prepare_kernel(
    slot_count, slots, q_hbm, k_hbm, v_hbm, packing, unpacking, q_vm, k_vm, v_vm, sems
):
    copies = [
        pltpu.make_async_copy(source, target, sems.at[index])
        for index, (source, target) in enumerate(
            zip((q_hbm, k_hbm, v_hbm), (q_vm, k_vm, v_vm))
        )
    ]
    for copy in copies:
        copy.start()
    places, requests = packing.shape
    owners = places // slot_count
    core, parity = lax.axis_index("pool"), lax.rem(lax.axis_index("tensor"), 2)
    natural = slot_matrix(slots, places)
    row = lax.broadcasted_iota(jnp.int32, (requests, requests), 0)
    column = lax.broadcasted_iota(jnp.int32, (requests, requests), 1)
    half_first = one_hot(lax.rem(column + core * (requests // 2), requests), row)
    packing[...] = dot_rows(natural, half_first).astype(jnp.bfloat16)
    half, quarter, local = requests // 2, requests // 4, requests // owners
    half_of = lax.rem(row // half + core, 2)
    side_of = lax.rem(row // quarter + parity, 2)
    pair, inner = lax.rem(row, quarter) // local, lax.rem(row, local)
    source = half_of * half + (pair * 2 + side_of) * local + inner
    unpacking[...] = dot_columns(one_hot(source, column), natural).astype(jnp.bfloat16)
    for copy in copies:
        copy.wait()


def prepare(slot_count, devices, slots, *weights):
    requests = slots.shape[0]
    places = devices * slot_count
    size = sum(2 * weight.size for weight in weights)
    return pl.pallas_call(
        functools.partial(prepare_kernel, slot_count),
        out_shape=(
            jax.ShapeDtypeStruct((places, requests), jnp.bfloat16),
            jax.ShapeDtypeStruct((requests, places), jnp.bfloat16),
        )
        + tuple(pltpu.VMEM(weight.shape, weight.dtype) for weight in weights),
        in_specs=[IN_VMEM] + [IN_HBM] * len(weights),
        out_specs=tuple([IN_VMEM] * (2 + len(weights))),
        scratch_shapes=[pltpu.SemaphoreType.DMA((len(weights),))],
        compiler_params=pltpu.CompilerParams(vmem_limit_bytes=MIB),
        cost_estimate=pl.CostEstimate(flops=0, bytes_accessed=size, transcendentals=0),
        name="prepare",
    )(slots.reshape(1, -1), *[keep_in_hbm(weight) for weight in weights])


def project_kernel(slot_count, own, other, gain, packing, q_vm, k_vm, v_vm, out, normed):
    half = own.shape[0] * own.shape[1]
    for index, source in enumerate((own, other)):
        rows = flat_rows(source)
        scale = lax.rsqrt(jnp.mean(rows * rows, axis=-1, keepdims=True) + eps)
        normed[pl.ds(index * half, half), :] = (rows * scale * gain[...]).astype(jnp.bfloat16)
    query_part = dot_rows(normed[...], q_vm[...])
    key_part = dot_columns(normed[...], k_vm[...])
    value_part = dot_columns(normed[...], v_vm[...])
    projected = jnp.concatenate([query_part, key_part, value_part], axis=1).astype(jnp.bfloat16)
    packed = dot_rows(packing[...], projected)
    for owner in range(out.shape[0]):
        out[owner] = packed[owner * slot_count : (owner + 1) * slot_count, :].astype(jnp.bfloat16)


def project(slot_count, own, other, gain, packing, weights):
    depth, query_cols = weights[0].shape
    width = query_cols + weights[1].shape[0] + weights[2].shape[0]
    places, requests = packing.shape
    return pl.pallas_call(
        functools.partial(project_kernel, slot_count),
        out_shape=jax.ShapeDtypeStruct((places // slot_count, slot_count, width), jnp.bfloat16),
        in_specs=[IN_VMEM] * 7,
        out_specs=IN_VMEM,
        scratch_shapes=[pltpu.VMEM((requests, depth), jnp.bfloat16)],
        compiler_params=pltpu.CompilerParams(vmem_limit_bytes=8 * MIB),
        name="project",
    )(
        own,
        other,
        gain.reshape(1, depth),
        packing,
        *[keep_in_vmem(weight) for weight in weights],
    )


def plan_kernel(
    slot_count,
    lengths,
    slots,
    frequency,
    key_hbm,
    value_hbm,
    first,
    last,
    cosine,
    sine,
    key_vm,
    value_vm,
    sems,
):
    copies = [
        pltpu.make_async_copy(key_hbm.at[pl.ds(0, key_vm.shape[0])], key_vm, sems.at[0]),
        pltpu.make_async_copy(value_hbm.at[pl.ds(0, value_vm.shape[0])], value_vm, sems.at[1]),
    ]
    for copy in copies:
        copy.start()
    start = lax.axis_index(("pool", "tensor")) * slot_count
    requests = slots.shape[1]
    place = slots[...] - start
    rows = lax.broadcasted_iota(jnp.int32, (slot_count, requests), 0)
    amounts = lengths[...].astype(jnp.float32)
    length = jnp.sum(jnp.where(place == rows, amounts, 0.0), axis=1, keepdims=True)
    offset = jnp.sum(
        jnp.where((place >= 0) & (place < rows), amounts, 0.0), axis=1, keepdims=True
    )
    angles = length * frequency[...]
    turn = jnp.sin(angles)
    lean = jnp.cos(angles)
    cosine[...] = jnp.concatenate([lean, lean], axis=1)
    sine[...] = jnp.concatenate([-turn, turn], axis=1)
    first[...] = jnp.broadcast_to(offset.astype(jnp.int32), first.shape)
    last[...] = jnp.broadcast_to((offset + length).astype(jnp.int32), last.shape)
    for copy in copies:
        copy.wait()


def plan(slot_count, head_dim, lengths, slots, key_cache, value_cache):
    tokens, width = key_cache.shape
    key_rows = min(tokens, FETCHED // (2 * width) // 256 * 256)
    value_rows = min(tokens, max(256, FETCHED // (2 * width) // 256 * 256 - key_rows))
    frequency = theta ** (-jnp.arange(head_dim // 2, dtype=jnp.float32) * 2.0 / head_dim)
    table = jax.ShapeDtypeStruct((slot_count, head_dim), jnp.float32)
    bound = jax.ShapeDtypeStruct((slot_count, head_dim), jnp.int32)
    return pl.pallas_call(
        functools.partial(plan_kernel, slot_count),
        out_shape=(
            bound,
            bound,
            table,
            table,
            pltpu.VMEM((key_rows, width), jnp.bfloat16),
            pltpu.VMEM((value_rows, width), jnp.bfloat16),
        ),
        in_specs=[IN_VMEM] * 3 + [IN_HBM] * 2,
        out_specs=tuple([IN_VMEM] * 6),
        scratch_shapes=[pltpu.SemaphoreType.DMA((2,))],
        compiler_params=pltpu.CompilerParams(vmem_limit_bytes=MIB),
        cost_estimate=pl.CostEstimate(
            flops=0, bytes_accessed=2 * width * (key_rows + value_rows), transcendentals=0
        ),
        name="plan",
    )(
        lengths.reshape(1, -1),
        slots.reshape(1, -1),
        frequency.reshape(1, -1),
        keep_in_hbm(key_cache),
        keep_in_hbm(value_cache),
    )


def attend_kernel(
    query_cols,
    key_cols,
    arrived,
    first,
    last,
    cosine,
    sine,
    query_gain,
    key_gain,
    key_near,
    value_near,
    key_hbm,
    value_hbm,
    out,
    key_far,
    value_far,
    queries,
    scores,
    sems,
):
    devices, slot_count, _ = arrived.shape
    tokens, width = key_hbm.shape
    head_dim = query_gain.shape[1]
    kv_count = devices * key_cols // head_dim
    sharers = devices // kv_count
    heads_here = query_cols // head_dim
    repeats = sharers * heads_here
    count = repeats * slot_count
    key_rows, value_rows = key_near.shape[0], value_near.shape[0]
    copies = []
    for source, target, start, sem in (
        (key_hbm, key_far, key_rows, 0),
        (value_hbm, value_far, value_rows, 1),
    ):
        if start < tokens:
            copies.append(
                pltpu.make_async_copy(
                    source.at[pl.ds(start, tokens - start)],
                    target.at[pl.ds(0, tokens - start)],
                    sems.at[sem],
                )
            )
    for copy in copies:
        copy.start()
    scale_factor = 1.0 / math.sqrt(head_dim)

    def tile(rows, times):
        return jnp.concatenate([rows] * times, axis=0)

    def prepare(rows, gain, times):
        rows = rows * lax.rsqrt(jnp.mean(rows * rows, axis=-1, keepdims=True) + eps) * gain[...]
        turned = pltpu.roll(rows, head_dim // 2, 1)
        return (rows * tile(cosine[...], times) + turned * tile(sine[...], times)).astype(
            jnp.bfloat16
        )

    blocks = [arrived[device].astype(jnp.float32) for device in range(devices)]
    rows = jnp.concatenate(
        [
            blocks[kv * sharers + place][:, head * head_dim : (head + 1) * head_dim]
            for kv in range(kv_count)
            for head in range(heads_here)
            for place in range(sharers)
        ],
        axis=0,
    )
    query = prepare(rows, query_gain, kv_count * repeats)

    def whole(begin):
        return [
            jnp.concatenate(
                [
                    blocks[kv * sharers + place][:, begin : begin + key_cols]
                    for place in range(sharers)
                ],
                axis=1,
            )
            for kv in range(kv_count)
        ]

    fresh = prepare(jnp.concatenate(whole(query_cols), axis=0), key_gain, kv_count)
    fresh = fresh.astype(jnp.float32)
    key_new = jnp.concatenate(
        [
            tile(fresh[kv * slot_count : (kv + 1) * slot_count, :], repeats)
            for kv in range(kv_count)
        ],
        axis=0,
    )
    value_new = [tile(rows, repeats) for rows in whole(query_cols + key_cols)]
    own_score = (
        jnp.sum(query.astype(jnp.float32) * key_new, axis=-1, keepdims=True) * scale_factor
    )
    queries[...] = jnp.zeros(queries.shape, queries.dtype)
    for kv in range(kv_count):
        queries[kv * count : (kv + 1) * count, kv * head_dim : (kv + 1) * head_dim] = query[
            kv * count : (kv + 1) * count, :
        ]
    start = tile(first[:, :1], kv_count * repeats)
    end = tile(last[:, :1], kv_count * repeats)
    step = 256
    largest = own_score
    for begin in range(0, tokens, step):
        if begin == key_rows:
            copies[0].wait()
        if begin < key_rows:
            keys = key_near[begin : begin + step, :]
        else:
            keys = key_far[begin - key_rows : begin - key_rows + step, :]
        positions = lax.broadcasted_iota(jnp.int32, (kv_count * count, step), 1) + begin
        inside = (positions >= start) & (positions < end)
        part = jnp.where(inside, dot_columns(queries[...], keys) * scale_factor, -1e30)
        scores[:, begin : begin + step] = part
        largest = jnp.maximum(largest, jnp.max(part, axis=1, keepdims=True))
    own_weight = jnp.exp(own_score - largest)
    denominator = own_weight
    summed = jnp.zeros((kv_count * count, width), jnp.float32)
    for begin in range(0, tokens, step):
        if begin == value_rows:
            copies[-1].wait()
        if begin < value_rows:
            values = value_near[begin : begin + step, :]
        else:
            values = value_far[begin - value_rows : begin - value_rows + step, :]
        weights = jnp.exp(scores[:, begin : begin + step] - largest)
        denominator = denominator + jnp.sum(weights, axis=1, keepdims=True)
        summed = summed + dot_rows(weights.astype(jnp.bfloat16), values)
    own_low = own_weight.astype(jnp.bfloat16).astype(jnp.float32)
    for kv in range(kv_count):
        span = slice(kv * count, (kv + 1) * count)
        mine = summed[span, kv * head_dim : (kv + 1) * head_dim]
        mine = (mine + own_low[span, :] * value_new[kv]) / denominator[span, :]
        for head in range(heads_here):
            for place in range(sharers):
                row = (head * sharers + place) * slot_count
                out[kv * sharers + place, :, head * head_dim : (head + 1) * head_dim] = mine[
                    row : row + slot_count, :
                ].astype(jnp.bfloat16)


def attend(arrived, planned, query_gain, key_gain, key_cache, value_cache, query_cols):
    first, last, cosine, sine, key_near, value_near = planned
    devices, slot_count, width = arrived.shape
    key_cols = (width - query_cols) // 2
    head_dim = query_gain.shape[0]
    tokens, cache_width = key_cache.shape
    rows = devices * query_cols // head_dim * slot_count
    return pl.pallas_call(
        functools.partial(attend_kernel, query_cols, key_cols),
        out_shape=jax.ShapeDtypeStruct((devices, slot_count, query_cols), jnp.bfloat16),
        in_specs=[IN_VMEM] * 9 + [IN_HBM] * 2,
        out_specs=IN_VMEM,
        scratch_shapes=[
            pltpu.VMEM((max(16, tokens - key_near.shape[0]), cache_width), jnp.bfloat16),
            pltpu.VMEM((max(16, tokens - value_near.shape[0]), cache_width), jnp.bfloat16),
            pltpu.VMEM((rows, cache_width), jnp.bfloat16),
            pltpu.VMEM((rows, tokens), jnp.float32),
            pltpu.SemaphoreType.DMA((2,)),
        ],
        compiler_params=pltpu.CompilerParams(vmem_limit_bytes=24 * MIB),
        name="attend",
    )(
        arrived,
        first,
        last,
        cosine,
        sine,
        query_gain.reshape(1, head_dim),
        key_gain.reshape(1, head_dim),
        keep_in_vmem(key_near),
        keep_in_vmem(value_near),
        keep_in_hbm(key_cache),
        keep_in_hbm(value_cache),
    )


def mix_kernel(returned, unpacking, weight, hidden, near_out, far_out, other_out):
    owners = returned.shape[0]
    quarter, width = near_out.shape
    local = hidden.shape[0]
    pair = lax.axis_index("tensor") // 2
    by_slot = jnp.concatenate(
        [returned[owner].astype(jnp.float32) for owner in range(owners)], axis=0
    ).astype(jnp.bfloat16)
    rows = dot_rows(unpacking[...], by_slot).astype(jnp.bfloat16)
    for start, size in pieces(width, 1024):
        columns = slice(start, start + size)
        total = dot_rows(rows, weight[:, columns])
        residual = hidden[:, columns].astype(jnp.float32)
        near_out[:, columns] = total[:quarter] + jnp.concatenate(
            [jnp.where(pair == index, residual, 0.0) for index in range(quarter // local)], axis=0
        )
        far_out[:, columns] = total[quarter : 2 * quarter]
        other_out[:, columns] = total[2 * quarter :].astype(other_out.dtype)


def mix(returned, unpacking, output_weight, hidden):
    quarter, width = unpacking.shape[0] // 4, output_weight.shape[1]
    return pl.pallas_call(
        mix_kernel,
        out_shape=(
            jax.ShapeDtypeStruct((quarter, width), jnp.float32),
            jax.ShapeDtypeStruct((quarter, width), jnp.float32),
            jax.ShapeDtypeStruct((2 * quarter, width), jnp.bfloat16),
        ),
        in_specs=[IN_VMEM] * 4,
        out_specs=(IN_VMEM, IN_VMEM, IN_VMEM),
        compiler_params=pltpu.CompilerParams(vmem_limit_bytes=8 * MIB),
        name="mix",
    )(returned, unpacking, keep_in_vmem(output_weight), hidden)


def renew_kernel(own, partner, gain, mixed, normed):
    local = mixed.shape[0]
    total = own[...].astype(jnp.float32) + partner[...].astype(jnp.float32)
    rows = total.astype(jnp.bfloat16).astype(jnp.float32)
    scale = lax.rsqrt(jnp.mean(rows * rows, axis=-1, keepdims=True) + eps)
    normed[...] = (rows * scale * gain[...]).astype(jnp.bfloat16)
    pair = lax.axis_index("tensor") // 2
    here = rows[:local]
    for index in range(1, rows.shape[0] // local):
        here = jnp.where(pair == index, rows[index * local : (index + 1) * local], here)
    mixed[...] = here.astype(jnp.bfloat16)


def renew(own, partner, gain, local):
    return pl.pallas_call(
        renew_kernel,
        out_shape=(
            jax.ShapeDtypeStruct((local, own.shape[1]), jnp.bfloat16),
            jax.ShapeDtypeStruct(own.shape, jnp.bfloat16),
        ),
        in_specs=[IN_VMEM] * 3,
        out_specs=(IN_VMEM, IN_VMEM),
        compiler_params=pltpu.CompilerParams(vmem_limit_bytes=4 * MIB),
        name="renew",
    )(own, partner, gain.reshape(1, -1))


def feed_kernel(spans, local, *refs):
    quarters, weights = refs[:4], refs[4 : 4 + len(spans)]
    own_out, other_out, rows = refs[4 + len(spans) :]
    half, width = own_out.shape
    quarter = half // 2

    def part(array, start, size):
        for (index, begin, end), ref in zip(spans, weights):
            if index == array and begin <= start and start + size <= end:
                span = slice(start - begin, start - begin + size)
                return ref[:, span] if index == 2 else ref[span, :]

    for index in range(2):
        rows[index * half : (index + 1) * half, :] = jnp.concatenate(
            [block[...].astype(jnp.float32) for block in quarters[2 * index : 2 * index + 2]],
            axis=0,
        ).astype(jnp.bfloat16)
    gate_part = up_part = 0.0
    for start, size in pieces(width, STEP):
        some = rows[:, start : start + size]
        gate_part = gate_part + dot_rows(some, part(0, start, size))
        up_part = up_part + dot_rows(some, part(1, start, size))
    active = (gate_part / (1.0 + jnp.exp(-gate_part)) * up_part).astype(jnp.bfloat16)
    parity = lax.rem(lax.axis_index("tensor"), 2)
    row = lax.broadcasted_iota(jnp.int32, (2 * half, 2 * half), 0)
    place = lax.rem(row, half)
    pair, inner = place // (2 * local), lax.rem(place, local)
    side_of = lax.rem(place // local + parity, 2)
    source = (row // half) * half + side_of * quarter + pair * local + inner
    order = one_hot(source, lax.broadcasted_iota(jnp.int32, (2 * half, 2 * half), 1))
    active = dot_rows(order, active).astype(jnp.bfloat16)
    for start, size in pieces(width, STEP):
        total = dot_rows(active, part(2, start, size))
        own_out[:, start : start + size] = total[:half]
        other_out[:, start : start + size] = total[half:].astype(other_out.dtype)


def feed(quarters, spans, weights, local):
    quarter, width = quarters[0].shape
    half = 2 * quarter
    return pl.pallas_call(
        functools.partial(feed_kernel, spans, local),
        out_shape=(
            jax.ShapeDtypeStruct((half, width), jnp.float32),
            jax.ShapeDtypeStruct((half, width), jnp.bfloat16),
        ),
        in_specs=[IN_VMEM] * (4 + len(spans)),
        out_specs=(IN_VMEM, IN_VMEM),
        scratch_shapes=[pltpu.VMEM((2 * half, width), jnp.bfloat16)],
        compiler_params=pltpu.CompilerParams(vmem_limit_bytes=4 * MIB),
        name="feed",
    )(*quarters, *[keep_in_vmem(weight) for weight in weights])


def on_device_kernels(
    hidden,
    input_gain,
    query_weight,
    key_weight,
    value_weight,
    query_gain,
    key_gain,
    output_weight,
    post_gain,
    gate_weight,
    up_weight,
    down_weight,
    key_cache,
    value_cache,
    lengths,
    request_slot,
):
    devices = lax.axis_size(("pool", "tensor"))
    chips = lax.axis_size("tensor")
    local, width = hidden.shape
    quarter = lengths.shape[0] // 4
    slot_count = SLOTS
    query_cols = query_weight.shape[1]
    head_dim = query_gain.shape[0]
    own, (packing, unpacking, *weights) = gather_half(
        hidden,
        chips,
        functools.partial(prepare, slot_count, devices),
        request_slot,
        query_weight,
        key_weight.T,
        value_weight.T,
    )
    outgoing = project(slot_count, own, swap_cores(own), input_gain, packing, weights)
    arrived, planned = beside(
        swap_all,
        outgoing,
        functools.partial(plan, slot_count, head_dim),
        lengths,
        request_slot,
        key_cache,
        value_cache,
    )
    head_out = attend(
        arrived, planned, query_gain, key_gain, key_cache, value_cache, query_cols
    )
    returned, weights = beside(
        swap_all, head_out, functools.partial(fetch, [(0, width)], [False]), output_weight
    )
    near_sum, far_sum, other_sum = mix(returned, unpacking, weights[0], hidden)

    layers = (gate_weight.T, up_weight.T, down_weight)
    steps = chips.bit_length()
    turned = split_columns([0, 1], width, [5] * (steps - 2) + [6, 4, 0])
    straight = split_columns([2], width, [2] * (steps - 1) + [3, 1])
    groups = [first + second for first, second in zip(turned, straight)]
    spans, fetched = [], []

    def beside_fetch(exchange, block):
        group = groups[len(fetched)]
        work = functools.partial(
            fetch,
            [(begin, end) for _, begin, end in group],
            [index < 2 for index, _, _ in group],
        )
        block, parts = beside(exchange, block, work, *[layers[index] for index, _, _ in group])
        spans.extend(group)
        fetched.append(parts)
        return block

    def plus(left, right):
        return left.astype(jnp.float32) + right.astype(jnp.float32)

    from_core = swap_cores(other_sum)
    far_sum = plus(far_sum, from_core[quarter:]).astype(jnp.bfloat16)
    from_side = beside_fetch(lambda block: swap_partners(block, 1), far_sum)
    total = plus(plus(near_sum, from_core[:quarter]), from_side).astype(jnp.bfloat16)
    mask = 2
    while 2 * mask < chips:
        partner = beside_fetch(lambda block: swap_partners(block, mask), total)
        total = plus(total, partner).astype(jnp.bfloat16)
        mask *= 2
    partner = beside_fetch(lambda block: swap_partners(block, mask), total)
    mixed_rows, normed = renew(total, partner, post_gain, local)
    across = swap_cores(normed)
    beyond = beside_fetch(lambda block: swap_partners(block, 1), normed)
    quarters = (normed, beyond, across, beside_fetch(swap_cores, beyond))
    own_sum, other_sum = feed(
        quarters, spans, [array for parts in fetched for array in parts], local
    )
    lowered = scatter_halves(own_sum, other_sum, chips)
    final_rows = (mixed_rows.astype(jnp.float32) + lowered).astype(jnp.bfloat16)
    return (mixed_rows, final_rows)


def gather_rows(rows, devices):
    copies = jnp.broadcast_to(rows[None], (devices,) + rows.shape)
    arrived = lax.all_to_all(copies, ("pool", "tensor"), split_axis=0, concat_axis=0, tiled=True)
    return arrived.reshape(devices * rows.shape[0], rows.shape[1])


def scatter_sum(partial, devices):
    blocks = partial.astype(jnp.bfloat16).reshape(devices, -1, partial.shape[1])
    arrived = lax.all_to_all(blocks, ("pool", "tensor"), split_axis=0, concat_axis=0, tiled=True)
    return jnp.sum(arrived.astype(jnp.float32), axis=0)


def on_device_general(
    hidden,
    input_gain,
    query_weight,
    key_weight,
    value_weight,
    query_gain,
    key_gain,
    output_weight,
    post_gain,
    gate_weight,
    up_weight,
    down_weight,
    key_cache,
    value_cache,
    lengths,
    request_slot,
):
    devices = lax.axis_size(("pool", "tensor"))
    device_index = lax.axis_index(("pool", "tensor"))
    local_rows = hidden.shape[0]
    query_cols = query_weight.shape[1]
    key_cols = key_weight.shape[1]
    width_sent = query_cols + 2 * key_cols
    head_dim = query_gain.shape[0]
    slot_count = SLOTS
    head_count = devices * query_cols // head_dim
    kv_count = devices * key_cols // head_dim
    group_size = head_count // kv_count
    normed = rms_scale(hidden, input_gain).astype(jnp.bfloat16)
    shard_rows = gather_rows(normed, devices)
    query_part = jnp.dot(shard_rows, query_weight, preferred_element_type=jnp.float32)
    key_part = jnp.dot(shard_rows, key_weight, preferred_element_type=jnp.float32)
    value_part = jnp.dot(shard_rows, value_weight, preferred_element_type=jnp.float32)
    projected = jnp.concatenate([query_part, key_part, value_part], axis=1).astype(jnp.bfloat16)
    outgoing = (
        jnp.zeros((devices * slot_count, width_sent), jnp.bfloat16).at[request_slot].set(projected)
    )
    outgoing = outgoing.reshape(devices, slot_count, width_sent)
    arrived = lax.all_to_all(
        outgoing, ("pool", "tensor"), split_axis=0, concat_axis=2, tiled=True
    ).reshape(slot_count, devices, width_sent)
    query_full = arrived[:, :, :query_cols].reshape(slot_count, head_count, head_dim)
    key_full = arrived[:, :, query_cols : query_cols + key_cols].reshape(
        slot_count, kv_count, head_dim
    )
    value_new = arrived[:, :, query_cols + key_cols :].reshape(slot_count, kv_count, head_dim)
    slot_ids = device_index * slot_count + jnp.arange(slot_count, dtype=jnp.int32)
    matches = request_slot[None, :] == slot_ids[:, None]
    slot_length = jnp.sum(jnp.where(matches, lengths[None, :], 0), axis=1)
    owner_of = request_slot // slot_count
    within = request_slot % slot_count
    earlier = (owner_of[None, :] == device_index) & (
        within[None, :] < jnp.arange(slot_count, dtype=jnp.int32)[:, None]
    )
    slot_offset = jnp.sum(jnp.where(earlier, lengths[None, :], 0), axis=1)
    position = slot_length.astype(jnp.float32)[:, None, None]
    query_heads = rotate(rms_scale(query_full, query_gain), position).astype(jnp.bfloat16)
    query_heads = query_heads.reshape(slot_count, kv_count, group_size, head_dim)
    key_new = rotate(rms_scale(key_full, key_gain), position).astype(jnp.bfloat16)
    pool_tokens = key_cache.shape[0]
    scale_factor = 1.0 / math.sqrt(head_dim)
    scores = jnp.stack(
        [
            jnp.einsum(
                "sgd,td->sgt",
                query_heads[:, kv],
                key_cache[:, kv * head_dim : (kv + 1) * head_dim],
                preferred_element_type=jnp.float32,
            )
            for kv in range(kv_count)
        ],
        axis=1,
    ) * scale_factor
    own_score = (
        jnp.einsum("skgd,skd->skg", query_heads, key_new, preferred_element_type=jnp.float32)
        * scale_factor
    )
    token_pos = jnp.arange(pool_tokens, dtype=jnp.int32)
    inside = (token_pos[None, :] >= slot_offset[:, None]) & (
        token_pos[None, :] < (slot_offset + slot_length)[:, None]
    )
    inside = inside[:, None, None, :]
    largest = jnp.maximum(jnp.max(jnp.where(inside, scores, -1e30), axis=3), own_score)
    weights = jnp.where(inside, jnp.exp(scores - largest[..., None]), 0.0)
    own_weight = jnp.exp(own_score - largest)
    denominator = jnp.sum(weights, axis=3) + own_weight
    weights_low = weights.astype(jnp.bfloat16)
    summed = jnp.stack(
        [
            jnp.einsum(
                "sgt,td->sgd",
                weights_low[:, kv],
                value_cache[:, kv * head_dim : (kv + 1) * head_dim],
                preferred_element_type=jnp.float32,
            )
            for kv in range(kv_count)
        ],
        axis=1,
    )
    own_low = own_weight.astype(jnp.bfloat16).astype(jnp.float32)
    summed = summed + own_low[..., None] * value_new.astype(jnp.float32)[:, :, None, :]
    head_out = (
        (summed / denominator[..., None])
        .astype(jnp.bfloat16)
        .reshape(slot_count, devices, query_cols)
    )
    returned = lax.all_to_all(head_out, ("pool", "tensor"), split_axis=1, concat_axis=0, tiled=True)
    head_rows = returned.reshape(devices * slot_count, query_cols)[request_slot]
    partial_value = jnp.dot(head_rows, output_weight, preferred_element_type=jnp.float32)
    mixed_rows = (hidden.astype(jnp.float32) + scatter_sum(partial_value, devices)).astype(jnp.bfloat16)
    post_normed = gather_rows(rms_scale(mixed_rows, post_gain).astype(jnp.bfloat16), devices)
    gate_part = jnp.dot(post_normed, gate_weight, preferred_element_type=jnp.float32)
    up_part = jnp.dot(post_normed, up_weight, preferred_element_type=jnp.float32)
    activated = (jax.nn.silu(gate_part) * up_part).astype(jnp.bfloat16)
    lowered = scatter_sum(
        jnp.dot(activated, down_weight, preferred_element_type=jnp.float32), devices
    )
    final_rows = (mixed_rows.astype(jnp.float32) + lowered).astype(jnp.bfloat16)
    return (mixed_rows, final_rows)


def on_device(*arrays):
    query_cols, key_cols = arrays[2].shape[1], arrays[3].shape[1]
    head_dim = arrays[5].shape[0]
    devices = lax.axis_size(("pool", "tensor"))
    kv_count = devices * key_cols // head_dim
    whole_heads = query_cols % head_dim == 0 and head_dim % LANES == 0
    shared = kv_count > 0 and devices % kv_count == 0
    chips = lax.axis_size("tensor")
    pairs = lax.axis_size("pool") == 2 and chips >= 4 and chips & (chips - 1) == 0
    pairs = pairs and arrays[14].shape[0] % 32 == 0
    if whole_heads and shared and pairs:
        return on_device_kernels(*arrays)
    return on_device_general(*arrays)


def solution(mesh):
    placed = (
        P(("groups", "pool", "tensor"), None),
        P(),
        P(None, ("pool", "tensor")),
        P(None, ("pool", "tensor")),
        P(None, ("pool", "tensor")),
        P(),
        P(),
        P(("pool", "tensor"), None),
        P(),
        P(None, ("pool", "tensor")),
        P(None, ("pool", "tensor")),
        P(("pool", "tensor"), None),
        P(("groups", "pool", "tensor"), None),
        P(("groups", "pool", "tensor"), None),
        P("groups"),
        P("groups"),
    )
    return jax.shard_map(
        on_device,
        mesh=mesh,
        in_specs=placed,
        out_specs=(P(("groups", "pool", "tensor"), None), P(("groups", "pool", "tensor"), None)),
        check_vma=False,
    )
```

```python
import functools
import math

import jax
import jax.numpy as jnp
from jax import lax
from jax.experimental import pallas as pl
from jax.experimental.pallas import tpu as pltpu
from jax.sharding import PartitionSpec as P

SLOTS = 4
LANES = 128
MIB = 2**20
TOKEN_STEP = 256
IN_VMEM = pl.BlockSpec(memory_space=pltpu.VMEM)
IN_HBM = pl.BlockSpec(memory_space=pl.ANY)


def cost(mib):
    return pl.CostEstimate(flops=0, bytes_accessed=mib * MIB, transcendentals=0)

STEP = 512


eps = 1e-06
theta = 1000000.0


def rms_scale(values, scales):
    values = values.astype(jnp.float32)
    return values * lax.rsqrt(jnp.mean(values * values, axis=-1, keepdims=True) + eps) * scales


def rotate(values, position):
    half_width = values.shape[-1] // 2
    frequency = theta ** (-jnp.arange(half_width, dtype=jnp.float32) * 2.0 / values.shape[-1])
    angles = position * frequency
    cosine = jnp.cos(angles)
    sine_part = jnp.sin(angles)
    front_half = values[..., :half_width]
    back_half = values[..., half_width:]
    return jnp.concatenate(
        [front_half * cosine - back_half * sine_part, back_half * cosine + front_half * sine_part],
        axis=-1,
    )


def swap_cores(block):
    return lax.ppermute(block, "pool", [(0, 1), (1, 0)])


def beside(exchange, blocks, work, *arrays):
    blocks, arrays = lax.optimization_barrier((blocks, arrays))
    return lax.optimization_barrier((exchange(blocks), work(*arrays)))


def swap_partners(block, mask):
    chips = lax.axis_size("tensor")
    return lax.ppermute(block, "tensor", [(chip, chip ^ mask) for chip in range(chips)])


def swap_chips(blocks):
    return lax.all_to_all(blocks, "tensor", split_axis=0, concat_axis=0, tiled=True)


def swap_all(blocks):
    return lax.all_to_all(blocks, ("pool", "tensor"), split_axis=0, concat_axis=0, tiled=True)


def spread_kernel(rows, unread, out):
    for chip in range(out.shape[0]):
        out[chip] = rows[...]


def spread(rows, chips, unread):
    return pl.pallas_call(
        spread_kernel,
        out_shape=jax.ShapeDtypeStruct((chips,) + rows.shape, rows.dtype),
        in_specs=[IN_VMEM, IN_HBM],
        out_specs=IN_VMEM,
        compiler_params=pltpu.CompilerParams(vmem_limit_bytes=MIB),
        cost_estimate=cost(8),
        name="spread",
    )(rows, keep_in_hbm(unread))


def gather_half(rows, chips, unread):
    return swap_chips(spread(rows, chips, unread))


def scatter_halves(own_half, other_half, chips):
    added = own_half.astype(jnp.float32) + swap_cores(other_half).astype(jnp.float32)
    blocks = added.astype(jnp.bfloat16).reshape(chips, -1, own_half.shape[1])
    return jnp.sum(swap_chips(blocks).astype(jnp.float32), axis=0)


def dot_rows(left, right):
    return lax.dot_general(
        left, right, (((1,), (0,)), ((), ())), preferred_element_type=jnp.float32
    )


def dot_columns(left, right):
    return lax.dot_general(
        left, right, (((1,), (1,)), ((), ())), preferred_element_type=jnp.float32
    )


def pieces(extent, step):
    return [(start, min(step, extent - start)) for start in range(0, extent, step)]


def keep_in_hbm(array):
    return pltpu.with_memory_space_constraint(array, pltpu.HBM)


def keep_in_vmem(array):
    return pltpu.with_memory_space_constraint(array, pltpu.VMEM)


def fetch_kernel(ranges, turned, *refs):
    count = len(ranges)
    sources, targets, stages = refs[:count], refs[count : 2 * count], list(refs[2 * count : -1])
    sems = refs[-1]
    copies, turns = [], []
    for index, (begin, end) in enumerate(ranges):
        if turned[index]:
            stage = stages.pop(0)
            for start, size in pieces(end - begin, STEP):
                turns.append((len(copies), stage, targets[index], start, size))
                copies.append(
                    pltpu.make_async_copy(
                        sources[index].at[:, pl.ds(begin + start, size)],
                        stage.at[:, pl.ds(start, size)],
                        sems.at[len(copies)],
                    )
                )
        else:
            copies.append(
                pltpu.make_async_copy(
                    sources[index].at[:, pl.ds(begin, end - begin)],
                    targets[index],
                    sems.at[len(copies)],
                )
            )
    for copy in copies:
        copy.start()
    for index, stage, target, start, size in turns:
        copies[index].wait()
        target[start : start + size, :] = stage[:, start : start + size].T
    turning = [index for index, *_ in turns]
    for index, copy in enumerate(copies):
        if index not in turning:
            copy.wait()


def fetch(ranges, turned, *arrays):
    shapes = [(array.shape[0], end - begin) for array, (begin, end) in zip(arrays, ranges)]
    size = sum(2 * rows * columns for rows, columns in shapes)
    stages = [pltpu.VMEM(shape, jnp.bfloat16) for shape, turn in zip(shapes, turned) if turn]
    count = sum(
        len(pieces(columns, STEP)) if turn else 1 for (_, columns), turn in zip(shapes, turned)
    )
    staged = sum(2 * rows * columns for (rows, columns), turn in zip(shapes, turned) if turn)
    return pl.pallas_call(
        functools.partial(fetch_kernel, ranges, turned),
        out_shape=tuple(
            pltpu.VMEM(shape[::-1] if turn else shape, array.dtype)
            for array, shape, turn in zip(arrays, shapes, turned)
        ),
        in_specs=[IN_HBM] * len(arrays),
        out_specs=tuple([IN_VMEM] * len(arrays)),
        scratch_shapes=stages + [pltpu.SemaphoreType.DMA((count,))],
        compiler_params=pltpu.CompilerParams(vmem_limit_bytes=2 * MIB + staged),
        cost_estimate=pl.CostEstimate(flops=0, bytes_accessed=size, transcendentals=0),
        name="fetch",
    )(*[keep_in_hbm(array) for array in arrays])


def split_columns(arrays, width, shares):
    blocks = [(array, start, size) for array in arrays for start, size in pieces(width, STEP)]
    result = []
    done = 0
    for index in range(len(shares)):
        upto = len(blocks) * sum(shares[: index + 1]) // sum(shares)
        part = blocks[done:upto]
        done = upto
        spans = []
        for array in arrays:
            mine = [(start, size) for which, start, size in part if which == array]
            if mine:
                spans.append((array, mine[0][0], mine[-1][0] + mine[-1][1]))
        result.append(spans)
    return result


def flat_rows(blocks):
    return jnp.concatenate(
        [blocks[chip].astype(jnp.float32) for chip in range(blocks.shape[0])], axis=0
    )


def one_hot(rows, columns):
    return jnp.where(rows == columns, 1.0, 0.0).astype(jnp.bfloat16)


def slot_matrix(slots, places):
    return one_hot(lax.broadcasted_iota(jnp.int32, (places, slots.shape[1]), 0), slots[...])


def prepare_kernel(
    slot_count,
    slots,
    lengths,
    frequency,
    packing,
    unpacking,
    first,
    last,
    cosine,
    sine,
):
    places, requests = packing.shape
    owners = places // slot_count
    core, parity = lax.axis_index("pool"), lax.rem(lax.axis_index("tensor"), 2)
    natural = slot_matrix(slots, places)
    row = lax.broadcasted_iota(jnp.int32, (requests, requests), 0)
    column = lax.broadcasted_iota(jnp.int32, (requests, requests), 1)
    half_first = one_hot(lax.rem(column + core * (requests // 2), requests), row)
    packing[...] = dot_rows(natural, half_first).astype(jnp.bfloat16)
    half, quarter, local = requests // 2, requests // 4, requests // owners
    half_of = lax.rem(row // half + core, 2)
    side_of = lax.rem(row // quarter + parity, 2)
    pair, inner = lax.rem(row, quarter) // local, lax.rem(row, local)
    source = half_of * half + (pair * 2 + side_of) * local + inner
    unpacking[...] = dot_columns(one_hot(source, column), natural).astype(jnp.bfloat16)
    start = lax.axis_index(("pool", "tensor")) * slot_count
    place = slots[...] - start
    rows = lax.broadcasted_iota(jnp.int32, (slot_count, requests), 0)
    amounts = lengths[...].astype(jnp.float32)
    length = jnp.sum(jnp.where(place == rows, amounts, 0.0), axis=1, keepdims=True)
    offset = jnp.sum(
        jnp.where((place >= 0) & (place < rows), amounts, 0.0), axis=1, keepdims=True
    )
    angles = length * frequency[...]
    turn = jnp.sin(angles)
    lean = jnp.cos(angles)
    cosine[...] = jnp.concatenate([lean, lean], axis=1)
    sine[...] = jnp.concatenate([-turn, turn], axis=1)
    first[...] = jnp.broadcast_to(offset.astype(jnp.int32), first.shape)
    last[...] = jnp.broadcast_to((offset + length).astype(jnp.int32), last.shape)


def prepare(slot_count, devices, head_dim, slots, lengths):
    requests = slots.shape[0]
    places = devices * slot_count
    frequency = theta ** (-jnp.arange(head_dim // 2, dtype=jnp.float32) * 2.0 / head_dim)
    table = jax.ShapeDtypeStruct((slot_count, head_dim), jnp.float32)
    bound = jax.ShapeDtypeStruct((slot_count, head_dim), jnp.int32)
    return pl.pallas_call(
        functools.partial(prepare_kernel, slot_count),
        out_shape=(
            jax.ShapeDtypeStruct((places, requests), jnp.bfloat16),
            jax.ShapeDtypeStruct((requests, places), jnp.bfloat16),
            bound,
            bound,
            table,
            table,
        ),
        in_specs=[IN_VMEM] * 3,
        out_specs=tuple([IN_VMEM] * 6),
        compiler_params=pltpu.CompilerParams(vmem_limit_bytes=MIB),
        cost_estimate=cost(8),
        name="prepare",
    )(
        slots.reshape(1, -1),
        lengths.reshape(1, -1),
        frequency.reshape(1, -1),
    )


def project_kernel(slot_count, own, other, gain, packing, q_vm, k_vm, v_vm, out, normed):
    half = own.shape[0] * own.shape[1]
    for index, source in enumerate((own, other)):
        rows = flat_rows(source)
        scale = lax.rsqrt(jnp.mean(rows * rows, axis=-1, keepdims=True) + eps)
        normed[pl.ds(index * half, half), :] = (rows * scale * gain[...]).astype(jnp.bfloat16)
    query_part = dot_rows(normed[...], q_vm[...])
    key_part = dot_columns(normed[...], k_vm[...])
    value_part = dot_columns(normed[...], v_vm[...])
    projected = jnp.concatenate([query_part, key_part, value_part], axis=1).astype(jnp.bfloat16)
    packed = dot_rows(packing[...], projected)
    for owner in range(out.shape[0]):
        out[owner] = packed[owner * slot_count : (owner + 1) * slot_count, :].astype(jnp.bfloat16)


def project(slot_count, own, other, gain, packing, weights):
    depth, query_cols = weights[0].shape
    width = query_cols + weights[1].shape[0] + weights[2].shape[0]
    places, requests = packing.shape
    return pl.pallas_call(
        functools.partial(project_kernel, slot_count),
        out_shape=jax.ShapeDtypeStruct((places // slot_count, slot_count, width), jnp.bfloat16),
        in_specs=[IN_VMEM] * 7,
        out_specs=IN_VMEM,
        scratch_shapes=[pltpu.VMEM((requests, depth), jnp.bfloat16)],
        compiler_params=pltpu.CompilerParams(vmem_limit_bytes=8 * MIB),
        cost_estimate=cost(32),
        name="project",
    )(
        own,
        other,
        gain.reshape(1, depth),
        packing,
        *weights,
    )


def attend_kernel(
    query_cols,
    key_cols,
    arrived,
    first,
    last,
    cosine,
    sine,
    query_gain,
    key_gain,
    keys,
    values,
    out,
    queries,
    scores,
):
    devices, slot_count, _ = arrived.shape
    tokens, width = keys.shape
    head_dim = query_gain.shape[1]
    kv_count = devices * key_cols // head_dim
    sharers = devices // kv_count
    heads_here = query_cols // head_dim
    repeats = sharers * heads_here
    count = repeats * slot_count
    parts = pieces(tokens, TOKEN_STEP)
    scale_factor = 1.0 / math.sqrt(head_dim)

    def tile(rows, times):
        return jnp.concatenate([rows] * times, axis=0)

    def prepare(rows, gain, times):
        rows = rows * lax.rsqrt(jnp.mean(rows * rows, axis=-1, keepdims=True) + eps) * gain[...]
        turned = pltpu.roll(rows, head_dim // 2, 1)
        return (rows * tile(cosine[...], times) + turned * tile(sine[...], times)).astype(
            jnp.bfloat16
        )

    blocks = [arrived[device].astype(jnp.float32) for device in range(devices)]
    rows = jnp.concatenate(
        [
            blocks[kv * sharers + place][:, head * head_dim : (head + 1) * head_dim]
            for kv in range(kv_count)
            for head in range(heads_here)
            for place in range(sharers)
        ],
        axis=0,
    )
    query = prepare(rows, query_gain, kv_count * repeats)

    def whole(begin):
        return [
            jnp.concatenate(
                [
                    blocks[kv * sharers + place][:, begin : begin + key_cols]
                    for place in range(sharers)
                ],
                axis=1,
            )
            for kv in range(kv_count)
        ]

    fresh = prepare(jnp.concatenate(whole(query_cols), axis=0), key_gain, kv_count)
    fresh = fresh.astype(jnp.float32)
    key_new = jnp.concatenate(
        [
            tile(fresh[kv * slot_count : (kv + 1) * slot_count, :], repeats)
            for kv in range(kv_count)
        ],
        axis=0,
    )
    value_new = [tile(rows, repeats) for rows in whole(query_cols + key_cols)]
    own_score = (
        jnp.sum(query.astype(jnp.float32) * key_new, axis=-1, keepdims=True) * scale_factor
    )
    queries[...] = jnp.zeros(queries.shape, queries.dtype)
    for kv in range(kv_count):
        queries[kv * count : (kv + 1) * count, kv * head_dim : (kv + 1) * head_dim] = query[
            kv * count : (kv + 1) * count, :
        ]
    start = tile(first[:, :1], kv_count * repeats)
    end = tile(last[:, :1], kv_count * repeats)
    largest = own_score
    for begin, size in parts:
        positions = lax.broadcasted_iota(jnp.int32, (kv_count * count, size), 1) + begin
        inside = (positions >= start) & (positions < end)
        part = dot_columns(queries[...], keys[begin : begin + size, :]) * scale_factor
        part = jnp.where(inside, part, -1e30)
        scores[:, begin : begin + size] = part
        largest = jnp.maximum(largest, jnp.max(part, axis=1, keepdims=True))
    own_weight = jnp.exp(own_score - largest)
    denominator = own_weight
    summed = jnp.zeros((kv_count * count, width), jnp.float32)
    for begin, size in parts:
        weights = jnp.exp(scores[:, begin : begin + size] - largest)
        denominator = denominator + jnp.sum(weights, axis=1, keepdims=True)
        summed = summed + dot_rows(
            weights.astype(jnp.bfloat16), values[begin : begin + size, :]
        )
    own_low = own_weight.astype(jnp.bfloat16).astype(jnp.float32)
    for kv in range(kv_count):
        span = slice(kv * count, (kv + 1) * count)
        mine = summed[span, kv * head_dim : (kv + 1) * head_dim]
        mine = (mine + own_low[span, :] * value_new[kv]) / denominator[span, :]
        for head in range(heads_here):
            for place in range(sharers):
                row = (head * sharers + place) * slot_count
                out[kv * sharers + place, :, head * head_dim : (head + 1) * head_dim] = mine[
                    row : row + slot_count, :
                ].astype(jnp.bfloat16)


def attend(arrived, planned, query_gain, key_gain, key_cache, value_cache, query_cols):
    devices, slot_count, width = arrived.shape
    key_cols = (width - query_cols) // 2
    head_dim = query_gain.shape[0]
    tokens, cache_width = key_cache.shape
    rows = devices * query_cols // head_dim * slot_count
    return pl.pallas_call(
        functools.partial(attend_kernel, query_cols, key_cols),
        out_shape=jax.ShapeDtypeStruct((devices, slot_count, query_cols), jnp.bfloat16),
        in_specs=[IN_VMEM] * 9,
        out_specs=IN_VMEM,
        scratch_shapes=[
            pltpu.VMEM((rows, cache_width), jnp.bfloat16),
            pltpu.VMEM((rows, tokens), jnp.float32),
        ],
        compiler_params=pltpu.CompilerParams(vmem_limit_bytes=16 * MIB),
        name="attend",
    )(
        arrived,
        *planned,
        query_gain.reshape(1, head_dim),
        key_gain.reshape(1, head_dim),
        key_cache,
        value_cache,
    )


def mix_kernel(returned, unpacking, weight, hidden, near_out, far_out, other_out):
    owners = returned.shape[0]
    quarter, width = near_out.shape
    local = hidden.shape[0]
    pair = lax.axis_index("tensor") // 2
    by_slot = jnp.concatenate(
        [returned[owner].astype(jnp.float32) for owner in range(owners)], axis=0
    ).astype(jnp.bfloat16)
    rows = dot_rows(unpacking[...], by_slot).astype(jnp.bfloat16)
    for start, size in pieces(width, 1024):
        columns = slice(start, start + size)
        total = dot_rows(rows, weight[:, columns])
        residual = hidden[:, columns].astype(jnp.float32)
        near_out[:, columns] = total[:quarter] + jnp.concatenate(
            [jnp.where(pair == index, residual, 0.0) for index in range(quarter // local)], axis=0
        )
        far_out[:, columns] = total[quarter : 2 * quarter]
        other_out[:, columns] = total[2 * quarter :].astype(other_out.dtype)


def mix(returned, unpacking, output_weight, hidden):
    quarter, width = unpacking.shape[0] // 4, output_weight.shape[1]
    return pl.pallas_call(
        mix_kernel,
        out_shape=(
            jax.ShapeDtypeStruct((quarter, width), jnp.float32),
            jax.ShapeDtypeStruct((quarter, width), jnp.float32),
            jax.ShapeDtypeStruct((2 * quarter, width), jnp.bfloat16),
        ),
        in_specs=[IN_VMEM] * 4,
        out_specs=(IN_VMEM, IN_VMEM, IN_VMEM),
        compiler_params=pltpu.CompilerParams(vmem_limit_bytes=8 * MIB),
        name="mix",
    )(returned, unpacking, output_weight, hidden)


def renew_kernel(own, partner, gain, mixed, normed):
    local = mixed.shape[0]
    total = own[...].astype(jnp.float32) + partner[...].astype(jnp.float32)
    rows = total.astype(jnp.bfloat16).astype(jnp.float32)
    scale = lax.rsqrt(jnp.mean(rows * rows, axis=-1, keepdims=True) + eps)
    normed[...] = (rows * scale * gain[...]).astype(jnp.bfloat16)
    pair = lax.axis_index("tensor") // 2
    here = rows[:local]
    for index in range(1, rows.shape[0] // local):
        here = jnp.where(pair == index, rows[index * local : (index + 1) * local], here)
    mixed[...] = here.astype(jnp.bfloat16)


def renew(own, partner, gain, local):
    return pl.pallas_call(
        renew_kernel,
        out_shape=(
            jax.ShapeDtypeStruct((local, own.shape[1]), jnp.bfloat16),
            jax.ShapeDtypeStruct(own.shape, jnp.bfloat16),
        ),
        in_specs=[IN_VMEM] * 3,
        out_specs=(IN_VMEM, IN_VMEM),
        compiler_params=pltpu.CompilerParams(vmem_limit_bytes=4 * MIB),
        name="renew",
    )(own, partner, gain.reshape(1, -1))


def feed_kernel(spans, local, *refs):
    quarters, weights = refs[:4], refs[4 : 4 + len(spans)]
    own_out, other_out, rows = refs[4 + len(spans) :]
    half, width = own_out.shape
    quarter = half // 2

    def part(array, start, size):
        for (index, begin, end), ref in zip(spans, weights):
            if index == array and begin <= start and start + size <= end:
                span = slice(start - begin, start - begin + size)
                return ref[:, span] if index == 2 else ref[span, :]

    for index in range(2):
        rows[index * half : (index + 1) * half, :] = jnp.concatenate(
            [block[...].astype(jnp.float32) for block in quarters[2 * index : 2 * index + 2]],
            axis=0,
        ).astype(jnp.bfloat16)
    gate_part = up_part = 0.0
    for start, size in pieces(width, STEP):
        some = rows[:, start : start + size]
        gate_part = gate_part + dot_rows(some, part(0, start, size))
        up_part = up_part + dot_rows(some, part(1, start, size))
    active = (gate_part / (1.0 + jnp.exp(-gate_part)) * up_part).astype(jnp.bfloat16)
    parity = lax.rem(lax.axis_index("tensor"), 2)
    row = lax.broadcasted_iota(jnp.int32, (2 * half, 2 * half), 0)
    place = lax.rem(row, half)
    pair, inner = place // (2 * local), lax.rem(place, local)
    side_of = lax.rem(place // local + parity, 2)
    source = (row // half) * half + side_of * quarter + pair * local + inner
    order = one_hot(source, lax.broadcasted_iota(jnp.int32, (2 * half, 2 * half), 1))
    active = dot_rows(order, active).astype(jnp.bfloat16)
    for start, size in pieces(width, STEP):
        total = dot_rows(active, part(2, start, size))
        own_out[:, start : start + size] = total[:half]
        other_out[:, start : start + size] = total[half:].astype(other_out.dtype)


def feed(quarters, spans, weights, local):
    quarter, width = quarters[0].shape
    half = 2 * quarter
    return pl.pallas_call(
        functools.partial(feed_kernel, spans, local),
        out_shape=(
            jax.ShapeDtypeStruct((half, width), jnp.float32),
            jax.ShapeDtypeStruct((half, width), jnp.bfloat16),
        ),
        in_specs=[IN_VMEM] * (4 + len(spans)),
        out_specs=(IN_VMEM, IN_VMEM),
        scratch_shapes=[pltpu.VMEM((2 * half, width), jnp.bfloat16)],
        compiler_params=pltpu.CompilerParams(vmem_limit_bytes=4 * MIB),
        name="feed",
    )(*quarters, *[keep_in_vmem(weight) for weight in weights])


def on_device_kernels(
    hidden,
    input_gain,
    query_weight,
    key_weight,
    value_weight,
    query_gain,
    key_gain,
    output_weight,
    post_gain,
    gate_weight,
    up_weight,
    down_weight,
    key_cache,
    value_cache,
    lengths,
    request_slot,
):
    devices = lax.axis_size(("pool", "tensor"))
    chips = lax.axis_size("tensor")
    local, width = hidden.shape
    quarter = lengths.shape[0] // 4
    slot_count = SLOTS
    query_cols = query_weight.shape[1]
    head_dim = query_gain.shape[0]
    own = gather_half(hidden, chips, gate_weight.T)
    packing, unpacking, *planned = prepare(
        slot_count, devices, head_dim, request_slot, lengths
    )
    other = swap_cores(own)
    weights = (query_weight, key_weight.T, value_weight.T)
    outgoing = project(slot_count, own, other, input_gain, packing, weights)
    head_out = attend(
        swap_all(outgoing), planned, query_gain, key_gain, key_cache, value_cache, query_cols
    )
    returned = swap_all(head_out)
    near_sum, far_sum, other_sum = mix(returned, unpacking, output_weight, hidden)

    layers = (gate_weight.T, up_weight.T, down_weight)
    steps = chips.bit_length()
    turned = split_columns([0, 1], width, [5] * (steps - 2) + [6, 4, 0])
    straight = split_columns([2], width, [2] * (steps - 1) + [3, 1])
    groups = [first + second for first, second in zip(turned, straight)]
    spans, fetched = [], []

    def beside_fetch(exchange, block):
        group = groups[len(fetched)]
        work = functools.partial(
            fetch,
            [(begin, end) for _, begin, end in group],
            [index < 2 for index, _, _ in group],
        )
        block, parts = beside(exchange, block, work, *[layers[index] for index, _, _ in group])
        spans.extend(group)
        fetched.append(parts)
        return block

    def plus(left, right):
        return left.astype(jnp.float32) + right.astype(jnp.float32)

    from_core = swap_cores(other_sum)
    far_sum = plus(far_sum, from_core[quarter:]).astype(jnp.bfloat16)
    from_side = beside_fetch(lambda block: swap_partners(block, 1), far_sum)
    total = plus(plus(near_sum, from_core[:quarter]), from_side).astype(jnp.bfloat16)
    mask = 2
    while 2 * mask < chips:
        partner = beside_fetch(lambda block: swap_partners(block, mask), total)
        total = plus(total, partner).astype(jnp.bfloat16)
        mask *= 2
    partner = beside_fetch(lambda block: swap_partners(block, mask), total)
    mixed_rows, normed = renew(total, partner, post_gain, local)
    beyond, across = beside_fetch(
        lambda block: (swap_partners(block, 1), swap_cores(block)), normed
    )
    quarters = (normed, beyond, across, beside_fetch(swap_cores, beyond))
    own_sum, other_sum = feed(
        quarters, spans, [array for parts in fetched for array in parts], local
    )
    lowered = scatter_halves(own_sum, other_sum, chips)
    final_rows = (mixed_rows.astype(jnp.float32) + lowered).astype(jnp.bfloat16)
    return (mixed_rows, final_rows)


def gather_rows(rows, devices):
    copies = jnp.broadcast_to(rows[None], (devices,) + rows.shape)
    arrived = lax.all_to_all(copies, ("pool", "tensor"), split_axis=0, concat_axis=0, tiled=True)
    return arrived.reshape(devices * rows.shape[0], rows.shape[1])


def scatter_sum(partial, devices):
    blocks = partial.astype(jnp.bfloat16).reshape(devices, -1, partial.shape[1])
    arrived = lax.all_to_all(blocks, ("pool", "tensor"), split_axis=0, concat_axis=0, tiled=True)
    return jnp.sum(arrived.astype(jnp.float32), axis=0)


def on_device_general(
    hidden,
    input_gain,
    query_weight,
    key_weight,
    value_weight,
    query_gain,
    key_gain,
    output_weight,
    post_gain,
    gate_weight,
    up_weight,
    down_weight,
    key_cache,
    value_cache,
    lengths,
    request_slot,
):
    devices = lax.axis_size(("pool", "tensor"))
    device_index = lax.axis_index(("pool", "tensor"))
    local_rows = hidden.shape[0]
    query_cols = query_weight.shape[1]
    key_cols = key_weight.shape[1]
    width_sent = query_cols + 2 * key_cols
    head_dim = query_gain.shape[0]
    slot_count = SLOTS
    head_count = devices * query_cols // head_dim
    kv_count = devices * key_cols // head_dim
    group_size = head_count // kv_count
    normed = rms_scale(hidden, input_gain).astype(jnp.bfloat16)
    shard_rows = gather_rows(normed, devices)
    query_part = jnp.dot(shard_rows, query_weight, preferred_element_type=jnp.float32)
    key_part = jnp.dot(shard_rows, key_weight, preferred_element_type=jnp.float32)
    value_part = jnp.dot(shard_rows, value_weight, preferred_element_type=jnp.float32)
    projected = jnp.concatenate([query_part, key_part, value_part], axis=1).astype(jnp.bfloat16)
    outgoing = (
        jnp.zeros((devices * slot_count, width_sent), jnp.bfloat16).at[request_slot].set(projected)
    )
    outgoing = outgoing.reshape(devices, slot_count, width_sent)
    arrived = lax.all_to_all(
        outgoing, ("pool", "tensor"), split_axis=0, concat_axis=2, tiled=True
    ).reshape(slot_count, devices, width_sent)
    query_full = arrived[:, :, :query_cols].reshape(slot_count, head_count, head_dim)
    key_full = arrived[:, :, query_cols : query_cols + key_cols].reshape(
        slot_count, kv_count, head_dim
    )
    value_new = arrived[:, :, query_cols + key_cols :].reshape(slot_count, kv_count, head_dim)
    slot_ids = device_index * slot_count + jnp.arange(slot_count, dtype=jnp.int32)
    matches = request_slot[None, :] == slot_ids[:, None]
    slot_length = jnp.sum(jnp.where(matches, lengths[None, :], 0), axis=1)
    owner_of = request_slot // slot_count
    within = request_slot % slot_count
    earlier = (owner_of[None, :] == device_index) & (
        within[None, :] < jnp.arange(slot_count, dtype=jnp.int32)[:, None]
    )
    slot_offset = jnp.sum(jnp.where(earlier, lengths[None, :], 0), axis=1)
    position = slot_length.astype(jnp.float32)[:, None, None]
    query_heads = rotate(rms_scale(query_full, query_gain), position).astype(jnp.bfloat16)
    query_heads = query_heads.reshape(slot_count, kv_count, group_size, head_dim)
    key_new = rotate(rms_scale(key_full, key_gain), position).astype(jnp.bfloat16)
    pool_tokens = key_cache.shape[0]
    scale_factor = 1.0 / math.sqrt(head_dim)
    scores = jnp.stack(
        [
            jnp.einsum(
                "sgd,td->sgt",
                query_heads[:, kv],
                key_cache[:, kv * head_dim : (kv + 1) * head_dim],
                preferred_element_type=jnp.float32,
            )
            for kv in range(kv_count)
        ],
        axis=1,
    ) * scale_factor
    own_score = (
        jnp.einsum("skgd,skd->skg", query_heads, key_new, preferred_element_type=jnp.float32)
        * scale_factor
    )
    token_pos = jnp.arange(pool_tokens, dtype=jnp.int32)
    inside = (token_pos[None, :] >= slot_offset[:, None]) & (
        token_pos[None, :] < (slot_offset + slot_length)[:, None]
    )
    inside = inside[:, None, None, :]
    largest = jnp.maximum(jnp.max(jnp.where(inside, scores, -1e30), axis=3), own_score)
    weights = jnp.where(inside, jnp.exp(scores - largest[..., None]), 0.0)
    own_weight = jnp.exp(own_score - largest)
    denominator = jnp.sum(weights, axis=3) + own_weight
    weights_low = weights.astype(jnp.bfloat16)
    summed = jnp.stack(
        [
            jnp.einsum(
                "sgt,td->sgd",
                weights_low[:, kv],
                value_cache[:, kv * head_dim : (kv + 1) * head_dim],
                preferred_element_type=jnp.float32,
            )
            for kv in range(kv_count)
        ],
        axis=1,
    )
    own_low = own_weight.astype(jnp.bfloat16).astype(jnp.float32)
    summed = summed + own_low[..., None] * value_new.astype(jnp.float32)[:, :, None, :]
    head_out = (
        (summed / denominator[..., None])
        .astype(jnp.bfloat16)
        .reshape(slot_count, devices, query_cols)
    )
    returned = lax.all_to_all(head_out, ("pool", "tensor"), split_axis=1, concat_axis=0, tiled=True)
    head_rows = returned.reshape(devices * slot_count, query_cols)[request_slot]
    partial_value = jnp.dot(head_rows, output_weight, preferred_element_type=jnp.float32)
    mixed_rows = (hidden.astype(jnp.float32) + scatter_sum(partial_value, devices)).astype(jnp.bfloat16)
    post_normed = gather_rows(rms_scale(mixed_rows, post_gain).astype(jnp.bfloat16), devices)
    gate_part = jnp.dot(post_normed, gate_weight, preferred_element_type=jnp.float32)
    up_part = jnp.dot(post_normed, up_weight, preferred_element_type=jnp.float32)
    activated = (jax.nn.silu(gate_part) * up_part).astype(jnp.bfloat16)
    lowered = scatter_sum(
        jnp.dot(activated, down_weight, preferred_element_type=jnp.float32), devices
    )
    final_rows = (mixed_rows.astype(jnp.float32) + lowered).astype(jnp.bfloat16)
    return (mixed_rows, final_rows)


def on_device(*arrays):
    query_cols, key_cols = arrays[2].shape[1], arrays[3].shape[1]
    head_dim = arrays[5].shape[0]
    devices = lax.axis_size(("pool", "tensor"))
    kv_count = devices * key_cols // head_dim
    whole_heads = query_cols % head_dim == 0 and head_dim % LANES == 0
    shared = kv_count > 0 and devices % kv_count == 0
    chips = lax.axis_size("tensor")
    pairs = lax.axis_size("pool") == 2 and chips >= 4 and chips & (chips - 1) == 0
    pairs = pairs and arrays[14].shape[0] % 32 == 0
    if whole_heads and shared and pairs:
        return on_device_kernels(*arrays)
    return on_device_general(*arrays)


def solution(mesh):
    placed = (
        P(("groups", "pool", "tensor"), None),
        P(),
        P(None, ("pool", "tensor")),
        P(None, ("pool", "tensor")),
        P(None, ("pool", "tensor")),
        P(),
        P(),
        P(("pool", "tensor"), None),
        P(),
        P(None, ("pool", "tensor")),
        P(None, ("pool", "tensor")),
        P(("pool", "tensor"), None),
        P(("groups", "pool", "tensor"), None),
        P(("groups", "pool", "tensor"), None),
        P("groups"),
        P("groups"),
    )
    return jax.shard_map(
        on_device,
        mesh=mesh,
        in_specs=placed,
        out_specs=(P(("groups", "pool", "tensor"), None), P(("groups", "pool", "tensor"), None)),
        check_vma=False,
    )
```

```python
import functools
import math

import jax
import jax.numpy as jnp
from jax import lax
from jax.experimental import pallas as pl
from jax.experimental.pallas import tpu as pltpu
from jax.sharding import PartitionSpec as P

SLOTS = 4
SIDES = 4
LANES = 128
MIB = 2**20
TOKEN_STEP = 256
IN_VMEM = pl.BlockSpec(memory_space=pltpu.VMEM)
IN_HBM = pl.BlockSpec(memory_space=pl.ANY)


def cost(mib):
    return pl.CostEstimate(flops=0, bytes_accessed=mib * MIB, transcendentals=0)

STEP = 512
FEED_STEP = 256


eps = 1e-06
theta = 1000000.0


def rms_scale(values, scales):
    values = values.astype(jnp.float32)
    return values * lax.rsqrt(jnp.mean(values * values, axis=-1, keepdims=True) + eps) * scales


def rotate(values, position):
    half_width = values.shape[-1] // 2
    frequency = theta ** (-jnp.arange(half_width, dtype=jnp.float32) * 2.0 / values.shape[-1])
    angles = position * frequency
    cosine = jnp.cos(angles)
    sine_part = jnp.sin(angles)
    front_half = values[..., :half_width]
    back_half = values[..., half_width:]
    return jnp.concatenate(
        [front_half * cosine - back_half * sine_part, back_half * cosine + front_half * sine_part],
        axis=-1,
    )


def swap_cores(block):
    return lax.ppermute(block, "pool", [(0, 1), (1, 0)])


def swap_partners(block, mask):
    chips = lax.axis_size("tensor")
    return lax.ppermute(block, "tensor", [(chip, chip ^ mask) for chip in range(chips)])


def swap_chips(blocks):
    return lax.all_to_all(blocks, "tensor", split_axis=0, concat_axis=0, tiled=True)


def swap_all(blocks):
    return lax.all_to_all(blocks, ("pool", "tensor"), split_axis=0, concat_axis=0, tiled=True)


def spread_kernel(rows, unread, out):
    for chip in range(out.shape[0]):
        out[chip] = rows[...]


def spread(rows, chips, unread):
    return pl.pallas_call(
        spread_kernel,
        out_shape=jax.ShapeDtypeStruct((chips,) + rows.shape, rows.dtype),
        in_specs=[IN_VMEM, IN_HBM],
        out_specs=IN_VMEM,
        compiler_params=pltpu.CompilerParams(vmem_limit_bytes=MIB),
        cost_estimate=cost(8),
        name="spread",
    )(rows, keep_in_hbm(unread))


def gather_half(rows, chips, unread):
    return swap_chips(spread(rows, chips, unread))


def scatter_halves(own_half, other_half, chips):
    added = own_half.astype(jnp.float32) + swap_cores(other_half).astype(jnp.float32)
    blocks = added.astype(jnp.bfloat16).reshape(chips, -1, own_half.shape[1])
    return jnp.sum(swap_chips(blocks).astype(jnp.float32), axis=0)


def dot_rows(left, right):
    return lax.dot_general(
        left, right, (((1,), (0,)), ((), ())), preferred_element_type=jnp.float32
    )


def dot_columns(left, right):
    return lax.dot_general(
        left, right, (((1,), (1,)), ((), ())), preferred_element_type=jnp.float32
    )


def pieces(extent, step):
    return [(start, min(step, extent - start)) for start in range(0, extent, step)]


def keep_in_hbm(array):
    return pltpu.with_memory_space_constraint(array, pltpu.HBM)


def keep_in_vmem(array):
    return pltpu.with_memory_space_constraint(array, pltpu.VMEM)


def split_range(count, shares):
    ends = [count * sum(shares[: index + 1]) // sum(shares) * STEP for index in range(len(shares))]
    starts = [0] + ends[:-1]
    return [(start, end) if start < end else None for start, end in zip(starts, ends)]


def load_kernel(far, near, token, far_rows, near_rows, *refs):
    outs = list(refs[: bool(far) + bool(near)])
    copies, stage = [], None
    if far:
        begin, end = far
        stage, sems = refs[-2:]
        for index, (start, size) in enumerate(pieces(end - begin, STEP)):
            copies.append(
                pltpu.make_async_copy(
                    far_rows.at[:, pl.ds(begin + start, size)],
                    stage.at[:, pl.ds(start, size)],
                    sems.at[index],
                )
            )
            copies[-1].start()
    if near:
        begin, end = near
        for start, size in pieces(end - begin, STEP):
            outs[-1][start : start + size, :] = near_rows[:, begin + start : begin + start + size].T
    for copy, (start, size) in zip(copies, pieces(far[1] - far[0], STEP) if far else []):
        copy.wait()
        outs[0][start : start + size, :] = stage[:, start : start + size].T


def load(far, near, token, far_rows, near_rows):
    units, width = far_rows.shape
    ranges = [span for span in (far, near) if span]
    staged = 2 * units * (far[1] - far[0]) if far else 0
    scratch = []
    if far:
        scratch = [
            pltpu.VMEM((units, far[1] - far[0]), far_rows.dtype),
            pltpu.SemaphoreType.DMA((len(pieces(far[1] - far[0], STEP)),)),
        ]
    return pl.pallas_call(
        functools.partial(load_kernel, far, near),
        out_shape=tuple(pltpu.VMEM((end - begin, units), far_rows.dtype) for begin, end in ranges),
        in_specs=[IN_HBM, IN_HBM, IN_VMEM if near else IN_HBM],
        out_specs=tuple([IN_VMEM] * len(ranges)),
        scratch_shapes=scratch,
        compiler_params=pltpu.CompilerParams(
            vmem_limit_bytes=2 * MIB + staged + (2 * units * width if near else 0)
        ),
        cost_estimate=cost(8),
        name="load",
    )(token, keep_in_hbm(far_rows), near_rows if near else keep_in_hbm(near_rows))


def flat_rows(blocks):
    return jnp.concatenate(
        [blocks[chip].astype(jnp.float32) for chip in range(blocks.shape[0])], axis=0
    )


def one_hot(rows, columns):
    return jnp.where(rows == columns, 1.0, 0.0).astype(jnp.bfloat16)


def differ(mask):
    here = lax.rem(lax.axis_index("tensor"), SIDES)
    low = lax.rem(lax.rem(mask, 2) + lax.rem(here, 2), 2)
    high = lax.rem(mask // 2 + here // 2, 2)
    return 2 * high + low


def slot_matrix(slots, places):
    return one_hot(lax.broadcasted_iota(jnp.int32, (places, slots.shape[1]), 0), slots[...])


def prepare_kernel(
    slot_count,
    slots,
    lengths,
    frequency,
    packing,
    unpacking,
    first,
    last,
    cosine,
    sine,
):
    places, requests = packing.shape
    owners = places // slot_count
    core = lax.axis_index("pool")
    natural = slot_matrix(slots, places)
    row = lax.broadcasted_iota(jnp.int32, (requests, requests), 0)
    column = lax.broadcasted_iota(jnp.int32, (requests, requests), 1)
    half_first = one_hot(lax.rem(column + core * (requests // 2), requests), row)
    packing[...] = dot_rows(natural, half_first).astype(jnp.bfloat16)
    half, block, local = requests // 2, requests // 2 // SIDES, requests // owners
    half_of = lax.rem(row // half + core, 2)
    side = differ(lax.rem(row, half) // block)
    inner = lax.rem(row, local)
    source = half_of * half + (lax.rem(row, block) // local * SIDES + side) * local + inner
    unpacking[...] = dot_columns(one_hot(source, column), natural).astype(jnp.bfloat16)
    start = lax.axis_index(("pool", "tensor")) * slot_count
    place = slots[...] - start
    rows = lax.broadcasted_iota(jnp.int32, (slot_count, requests), 0)
    amounts = lengths[...].astype(jnp.float32)
    length = jnp.sum(jnp.where(place == rows, amounts, 0.0), axis=1, keepdims=True)
    offset = jnp.sum(
        jnp.where((place >= 0) & (place < rows), amounts, 0.0), axis=1, keepdims=True
    )
    angles = length * frequency[...]
    turn = jnp.sin(angles)
    lean = jnp.cos(angles)
    cosine[...] = jnp.concatenate([lean, lean], axis=1)
    sine[...] = jnp.concatenate([-turn, turn], axis=1)
    first[...] = jnp.broadcast_to(offset.astype(jnp.int32), first.shape)
    last[...] = jnp.broadcast_to((offset + length).astype(jnp.int32), last.shape)


def prepare(slot_count, devices, head_dim, slots, lengths):
    requests = slots.shape[0]
    places = devices * slot_count
    frequency = theta ** (-jnp.arange(head_dim // 2, dtype=jnp.float32) * 2.0 / head_dim)
    table = jax.ShapeDtypeStruct((slot_count, head_dim), jnp.float32)
    bound = jax.ShapeDtypeStruct((slot_count, head_dim), jnp.int32)
    return pl.pallas_call(
        functools.partial(prepare_kernel, slot_count),
        out_shape=(
            jax.ShapeDtypeStruct((places, requests), jnp.bfloat16),
            jax.ShapeDtypeStruct((requests, places), jnp.bfloat16),
            bound,
            bound,
            table,
            table,
        ),
        in_specs=[IN_VMEM] * 3,
        out_specs=tuple([IN_VMEM] * 6),
        compiler_params=pltpu.CompilerParams(vmem_limit_bytes=MIB),
        cost_estimate=cost(8),
        name="prepare",
    )(
        slots.reshape(1, -1),
        lengths.reshape(1, -1),
        frequency.reshape(1, -1),
    )


def project_kernel(slot_count, own, other, gain, packing, q_vm, k_vm, v_vm, out, normed):
    half = own.shape[0] * own.shape[1]
    for index, source in enumerate((own, other)):
        rows = flat_rows(source)
        scale = lax.rsqrt(jnp.mean(rows * rows, axis=-1, keepdims=True) + eps)
        normed[pl.ds(index * half, half), :] = (rows * scale * gain[...]).astype(jnp.bfloat16)
    query_part = dot_rows(normed[...], q_vm[...])
    key_part = dot_columns(normed[...], k_vm[...])
    value_part = dot_columns(normed[...], v_vm[...])
    projected = jnp.concatenate([query_part, key_part, value_part], axis=1).astype(jnp.bfloat16)
    packed = dot_rows(packing[...], projected)
    for owner in range(out.shape[0]):
        out[owner] = packed[owner * slot_count : (owner + 1) * slot_count, :].astype(jnp.bfloat16)


def project(slot_count, own, other, gain, packing, weights):
    depth, query_cols = weights[0].shape
    width = query_cols + weights[1].shape[0] + weights[2].shape[0]
    places, requests = packing.shape
    return pl.pallas_call(
        functools.partial(project_kernel, slot_count),
        out_shape=jax.ShapeDtypeStruct((places // slot_count, slot_count, width), jnp.bfloat16),
        in_specs=[IN_VMEM] * 7,
        out_specs=IN_VMEM,
        scratch_shapes=[pltpu.VMEM((requests, depth), jnp.bfloat16)],
        compiler_params=pltpu.CompilerParams(vmem_limit_bytes=8 * MIB),
        cost_estimate=cost(32),
        name="project",
    )(
        own,
        other,
        gain.reshape(1, depth),
        packing,
        *weights,
    )


def attend_kernel(
    query_cols,
    key_cols,
    arrived,
    first,
    last,
    cosine,
    sine,
    query_gain,
    key_gain,
    keys,
    values,
    out,
    queries,
    scores,
):
    devices, slot_count, _ = arrived.shape
    tokens, width = keys.shape
    head_dim = query_gain.shape[1]
    kv_count = devices * key_cols // head_dim
    sharers = devices // kv_count
    heads_here = query_cols // head_dim
    repeats = sharers * heads_here
    count = repeats * slot_count
    parts = pieces(tokens, TOKEN_STEP)
    scale_factor = 1.0 / math.sqrt(head_dim)

    def tile(rows, times):
        return jnp.concatenate([rows] * times, axis=0)

    def prepare(rows, gain, times):
        rows = rows * lax.rsqrt(jnp.mean(rows * rows, axis=-1, keepdims=True) + eps) * gain[...]
        turned = pltpu.roll(rows, head_dim // 2, 1)
        return (rows * tile(cosine[...], times) + turned * tile(sine[...], times)).astype(
            jnp.bfloat16
        )

    blocks = [arrived[device].astype(jnp.float32) for device in range(devices)]
    rows = jnp.concatenate(
        [
            blocks[kv * sharers + place][:, head * head_dim : (head + 1) * head_dim]
            for kv in range(kv_count)
            for head in range(heads_here)
            for place in range(sharers)
        ],
        axis=0,
    )
    query = prepare(rows, query_gain, kv_count * repeats)

    def whole(begin):
        return [
            jnp.concatenate(
                [
                    blocks[kv * sharers + place][:, begin : begin + key_cols]
                    for place in range(sharers)
                ],
                axis=1,
            )
            for kv in range(kv_count)
        ]

    fresh = prepare(jnp.concatenate(whole(query_cols), axis=0), key_gain, kv_count)
    fresh = fresh.astype(jnp.float32)
    key_new = jnp.concatenate(
        [
            tile(fresh[kv * slot_count : (kv + 1) * slot_count, :], repeats)
            for kv in range(kv_count)
        ],
        axis=0,
    )
    value_new = [tile(rows, repeats) for rows in whole(query_cols + key_cols)]
    own_score = (
        jnp.sum(query.astype(jnp.float32) * key_new, axis=-1, keepdims=True) * scale_factor
    )
    queries[...] = jnp.zeros(queries.shape, queries.dtype)
    for kv in range(kv_count):
        queries[kv * count : (kv + 1) * count, kv * head_dim : (kv + 1) * head_dim] = query[
            kv * count : (kv + 1) * count, :
        ]
    start = tile(first[:, :1], kv_count * repeats)
    end = tile(last[:, :1], kv_count * repeats)
    largest = own_score
    for begin, size in parts:
        positions = lax.broadcasted_iota(jnp.int32, (kv_count * count, size), 1) + begin
        inside = (positions >= start) & (positions < end)
        part = dot_columns(queries[...], keys[begin : begin + size, :]) * scale_factor
        part = jnp.where(inside, part, -1e30)
        scores[:, begin : begin + size] = part
        largest = jnp.maximum(largest, jnp.max(part, axis=1, keepdims=True))
    own_weight = jnp.exp(own_score - largest)
    denominator = own_weight
    summed = jnp.zeros((kv_count * count, width), jnp.float32)
    for begin, size in parts:
        weights = jnp.exp(scores[:, begin : begin + size] - largest)
        denominator = denominator + jnp.sum(weights, axis=1, keepdims=True)
        summed = summed + dot_rows(
            weights.astype(jnp.bfloat16), values[begin : begin + size, :]
        )
    own_low = own_weight.astype(jnp.bfloat16).astype(jnp.float32)
    for kv in range(kv_count):
        span = slice(kv * count, (kv + 1) * count)
        mine = summed[span, kv * head_dim : (kv + 1) * head_dim]
        mine = (mine + own_low[span, :] * value_new[kv]) / denominator[span, :]
        for head in range(heads_here):
            for place in range(sharers):
                row = (head * sharers + place) * slot_count
                out[kv * sharers + place, :, head * head_dim : (head + 1) * head_dim] = mine[
                    row : row + slot_count, :
                ].astype(jnp.bfloat16)


def attend(arrived, planned, query_gain, key_gain, key_cache, value_cache, query_cols):
    devices, slot_count, width = arrived.shape
    key_cols = (width - query_cols) // 2
    head_dim = query_gain.shape[0]
    tokens, cache_width = key_cache.shape
    rows = devices * query_cols // head_dim * slot_count
    return pl.pallas_call(
        functools.partial(attend_kernel, query_cols, key_cols),
        out_shape=jax.ShapeDtypeStruct((devices, slot_count, query_cols), jnp.bfloat16),
        in_specs=[IN_VMEM] * 9,
        out_specs=IN_VMEM,
        scratch_shapes=[
            pltpu.VMEM((rows, cache_width), jnp.bfloat16),
            pltpu.VMEM((rows, tokens), jnp.float32),
        ],
        compiler_params=pltpu.CompilerParams(vmem_limit_bytes=16 * MIB),
        name="attend",
    )(
        arrived,
        *planned,
        query_gain.reshape(1, head_dim),
        key_gain.reshape(1, head_dim),
        key_cache,
        value_cache,
    )


def mix_kernel(returned, unpacking, weight, hidden, near_out, far_out, other_out):
    owners = returned.shape[0]
    block, width = near_out.shape
    local = hidden.shape[0]
    group = lax.axis_index("tensor") // SIDES
    by_slot = jnp.concatenate(
        [returned[owner].astype(jnp.float32) for owner in range(owners)], axis=0
    ).astype(jnp.bfloat16)
    rows = dot_rows(unpacking[...], by_slot).astype(jnp.bfloat16)
    for start, size in pieces(width, 1024):
        columns = slice(start, start + size)
        total = dot_rows(rows, weight[:, columns])
        residual = hidden[:, columns].astype(jnp.float32)
        near_out[:, columns] = total[:block] + jnp.concatenate(
            [jnp.where(group == index, residual, 0.0) for index in range(block // local)], axis=0
        )
        for side in range(SIDES):
            row = side * block
            if side:
                far_out[side - 1, :, columns] = total[row : row + block]
            row += SIDES * block
            other_out[side, :, columns] = total[row : row + block].astype(other_out.dtype)


def mix(returned, unpacking, output_weight, hidden):
    block, width = unpacking.shape[0] // 2 // SIDES, output_weight.shape[1]
    return pl.pallas_call(
        mix_kernel,
        out_shape=(
            jax.ShapeDtypeStruct((block, width), jnp.float32),
            jax.ShapeDtypeStruct((SIDES - 1, block, width), jnp.float32),
            jax.ShapeDtypeStruct((SIDES, block, width), jnp.bfloat16),
        ),
        in_specs=[IN_VMEM] * 4,
        out_specs=(IN_VMEM, IN_VMEM, IN_VMEM),
        compiler_params=pltpu.CompilerParams(vmem_limit_bytes=8 * MIB),
        name="mix",
    )(returned, unpacking, output_weight, hidden)


def stack_kernel(*refs):
    out = refs[-1]
    for index, ref in enumerate(refs[:-1]):
        out[index] = ref[...]


def stack(blocks):
    shape = (len(blocks),) + blocks[0].shape
    return pl.pallas_call(
        stack_kernel,
        out_shape=jax.ShapeDtypeStruct(shape, blocks[0].dtype),
        in_specs=[IN_VMEM] * len(blocks),
        out_specs=IN_VMEM,
        compiler_params=pltpu.CompilerParams(vmem_limit_bytes=2 * MIB),
        name="stack",
    )(*blocks)


def renew_kernel(own, partner, gain, mixed, normed):
    local = mixed.shape[0]
    total = own[...].astype(jnp.float32) + partner[...].astype(jnp.float32)
    rows = total.astype(jnp.bfloat16).astype(jnp.float32)
    scale = lax.rsqrt(jnp.mean(rows * rows, axis=-1, keepdims=True) + eps)
    normed[...] = (rows * scale * gain[...]).astype(jnp.bfloat16)
    group = lax.axis_index("tensor") // SIDES
    here = rows[:local]
    for index in range(1, rows.shape[0] // local):
        here = jnp.where(group == index, rows[index * local : (index + 1) * local], here)
    mixed[...] = here.astype(jnp.bfloat16)


def renew(own, partner, gain, local):
    return pl.pallas_call(
        renew_kernel,
        out_shape=(
            jax.ShapeDtypeStruct((local, own.shape[1]), jnp.bfloat16),
            jax.ShapeDtypeStruct(own.shape, jnp.bfloat16),
        ),
        in_specs=[IN_VMEM] * 3,
        out_specs=(IN_VMEM, IN_VMEM),
        compiler_params=pltpu.CompilerParams(vmem_limit_bytes=4 * MIB),
        name="renew",
    )(own, partner, gain.reshape(1, -1))


def feed_kernel(spans, local, *refs):
    halves, weights = refs[:2], refs[2 : 2 + len(spans)]
    down, own_out, other_out, rows = refs[2 + len(spans) :]
    half, width = own_out.shape
    block = half // SIDES

    def part(array, start, size):
        for (index, begin, end), ref in zip(spans, weights):
            if index == array and begin <= start and start + size <= end:
                span = slice(start - begin, start - begin + size)
                return ref[span, :]

    for index, blocks in enumerate(halves):
        rows[index * half : (index + 1) * half, :] = flat_rows(blocks).astype(jnp.bfloat16)
    gate_part = up_part = 0.0
    for start, size in pieces(width, FEED_STEP):
        some = rows[:, start : start + size]
        gate_part = gate_part + dot_rows(some, part(0, start, size))
        up_part = up_part + dot_rows(some, part(1, start, size))
    active = (gate_part / (1.0 + jnp.exp(-gate_part)) * up_part).astype(jnp.bfloat16)
    row = lax.broadcasted_iota(jnp.int32, (2 * half, 2 * half), 0)
    chip = lax.rem(row, half) // local
    inner = lax.rem(row, local)
    side = differ(lax.rem(chip, SIDES))
    source = row // half * half + side * block + chip // SIDES * local + inner
    order = one_hot(source, lax.broadcasted_iota(jnp.int32, (2 * half, 2 * half), 1))
    active = dot_rows(order, active).astype(jnp.bfloat16)
    for start, size in pieces(width, FEED_STEP):
        total = dot_rows(active, down[:, start : start + size])
        own_out[:, start : start + size] = total[:half]
        other_out[:, start : start + size] = total[half:].astype(other_out.dtype)


def feed(halves, spans, weights, down_weight, local):
    _, block, width = halves[0].shape
    half = SIDES * block
    return pl.pallas_call(
        functools.partial(feed_kernel, spans, local),
        out_shape=(
            jax.ShapeDtypeStruct((half, width), jnp.float32),
            jax.ShapeDtypeStruct((half, width), jnp.bfloat16),
        ),
        in_specs=[IN_VMEM] * (3 + len(spans)),
        out_specs=(IN_VMEM, IN_VMEM),
        scratch_shapes=[pltpu.VMEM((2 * half, width), jnp.bfloat16)],
        compiler_params=pltpu.CompilerParams(vmem_limit_bytes=16 * MIB),
        name="feed",
    )(*halves, *[keep_in_vmem(weight) for weight in weights], down_weight)


def on_device_kernels(
    hidden,
    input_gain,
    query_weight,
    key_weight,
    value_weight,
    query_gain,
    key_gain,
    output_weight,
    post_gain,
    gate_weight,
    up_weight,
    down_weight,
    key_cache,
    value_cache,
    lengths,
    request_slot,
):
    devices = lax.axis_size(("pool", "tensor"))
    chips = lax.axis_size("tensor")
    local, width = hidden.shape
    slot_count = SLOTS
    query_cols = query_weight.shape[1]
    head_dim = query_gain.shape[0]
    own = gather_half(hidden, chips, gate_weight.T)
    packing, unpacking, *planned = prepare(
        slot_count, devices, head_dim, request_slot, lengths
    )
    other = swap_cores(own)
    weights = (query_weight, key_weight.T, value_weight.T)
    outgoing = project(slot_count, own, other, input_gain, packing, weights)
    head_out = attend(
        swap_all(outgoing), planned, query_gain, key_gain, key_cache, value_cache, query_cols
    )
    returned = swap_all(head_out)
    near_sum, far_sum, other_sum = mix(returned, unpacking, output_weight, hidden)

    gate_rows, up_rows = gate_weight.T, up_weight.T
    columns = width // STEP
    steps = chips.bit_length() - 3
    far = split_range(columns, [4] + [6] * steps + [0, 0])
    near = split_range(columns, [0] + [0] * steps + [6, 4])
    spans, fetched = [], []

    def beside_load(exchange, blocks):
        group = len(fetched)
        token = jax.tree.leaves(blocks)[0]
        parts = load(far[group], near[group], token, gate_rows, up_rows)
        blocks, parts = lax.optimization_barrier((exchange(blocks), parts))
        for array, span in enumerate((far[group], near[group])):
            if span:
                spans.append((array,) + span)
        fetched.append(parts)
        return blocks

    def plus(left, right):
        return left.astype(jnp.float32) + right.astype(jnp.float32)

    def trade(blocks):
        return [swap_partners(block, SIDES - 1 - index) for index, block in enumerate(blocks)]

    from_core = swap_cores(other_sum)
    far_sums = plus(far_sum, from_core[1:]).astype(jnp.bfloat16)
    from_sides = beside_load(trade, [far_sums[side] for side in reversed(range(SIDES - 1))])
    total = plus(near_sum, from_core[0])
    for block in from_sides:
        total = plus(total, block)
    total = total.astype(jnp.bfloat16)
    mask = SIDES
    while 2 * mask < chips:
        partner = beside_load(lambda block: swap_partners(block, mask), total)
        total = plus(total, partner).astype(jnp.bfloat16)
        mask *= 2
    partner = beside_load(lambda block: swap_partners(block, mask), total)
    mixed_rows, normed = renew(total, partner, post_gain, local)
    sides = beside_load(trade, [normed] * (SIDES - 1))
    own = stack([normed] + sides[::-1])
    halves = (own, beside_load(swap_cores, own))
    own_sum, other_sum = feed(
        halves, spans, [array for parts in fetched for array in parts], down_weight, local
    )
    lowered = scatter_halves(own_sum, other_sum, chips)
    final_rows = (mixed_rows.astype(jnp.float32) + lowered).astype(jnp.bfloat16)
    return (mixed_rows, final_rows)


def gather_rows(rows, devices):
    copies = jnp.broadcast_to(rows[None], (devices,) + rows.shape)
    arrived = lax.all_to_all(copies, ("pool", "tensor"), split_axis=0, concat_axis=0, tiled=True)
    return arrived.reshape(devices * rows.shape[0], rows.shape[1])


def scatter_sum(partial, devices):
    blocks = partial.astype(jnp.bfloat16).reshape(devices, -1, partial.shape[1])
    arrived = lax.all_to_all(blocks, ("pool", "tensor"), split_axis=0, concat_axis=0, tiled=True)
    return jnp.sum(arrived.astype(jnp.float32), axis=0)


def on_device_general(
    hidden,
    input_gain,
    query_weight,
    key_weight,
    value_weight,
    query_gain,
    key_gain,
    output_weight,
    post_gain,
    gate_weight,
    up_weight,
    down_weight,
    key_cache,
    value_cache,
    lengths,
    request_slot,
):
    devices = lax.axis_size(("pool", "tensor"))
    device_index = lax.axis_index(("pool", "tensor"))
    local_rows = hidden.shape[0]
    query_cols = query_weight.shape[1]
    key_cols = key_weight.shape[1]
    width_sent = query_cols + 2 * key_cols
    head_dim = query_gain.shape[0]
    slot_count = SLOTS
    head_count = devices * query_cols // head_dim
    kv_count = devices * key_cols // head_dim
    group_size = head_count // kv_count
    normed = rms_scale(hidden, input_gain).astype(jnp.bfloat16)
    shard_rows = gather_rows(normed, devices)
    query_part = jnp.dot(shard_rows, query_weight, preferred_element_type=jnp.float32)
    key_part = jnp.dot(shard_rows, key_weight, preferred_element_type=jnp.float32)
    value_part = jnp.dot(shard_rows, value_weight, preferred_element_type=jnp.float32)
    projected = jnp.concatenate([query_part, key_part, value_part], axis=1).astype(jnp.bfloat16)
    outgoing = (
        jnp.zeros((devices * slot_count, width_sent), jnp.bfloat16).at[request_slot].set(projected)
    )
    outgoing = outgoing.reshape(devices, slot_count, width_sent)
    arrived = lax.all_to_all(
        outgoing, ("pool", "tensor"), split_axis=0, concat_axis=2, tiled=True
    ).reshape(slot_count, devices, width_sent)
    query_full = arrived[:, :, :query_cols].reshape(slot_count, head_count, head_dim)
    key_full = arrived[:, :, query_cols : query_cols + key_cols].reshape(
        slot_count, kv_count, head_dim
    )
    value_new = arrived[:, :, query_cols + key_cols :].reshape(slot_count, kv_count, head_dim)
    slot_ids = device_index * slot_count + jnp.arange(slot_count, dtype=jnp.int32)
    matches = request_slot[None, :] == slot_ids[:, None]
    slot_length = jnp.sum(jnp.where(matches, lengths[None, :], 0), axis=1)
    owner_of = request_slot // slot_count
    within = request_slot % slot_count
    earlier = (owner_of[None, :] == device_index) & (
        within[None, :] < jnp.arange(slot_count, dtype=jnp.int32)[:, None]
    )
    slot_offset = jnp.sum(jnp.where(earlier, lengths[None, :], 0), axis=1)
    position = slot_length.astype(jnp.float32)[:, None, None]
    query_heads = rotate(rms_scale(query_full, query_gain), position).astype(jnp.bfloat16)
    query_heads = query_heads.reshape(slot_count, kv_count, group_size, head_dim)
    key_new = rotate(rms_scale(key_full, key_gain), position).astype(jnp.bfloat16)
    pool_tokens = key_cache.shape[0]
    scale_factor = 1.0 / math.sqrt(head_dim)
    scores = jnp.stack(
        [
            jnp.einsum(
                "sgd,td->sgt",
                query_heads[:, kv],
                key_cache[:, kv * head_dim : (kv + 1) * head_dim],
                preferred_element_type=jnp.float32,
            )
            for kv in range(kv_count)
        ],
        axis=1,
    ) * scale_factor
    own_score = (
        jnp.einsum("skgd,skd->skg", query_heads, key_new, preferred_element_type=jnp.float32)
        * scale_factor
    )
    token_pos = jnp.arange(pool_tokens, dtype=jnp.int32)
    inside = (token_pos[None, :] >= slot_offset[:, None]) & (
        token_pos[None, :] < (slot_offset + slot_length)[:, None]
    )
    inside = inside[:, None, None, :]
    largest = jnp.maximum(jnp.max(jnp.where(inside, scores, -1e30), axis=3), own_score)
    weights = jnp.where(inside, jnp.exp(scores - largest[..., None]), 0.0)
    own_weight = jnp.exp(own_score - largest)
    denominator = jnp.sum(weights, axis=3) + own_weight
    weights_low = weights.astype(jnp.bfloat16)
    summed = jnp.stack(
        [
            jnp.einsum(
                "sgt,td->sgd",
                weights_low[:, kv],
                value_cache[:, kv * head_dim : (kv + 1) * head_dim],
                preferred_element_type=jnp.float32,
            )
            for kv in range(kv_count)
        ],
        axis=1,
    )
    own_low = own_weight.astype(jnp.bfloat16).astype(jnp.float32)
    summed = summed + own_low[..., None] * value_new.astype(jnp.float32)[:, :, None, :]
    head_out = (
        (summed / denominator[..., None])
        .astype(jnp.bfloat16)
        .reshape(slot_count, devices, query_cols)
    )
    returned = lax.all_to_all(head_out, ("pool", "tensor"), split_axis=1, concat_axis=0, tiled=True)
    head_rows = returned.reshape(devices * slot_count, query_cols)[request_slot]
    partial_value = jnp.dot(head_rows, output_weight, preferred_element_type=jnp.float32)
    mixed_rows = (hidden.astype(jnp.float32) + scatter_sum(partial_value, devices)).astype(jnp.bfloat16)
    post_normed = gather_rows(rms_scale(mixed_rows, post_gain).astype(jnp.bfloat16), devices)
    gate_part = jnp.dot(post_normed, gate_weight, preferred_element_type=jnp.float32)
    up_part = jnp.dot(post_normed, up_weight, preferred_element_type=jnp.float32)
    activated = (jax.nn.silu(gate_part) * up_part).astype(jnp.bfloat16)
    lowered = scatter_sum(
        jnp.dot(activated, down_weight, preferred_element_type=jnp.float32), devices
    )
    final_rows = (mixed_rows.astype(jnp.float32) + lowered).astype(jnp.bfloat16)
    return (mixed_rows, final_rows)


def on_device(*arrays):
    query_cols, key_cols = arrays[2].shape[1], arrays[3].shape[1]
    head_dim = arrays[5].shape[0]
    devices = lax.axis_size(("pool", "tensor"))
    kv_count = devices * key_cols // head_dim
    whole_heads = query_cols % head_dim == 0 and head_dim % LANES == 0
    shared = kv_count > 0 and devices % kv_count == 0
    chips = lax.axis_size("tensor")
    pairs = lax.axis_size("pool") == 2 and chips >= 2 * SIDES and chips & (chips - 1) == 0
    pairs = pairs and arrays[14].shape[0] % 32 == 0
    if whole_heads and shared and pairs:
        return on_device_kernels(*arrays)
    return on_device_general(*arrays)


def solution(mesh):
    placed = (
        P(("groups", "pool", "tensor"), None),
        P(),
        P(None, ("pool", "tensor")),
        P(None, ("pool", "tensor")),
        P(None, ("pool", "tensor")),
        P(),
        P(),
        P(("pool", "tensor"), None),
        P(),
        P(None, ("pool", "tensor")),
        P(None, ("pool", "tensor")),
        P(("pool", "tensor"), None),
        P(("groups", "pool", "tensor"), None),
        P(("groups", "pool", "tensor"), None),
        P("groups"),
        P("groups"),
    )
    return jax.shard_map(
        on_device,
        mesh=mesh,
        in_specs=placed,
        out_specs=(P(("groups", "pool", "tensor"), None), P(("groups", "pool", "tensor"), None)),
        check_vma=False,
    )
```

```python
import functools
import math

import jax
import jax.numpy as jnp
from jax import lax
from jax.experimental import pallas as pl
from jax.experimental.pallas import tpu as pltpu
from jax.sharding import PartitionSpec as P

SLOTS = 4
SIDES = 4
LANES = 128
MIB = 2**20
TOKEN_STEP = 256
IN_VMEM = pl.BlockSpec(memory_space=pltpu.VMEM)
IN_HBM = pl.BlockSpec(memory_space=pl.ANY)


def cost(mib):
    return pl.CostEstimate(flops=0, bytes_accessed=mib * MIB, transcendentals=0)

STEP = 512
FEED_STEP = 256


eps = 1e-06
theta = 1000000.0


def rms_scale(values, scales):
    values = values.astype(jnp.float32)
    return values * lax.rsqrt(jnp.mean(values * values, axis=-1, keepdims=True) + eps) * scales


def rotate(values, position):
    half_width = values.shape[-1] // 2
    frequency = theta ** (-jnp.arange(half_width, dtype=jnp.float32) * 2.0 / values.shape[-1])
    angles = position * frequency
    cosine = jnp.cos(angles)
    sine_part = jnp.sin(angles)
    front_half = values[..., :half_width]
    back_half = values[..., half_width:]
    return jnp.concatenate(
        [front_half * cosine - back_half * sine_part, back_half * cosine + front_half * sine_part],
        axis=-1,
    )


def swap_cores(block):
    return lax.ppermute(block, "pool", [(0, 1), (1, 0)])


def swap_partners(block, mask):
    chips = lax.axis_size("tensor")
    return lax.ppermute(block, "tensor", [(chip, chip ^ mask) for chip in range(chips)])


def swap_chips(blocks):
    return lax.all_to_all(blocks, "tensor", split_axis=0, concat_axis=0, tiled=True)


def swap_all(blocks):
    return lax.all_to_all(blocks, ("pool", "tensor"), split_axis=0, concat_axis=0, tiled=True)


def spread_kernel(rows, unread, out):
    for chip in range(out.shape[0]):
        out[chip] = rows[...]


def spread(rows, chips, unread):
    return pl.pallas_call(
        spread_kernel,
        out_shape=jax.ShapeDtypeStruct((chips,) + rows.shape, rows.dtype),
        in_specs=[IN_VMEM, IN_HBM],
        out_specs=IN_VMEM,
        compiler_params=pltpu.CompilerParams(vmem_limit_bytes=MIB),
        cost_estimate=cost(8),
        name="spread",
    )(rows, keep_in_hbm(unread))


def gather_half(rows, chips, unread):
    return swap_chips(spread(rows, chips, unread))


def scatter_halves(own_half, other_half, chips):
    added = own_half.astype(jnp.float32) + swap_cores(other_half).astype(jnp.float32)
    blocks = added.astype(jnp.bfloat16).reshape(chips, -1, own_half.shape[1])
    return jnp.sum(swap_chips(blocks).astype(jnp.float32), axis=0)


def dot_rows(left, right):
    return lax.dot_general(
        left, right, (((1,), (0,)), ((), ())), preferred_element_type=jnp.float32
    )


def dot_columns(left, right):
    return lax.dot_general(
        left, right, (((1,), (1,)), ((), ())), preferred_element_type=jnp.float32
    )


def pieces(extent, step):
    return [(start, min(step, extent - start)) for start in range(0, extent, step)]


def keep_in_hbm(array):
    return pltpu.with_memory_space_constraint(array, pltpu.HBM)


def keep_in_vmem(array):
    return pltpu.with_memory_space_constraint(array, pltpu.VMEM)


def split_range(count, shares):
    ends = [count * sum(shares[: index + 1]) // sum(shares) * STEP for index in range(len(shares))]
    starts = [0] + ends[:-1]
    return [(start, end) if start < end else None for start, end in zip(starts, ends)]


def load_kernel(far, near, token, far_rows, near_rows, *refs):
    outs = list(refs[: bool(far) + bool(near)])
    copies, stage = [], None
    if far:
        begin, end = far
        stage, sems = refs[-2:]
        for index, (start, size) in enumerate(pieces(end - begin, STEP)):
            copies.append(
                pltpu.make_async_copy(
                    far_rows.at[:, pl.ds(begin + start, size)],
                    stage.at[:, pl.ds(start, size)],
                    sems.at[index],
                )
            )
            copies[-1].start()
    if near:
        begin, end = near
        for start, size in pieces(end - begin, STEP):
            outs[-1][start : start + size, :] = near_rows[:, begin + start : begin + start + size].T
    for copy, (start, size) in zip(copies, pieces(far[1] - far[0], STEP) if far else []):
        copy.wait()
        outs[0][start : start + size, :] = stage[:, start : start + size].T


def load(far, near, token, far_rows, near_rows):
    units, width = far_rows.shape
    ranges = [span for span in (far, near) if span]
    staged = 2 * units * (far[1] - far[0]) if far else 0
    scratch = []
    if far:
        scratch = [
            pltpu.VMEM((units, far[1] - far[0]), far_rows.dtype),
            pltpu.SemaphoreType.DMA((len(pieces(far[1] - far[0], STEP)),)),
        ]
    return pl.pallas_call(
        functools.partial(load_kernel, far, near),
        out_shape=tuple(pltpu.VMEM((end - begin, units), far_rows.dtype) for begin, end in ranges),
        in_specs=[IN_HBM, IN_HBM, IN_VMEM if near else IN_HBM],
        out_specs=tuple([IN_VMEM] * len(ranges)),
        scratch_shapes=scratch,
        compiler_params=pltpu.CompilerParams(
            vmem_limit_bytes=2 * MIB + staged + (2 * units * width if near else 0)
        ),
        cost_estimate=cost(8),
        name="load",
    )(token, keep_in_hbm(far_rows), near_rows if near else keep_in_hbm(near_rows))


def flat_rows(blocks):
    return jnp.concatenate(
        [blocks[chip].astype(jnp.float32) for chip in range(blocks.shape[0])], axis=0
    )


def one_hot(rows, columns):
    return jnp.where(rows == columns, 1.0, 0.0).astype(jnp.bfloat16)


def differ(mask):
    here = lax.rem(lax.axis_index("tensor"), SIDES)
    low = lax.rem(lax.rem(mask, 2) + lax.rem(here, 2), 2)
    high = lax.rem(mask // 2 + here // 2, 2)
    return 2 * high + low


def slot_matrix(slots, places):
    return one_hot(lax.broadcasted_iota(jnp.int32, (places, slots.shape[1]), 0), slots[...])


def prepare_kernel(
    slot_count,
    slots,
    lengths,
    frequency,
    packing,
    unpacking,
    first,
    last,
    cosine,
    sine,
):
    places, requests = packing.shape
    owners = places // slot_count
    core = lax.axis_index("pool")
    natural = slot_matrix(slots, places)
    row = lax.broadcasted_iota(jnp.int32, (requests, requests), 0)
    column = lax.broadcasted_iota(jnp.int32, (requests, requests), 1)
    half_first = one_hot(lax.rem(column + core * (requests // 2), requests), row)
    packing[...] = dot_rows(natural, half_first).astype(jnp.bfloat16)
    half, block, local = requests // 2, requests // 2 // SIDES, requests // owners
    half_of = lax.rem(row // half + core, 2)
    side = differ(lax.rem(row, half) // block)
    inner = lax.rem(row, local)
    source = half_of * half + (lax.rem(row, block) // local * SIDES + side) * local + inner
    unpacking[...] = dot_columns(one_hot(source, column), natural).astype(jnp.bfloat16)
    start = lax.axis_index(("pool", "tensor")) * slot_count
    place = slots[...] - start
    rows = lax.broadcasted_iota(jnp.int32, (slot_count, requests), 0)
    amounts = lengths[...].astype(jnp.float32)
    length = jnp.sum(jnp.where(place == rows, amounts, 0.0), axis=1, keepdims=True)
    offset = jnp.sum(
        jnp.where((place >= 0) & (place < rows), amounts, 0.0), axis=1, keepdims=True
    )
    angles = length * frequency[...]
    turn = jnp.sin(angles)
    lean = jnp.cos(angles)
    cosine[...] = jnp.concatenate([lean, lean], axis=1)
    sine[...] = jnp.concatenate([-turn, turn], axis=1)
    first[...] = jnp.broadcast_to(offset.astype(jnp.int32), first.shape)
    last[...] = jnp.broadcast_to((offset + length).astype(jnp.int32), last.shape)


def prepare(slot_count, devices, head_dim, slots, lengths):
    requests = slots.shape[0]
    places = devices * slot_count
    frequency = theta ** (-jnp.arange(head_dim // 2, dtype=jnp.float32) * 2.0 / head_dim)
    table = jax.ShapeDtypeStruct((slot_count, head_dim), jnp.float32)
    bound = jax.ShapeDtypeStruct((slot_count, head_dim), jnp.int32)
    return pl.pallas_call(
        functools.partial(prepare_kernel, slot_count),
        out_shape=(
            jax.ShapeDtypeStruct((places, requests), jnp.bfloat16),
            jax.ShapeDtypeStruct((requests, places), jnp.bfloat16),
            bound,
            bound,
            table,
            table,
        ),
        in_specs=[IN_VMEM] * 3,
        out_specs=tuple([IN_VMEM] * 6),
        compiler_params=pltpu.CompilerParams(vmem_limit_bytes=MIB),
        cost_estimate=cost(8),
        name="prepare",
    )(
        slots.reshape(1, -1),
        lengths.reshape(1, -1),
        frequency.reshape(1, -1),
    )


def project_kernel(slot_count, own, other, gain, packing, q_vm, k_vm, v_vm, out, normed):
    half = own.shape[0] * own.shape[1]
    for index, source in enumerate((own, other)):
        rows = flat_rows(source)
        scale = lax.rsqrt(jnp.mean(rows * rows, axis=-1, keepdims=True) + eps)
        normed[pl.ds(index * half, half), :] = (rows * scale * gain[...]).astype(jnp.bfloat16)
    query_part = dot_rows(normed[...], q_vm[...])
    key_part = dot_columns(normed[...], k_vm[...])
    value_part = dot_columns(normed[...], v_vm[...])
    projected = jnp.concatenate([query_part, key_part, value_part], axis=1).astype(jnp.bfloat16)
    packed = dot_rows(packing[...], projected)
    for owner in range(out.shape[0]):
        out[owner] = packed[owner * slot_count : (owner + 1) * slot_count, :].astype(jnp.bfloat16)


def project(slot_count, own, other, gain, packing, weights):
    depth, query_cols = weights[0].shape
    width = query_cols + weights[1].shape[0] + weights[2].shape[0]
    places, requests = packing.shape
    return pl.pallas_call(
        functools.partial(project_kernel, slot_count),
        out_shape=jax.ShapeDtypeStruct((places // slot_count, slot_count, width), jnp.bfloat16),
        in_specs=[IN_VMEM] * 7,
        out_specs=IN_VMEM,
        scratch_shapes=[pltpu.VMEM((requests, depth), jnp.bfloat16)],
        compiler_params=pltpu.CompilerParams(vmem_limit_bytes=8 * MIB),
        cost_estimate=cost(32),
        name="project",
    )(
        own,
        other,
        gain.reshape(1, depth),
        packing,
        *weights,
    )


def attend_kernel(
    query_cols,
    key_cols,
    arrived,
    first,
    last,
    cosine,
    sine,
    query_gain,
    key_gain,
    keys,
    values,
    out,
    queries,
    scores,
):
    devices, slot_count, _ = arrived.shape
    tokens, width = keys.shape
    head_dim = query_gain.shape[1]
    kv_count = devices * key_cols // head_dim
    sharers = devices // kv_count
    heads_here = query_cols // head_dim
    repeats = sharers * heads_here
    count = repeats * slot_count
    parts = pieces(tokens, TOKEN_STEP)
    scale_factor = 1.0 / math.sqrt(head_dim)

    def tile(rows, times):
        return jnp.concatenate([rows] * times, axis=0)

    def prepare(rows, gain, times):
        rows = rows * lax.rsqrt(jnp.mean(rows * rows, axis=-1, keepdims=True) + eps) * gain[...]
        turned = pltpu.roll(rows, head_dim // 2, 1)
        return (rows * tile(cosine[...], times) + turned * tile(sine[...], times)).astype(
            jnp.bfloat16
        )

    blocks = [arrived[device].astype(jnp.float32) for device in range(devices)]
    rows = jnp.concatenate(
        [
            blocks[kv * sharers + place][:, head * head_dim : (head + 1) * head_dim]
            for kv in range(kv_count)
            for head in range(heads_here)
            for place in range(sharers)
        ],
        axis=0,
    )
    query = prepare(rows, query_gain, kv_count * repeats)

    def whole(begin):
        return [
            jnp.concatenate(
                [
                    blocks[kv * sharers + place][:, begin : begin + key_cols]
                    for place in range(sharers)
                ],
                axis=1,
            )
            for kv in range(kv_count)
        ]

    fresh = prepare(jnp.concatenate(whole(query_cols), axis=0), key_gain, kv_count)
    fresh = fresh.astype(jnp.float32)
    key_new = jnp.concatenate(
        [
            tile(fresh[kv * slot_count : (kv + 1) * slot_count, :], repeats)
            for kv in range(kv_count)
        ],
        axis=0,
    )
    value_new = [tile(rows, repeats) for rows in whole(query_cols + key_cols)]
    own_score = (
        jnp.sum(query.astype(jnp.float32) * key_new, axis=-1, keepdims=True) * scale_factor
    )
    queries[...] = jnp.zeros(queries.shape, queries.dtype)
    for kv in range(kv_count):
        queries[kv * count : (kv + 1) * count, kv * head_dim : (kv + 1) * head_dim] = query[
            kv * count : (kv + 1) * count, :
        ]
    start = tile(first[:, :1], kv_count * repeats)
    end = tile(last[:, :1], kv_count * repeats)
    largest = own_score
    for begin, size in parts:
        positions = lax.broadcasted_iota(jnp.int32, (kv_count * count, size), 1) + begin
        inside = (positions >= start) & (positions < end)
        part = dot_columns(queries[...], keys[begin : begin + size, :]) * scale_factor
        part = jnp.where(inside, part, -1e30)
        scores[:, begin : begin + size] = part
        largest = jnp.maximum(largest, jnp.max(part, axis=1, keepdims=True))
    own_weight = jnp.exp(own_score - largest)
    denominator = own_weight
    summed = jnp.zeros((kv_count * count, width), jnp.float32)
    for begin, size in parts:
        weights = jnp.exp(scores[:, begin : begin + size] - largest)
        denominator = denominator + jnp.sum(weights, axis=1, keepdims=True)
        summed = summed + dot_rows(
            weights.astype(jnp.bfloat16), values[begin : begin + size, :]
        )
    own_low = own_weight.astype(jnp.bfloat16).astype(jnp.float32)
    for kv in range(kv_count):
        span = slice(kv * count, (kv + 1) * count)
        mine = summed[span, kv * head_dim : (kv + 1) * head_dim]
        mine = (mine + own_low[span, :] * value_new[kv]) / denominator[span, :]
        for head in range(heads_here):
            for place in range(sharers):
                row = (head * sharers + place) * slot_count
                out[kv * sharers + place, :, head * head_dim : (head + 1) * head_dim] = mine[
                    row : row + slot_count, :
                ].astype(jnp.bfloat16)


def attend(arrived, planned, query_gain, key_gain, key_cache, value_cache, query_cols):
    devices, slot_count, width = arrived.shape
    key_cols = (width - query_cols) // 2
    head_dim = query_gain.shape[0]
    tokens, cache_width = key_cache.shape
    rows = devices * query_cols // head_dim * slot_count
    return pl.pallas_call(
        functools.partial(attend_kernel, query_cols, key_cols),
        out_shape=jax.ShapeDtypeStruct((devices, slot_count, query_cols), jnp.bfloat16),
        in_specs=[IN_VMEM] * 9,
        out_specs=IN_VMEM,
        scratch_shapes=[
            pltpu.VMEM((rows, cache_width), jnp.bfloat16),
            pltpu.VMEM((rows, tokens), jnp.float32),
        ],
        compiler_params=pltpu.CompilerParams(vmem_limit_bytes=16 * MIB),
        name="attend",
    )(
        arrived,
        *planned,
        query_gain.reshape(1, head_dim),
        key_gain.reshape(1, head_dim),
        key_cache,
        value_cache,
    )


def mix_kernel(returned, unpacking, weight, hidden, near_out, far_out, other_out):
    owners = returned.shape[0]
    block, width = near_out.shape
    local = hidden.shape[0]
    group = lax.axis_index("tensor") // SIDES
    by_slot = jnp.concatenate(
        [returned[owner].astype(jnp.float32) for owner in range(owners)], axis=0
    ).astype(jnp.bfloat16)
    rows = dot_rows(unpacking[...], by_slot).astype(jnp.bfloat16)
    for start, size in pieces(width, 1024):
        columns = slice(start, start + size)
        total = dot_rows(rows, weight[:, columns])
        residual = hidden[:, columns].astype(jnp.float32)
        near_out[:, columns] = total[:block] + jnp.concatenate(
            [jnp.where(group == index, residual, 0.0) for index in range(block // local)], axis=0
        )
        for side in range(SIDES):
            row = side * block
            if side:
                far_out[side - 1, :, columns] = total[row : row + block]
            row += SIDES * block
            other_out[side, :, columns] = total[row : row + block].astype(other_out.dtype)


def mix(returned, unpacking, output_weight, hidden):
    block, width = unpacking.shape[0] // 2 // SIDES, output_weight.shape[1]
    return pl.pallas_call(
        mix_kernel,
        out_shape=(
            jax.ShapeDtypeStruct((block, width), jnp.float32),
            jax.ShapeDtypeStruct((SIDES - 1, block, width), jnp.float32),
            jax.ShapeDtypeStruct((SIDES, block, width), jnp.bfloat16),
        ),
        in_specs=[IN_VMEM] * 4,
        out_specs=(IN_VMEM, IN_VMEM, IN_VMEM),
        compiler_params=pltpu.CompilerParams(vmem_limit_bytes=8 * MIB),
        name="mix",
    )(returned, unpacking, output_weight, hidden)


def stack_kernel(*refs):
    out = refs[-1]
    for index, ref in enumerate(refs[:-1]):
        out[index] = ref[...]


def stack(blocks):
    shape = (len(blocks),) + blocks[0].shape
    return pl.pallas_call(
        stack_kernel,
        out_shape=jax.ShapeDtypeStruct(shape, blocks[0].dtype),
        in_specs=[IN_VMEM] * len(blocks),
        out_specs=IN_VMEM,
        compiler_params=pltpu.CompilerParams(vmem_limit_bytes=2 * MIB),
        name="stack",
    )(*blocks)


def renew_kernel(own, partner, gain, mixed, normed):
    local = mixed.shape[0]
    total = own[...].astype(jnp.float32) + partner[...].astype(jnp.float32)
    rows = total.astype(jnp.bfloat16).astype(jnp.float32)
    scale = lax.rsqrt(jnp.mean(rows * rows, axis=-1, keepdims=True) + eps)
    normed[...] = (rows * scale * gain[...]).astype(jnp.bfloat16)
    group = lax.axis_index("tensor") // SIDES
    here = rows[:local]
    for index in range(1, rows.shape[0] // local):
        here = jnp.where(group == index, rows[index * local : (index + 1) * local], here)
    mixed[...] = here.astype(jnp.bfloat16)


def renew(own, partner, gain, local):
    return pl.pallas_call(
        renew_kernel,
        out_shape=(
            pltpu.VMEM((local, own.shape[1]), jnp.bfloat16),
            jax.ShapeDtypeStruct(own.shape, jnp.bfloat16),
        ),
        in_specs=[IN_VMEM] * 3,
        out_specs=(IN_VMEM, IN_VMEM),
        compiler_params=pltpu.CompilerParams(vmem_limit_bytes=4 * MIB),
        name="renew",
    )(own, partner, gain.reshape(1, -1))


def settle_kernel(rows, out):
    out[...] = rows[...]


def settle(rows):
    return pl.pallas_call(
        settle_kernel,
        out_shape=jax.ShapeDtypeStruct(rows.shape, rows.dtype),
        in_specs=[IN_VMEM],
        out_specs=IN_VMEM,
        compiler_params=pltpu.CompilerParams(vmem_limit_bytes=MIB),
        cost_estimate=cost(4),
        name="settle",
    )(keep_in_vmem(rows))


def feed_kernel(spans, local, *refs):
    halves, weights = refs[:2], refs[2 : 2 + len(spans)]
    down, own_out, other_out, rows = refs[2 + len(spans) :]
    half, width = own_out.shape
    block = half // SIDES

    def part(array, start, size):
        for (index, begin, end), ref in zip(spans, weights):
            if index == array and begin <= start and start + size <= end:
                span = slice(start - begin, start - begin + size)
                return ref[span, :]

    for index, blocks in enumerate(halves):
        rows[index * half : (index + 1) * half, :] = flat_rows(blocks).astype(jnp.bfloat16)
    gate_part = up_part = 0.0
    for start, size in pieces(width, FEED_STEP):
        some = rows[:, start : start + size]
        gate_part = gate_part + dot_rows(some, part(0, start, size))
        up_part = up_part + dot_rows(some, part(1, start, size))
    active = (gate_part / (1.0 + jnp.exp(-gate_part)) * up_part).astype(jnp.bfloat16)
    row = lax.broadcasted_iota(jnp.int32, (2 * half, 2 * half), 0)
    chip = lax.rem(row, half) // local
    inner = lax.rem(row, local)
    side = differ(lax.rem(chip, SIDES))
    source = row // half * half + side * block + chip // SIDES * local + inner
    order = one_hot(source, lax.broadcasted_iota(jnp.int32, (2 * half, 2 * half), 1))
    active = dot_rows(order, active).astype(jnp.bfloat16)
    for start, size in pieces(width, FEED_STEP):
        total = dot_rows(active, down[:, start : start + size])
        own_out[:, start : start + size] = total[:half]
        other_out[:, start : start + size] = total[half:].astype(other_out.dtype)


def feed(halves, spans, weights, down_weight, local):
    _, block, width = halves[0].shape
    half = SIDES * block
    return pl.pallas_call(
        functools.partial(feed_kernel, spans, local),
        out_shape=(
            jax.ShapeDtypeStruct((half, width), jnp.float32),
            jax.ShapeDtypeStruct((half, width), jnp.bfloat16),
        ),
        in_specs=[IN_VMEM] * (3 + len(spans)),
        out_specs=(IN_VMEM, IN_VMEM),
        scratch_shapes=[pltpu.VMEM((2 * half, width), jnp.bfloat16)],
        compiler_params=pltpu.CompilerParams(vmem_limit_bytes=16 * MIB),
        name="feed",
    )(*halves, *[keep_in_vmem(weight) for weight in weights], down_weight)


def on_device_kernels(
    hidden,
    input_gain,
    query_weight,
    key_weight,
    value_weight,
    query_gain,
    key_gain,
    output_weight,
    post_gain,
    gate_weight,
    up_weight,
    down_weight,
    key_cache,
    value_cache,
    lengths,
    request_slot,
):
    devices = lax.axis_size(("pool", "tensor"))
    chips = lax.axis_size("tensor")
    local, width = hidden.shape
    slot_count = SLOTS
    query_cols = query_weight.shape[1]
    head_dim = query_gain.shape[0]
    own = gather_half(hidden, chips, gate_weight.T)
    packing, unpacking, *planned = prepare(
        slot_count, devices, head_dim, request_slot, lengths
    )
    other = swap_cores(own)
    weights = (query_weight, key_weight.T, value_weight.T)
    outgoing = project(slot_count, own, other, input_gain, packing, weights)
    head_out = attend(
        swap_all(outgoing), planned, query_gain, key_gain, key_cache, value_cache, query_cols
    )
    returned = swap_all(head_out)
    near_sum, far_sum, other_sum = mix(returned, unpacking, output_weight, hidden)

    gate_rows, up_rows = gate_weight.T, up_weight.T
    columns = width // STEP
    steps = chips.bit_length() - 3
    far = split_range(columns, [4] + [6] * steps + [0, 0])
    near = split_range(columns, [0] + [0] * steps + [6, 4])
    spans, fetched = [], []

    def beside_load(exchange, blocks):
        group = len(fetched)
        token = jax.tree.leaves(blocks)[0]
        parts = load(far[group], near[group], token, gate_rows, up_rows)
        blocks, parts = lax.optimization_barrier((exchange(blocks), parts))
        for array, span in enumerate((far[group], near[group])):
            if span:
                spans.append((array,) + span)
        fetched.append(parts)
        return blocks

    def plus(left, right):
        return left.astype(jnp.float32) + right.astype(jnp.float32)

    def trade(blocks):
        return [swap_partners(block, SIDES - 1 - index) for index, block in enumerate(blocks)]

    from_core = swap_cores(other_sum)
    far_sums = plus(far_sum, from_core[1:]).astype(jnp.bfloat16)
    from_sides = beside_load(trade, [far_sums[side] for side in reversed(range(SIDES - 1))])
    total = plus(near_sum, from_core[0])
    for block in from_sides:
        total = plus(total, block)
    total = total.astype(jnp.bfloat16)
    mask = SIDES
    while 2 * mask < chips:
        partner = beside_load(lambda block: swap_partners(block, mask), total)
        total = plus(total, partner).astype(jnp.bfloat16)
        mask *= 2
    partner = beside_load(lambda block: swap_partners(block, mask), total)
    mixed_rows, normed = renew(total, partner, post_gain, local)
    held = settle(mixed_rows)
    sides, held = lax.optimization_barrier((beside_load(trade, [normed] * (SIDES - 1)), held))
    own = stack([normed] + sides[::-1])
    halves = (own, beside_load(swap_cores, own))
    own_sum, other_sum = feed(
        halves, spans, [array for parts in fetched for array in parts], down_weight, local
    )
    lowered = scatter_halves(own_sum, other_sum, chips)
    final_rows = (mixed_rows.astype(jnp.float32) + lowered).astype(jnp.bfloat16)
    return (held, final_rows)


def gather_rows(rows, devices):
    copies = jnp.broadcast_to(rows[None], (devices,) + rows.shape)
    arrived = lax.all_to_all(copies, ("pool", "tensor"), split_axis=0, concat_axis=0, tiled=True)
    return arrived.reshape(devices * rows.shape[0], rows.shape[1])


def scatter_sum(partial, devices):
    blocks = partial.astype(jnp.bfloat16).reshape(devices, -1, partial.shape[1])
    arrived = lax.all_to_all(blocks, ("pool", "tensor"), split_axis=0, concat_axis=0, tiled=True)
    return jnp.sum(arrived.astype(jnp.float32), axis=0)


def on_device_general(
    hidden,
    input_gain,
    query_weight,
    key_weight,
    value_weight,
    query_gain,
    key_gain,
    output_weight,
    post_gain,
    gate_weight,
    up_weight,
    down_weight,
    key_cache,
    value_cache,
    lengths,
    request_slot,
):
    devices = lax.axis_size(("pool", "tensor"))
    device_index = lax.axis_index(("pool", "tensor"))
    local_rows = hidden.shape[0]
    query_cols = query_weight.shape[1]
    key_cols = key_weight.shape[1]
    width_sent = query_cols + 2 * key_cols
    head_dim = query_gain.shape[0]
    slot_count = SLOTS
    head_count = devices * query_cols // head_dim
    kv_count = devices * key_cols // head_dim
    group_size = head_count // kv_count
    normed = rms_scale(hidden, input_gain).astype(jnp.bfloat16)
    shard_rows = gather_rows(normed, devices)
    query_part = jnp.dot(shard_rows, query_weight, preferred_element_type=jnp.float32)
    key_part = jnp.dot(shard_rows, key_weight, preferred_element_type=jnp.float32)
    value_part = jnp.dot(shard_rows, value_weight, preferred_element_type=jnp.float32)
    projected = jnp.concatenate([query_part, key_part, value_part], axis=1).astype(jnp.bfloat16)
    outgoing = (
        jnp.zeros((devices * slot_count, width_sent), jnp.bfloat16).at[request_slot].set(projected)
    )
    outgoing = outgoing.reshape(devices, slot_count, width_sent)
    arrived = lax.all_to_all(
        outgoing, ("pool", "tensor"), split_axis=0, concat_axis=2, tiled=True
    ).reshape(slot_count, devices, width_sent)
    query_full = arrived[:, :, :query_cols].reshape(slot_count, head_count, head_dim)
    key_full = arrived[:, :, query_cols : query_cols + key_cols].reshape(
        slot_count, kv_count, head_dim
    )
    value_new = arrived[:, :, query_cols + key_cols :].reshape(slot_count, kv_count, head_dim)
    slot_ids = device_index * slot_count + jnp.arange(slot_count, dtype=jnp.int32)
    matches = request_slot[None, :] == slot_ids[:, None]
    slot_length = jnp.sum(jnp.where(matches, lengths[None, :], 0), axis=1)
    owner_of = request_slot // slot_count
    within = request_slot % slot_count
    earlier = (owner_of[None, :] == device_index) & (
        within[None, :] < jnp.arange(slot_count, dtype=jnp.int32)[:, None]
    )
    slot_offset = jnp.sum(jnp.where(earlier, lengths[None, :], 0), axis=1)
    position = slot_length.astype(jnp.float32)[:, None, None]
    query_heads = rotate(rms_scale(query_full, query_gain), position).astype(jnp.bfloat16)
    query_heads = query_heads.reshape(slot_count, kv_count, group_size, head_dim)
    key_new = rotate(rms_scale(key_full, key_gain), position).astype(jnp.bfloat16)
    pool_tokens = key_cache.shape[0]
    scale_factor = 1.0 / math.sqrt(head_dim)
    scores = jnp.stack(
        [
            jnp.einsum(
                "sgd,td->sgt",
                query_heads[:, kv],
                key_cache[:, kv * head_dim : (kv + 1) * head_dim],
                preferred_element_type=jnp.float32,
            )
            for kv in range(kv_count)
        ],
        axis=1,
    ) * scale_factor
    own_score = (
        jnp.einsum("skgd,skd->skg", query_heads, key_new, preferred_element_type=jnp.float32)
        * scale_factor
    )
    token_pos = jnp.arange(pool_tokens, dtype=jnp.int32)
    inside = (token_pos[None, :] >= slot_offset[:, None]) & (
        token_pos[None, :] < (slot_offset + slot_length)[:, None]
    )
    inside = inside[:, None, None, :]
    largest = jnp.maximum(jnp.max(jnp.where(inside, scores, -1e30), axis=3), own_score)
    weights = jnp.where(inside, jnp.exp(scores - largest[..., None]), 0.0)
    own_weight = jnp.exp(own_score - largest)
    denominator = jnp.sum(weights, axis=3) + own_weight
    weights_low = weights.astype(jnp.bfloat16)
    summed = jnp.stack(
        [
            jnp.einsum(
                "sgt,td->sgd",
                weights_low[:, kv],
                value_cache[:, kv * head_dim : (kv + 1) * head_dim],
                preferred_element_type=jnp.float32,
            )
            for kv in range(kv_count)
        ],
        axis=1,
    )
    own_low = own_weight.astype(jnp.bfloat16).astype(jnp.float32)
    summed = summed + own_low[..., None] * value_new.astype(jnp.float32)[:, :, None, :]
    head_out = (
        (summed / denominator[..., None])
        .astype(jnp.bfloat16)
        .reshape(slot_count, devices, query_cols)
    )
    returned = lax.all_to_all(head_out, ("pool", "tensor"), split_axis=1, concat_axis=0, tiled=True)
    head_rows = returned.reshape(devices * slot_count, query_cols)[request_slot]
    partial_value = jnp.dot(head_rows, output_weight, preferred_element_type=jnp.float32)
    mixed_rows = (hidden.astype(jnp.float32) + scatter_sum(partial_value, devices)).astype(jnp.bfloat16)
    post_normed = gather_rows(rms_scale(mixed_rows, post_gain).astype(jnp.bfloat16), devices)
    gate_part = jnp.dot(post_normed, gate_weight, preferred_element_type=jnp.float32)
    up_part = jnp.dot(post_normed, up_weight, preferred_element_type=jnp.float32)
    activated = (jax.nn.silu(gate_part) * up_part).astype(jnp.bfloat16)
    lowered = scatter_sum(
        jnp.dot(activated, down_weight, preferred_element_type=jnp.float32), devices
    )
    final_rows = (mixed_rows.astype(jnp.float32) + lowered).astype(jnp.bfloat16)
    return (mixed_rows, final_rows)


def on_device(*arrays):
    query_cols, key_cols = arrays[2].shape[1], arrays[3].shape[1]
    head_dim = arrays[5].shape[0]
    devices = lax.axis_size(("pool", "tensor"))
    kv_count = devices * key_cols // head_dim
    whole_heads = query_cols % head_dim == 0 and head_dim % LANES == 0
    shared = kv_count > 0 and devices % kv_count == 0
    chips = lax.axis_size("tensor")
    pairs = lax.axis_size("pool") == 2 and chips >= 2 * SIDES and chips & (chips - 1) == 0
    pairs = pairs and arrays[14].shape[0] % 32 == 0
    if whole_heads and shared and pairs:
        return on_device_kernels(*arrays)
    return on_device_general(*arrays)


def solution(mesh):
    placed = (
        P(("groups", "pool", "tensor"), None),
        P(),
        P(None, ("pool", "tensor")),
        P(None, ("pool", "tensor")),
        P(None, ("pool", "tensor")),
        P(),
        P(),
        P(("pool", "tensor"), None),
        P(),
        P(None, ("pool", "tensor")),
        P(None, ("pool", "tensor")),
        P(("pool", "tensor"), None),
        P(("groups", "pool", "tensor"), None),
        P(("groups", "pool", "tensor"), None),
        P("groups"),
        P("groups"),
    )
    return jax.shard_map(
        on_device,
        mesh=mesh,
        in_specs=placed,
        out_specs=(P(("groups", "pool", "tensor"), None), P(("groups", "pool", "tensor"), None)),
        check_vma=False,
    )
```

```python
import functools
import math

import jax
import jax.numpy as jnp
from jax import lax
from jax.experimental import pallas as pl
from jax.experimental.pallas import tpu as pltpu
from jax.sharding import PartitionSpec as P

SLOTS = 4
SIDES = 4
MASKS = ((1, 3, 2), (2, 1, 3))
LANES = 128
MIB = 2**20
TOKEN_STEP = 256
IN_VMEM = pl.BlockSpec(memory_space=pltpu.VMEM)
IN_HBM = pl.BlockSpec(memory_space=pl.ANY)


def cost(mib):
    return pl.CostEstimate(flops=0, bytes_accessed=mib * MIB, transcendentals=0)

STEP = 512
FEED_STEP = 256


eps = 1e-06
theta = 1000000.0


def rms_scale(values, scales):
    values = values.astype(jnp.float32)
    return values * lax.rsqrt(jnp.mean(values * values, axis=-1, keepdims=True) + eps) * scales


def rotate(values, position):
    half_width = values.shape[-1] // 2
    frequency = theta ** (-jnp.arange(half_width, dtype=jnp.float32) * 2.0 / values.shape[-1])
    angles = position * frequency
    cosine = jnp.cos(angles)
    sine_part = jnp.sin(angles)
    front_half = values[..., :half_width]
    back_half = values[..., half_width:]
    return jnp.concatenate(
        [front_half * cosine - back_half * sine_part, back_half * cosine + front_half * sine_part],
        axis=-1,
    )


def swap_cores(block):
    return lax.ppermute(block, "pool", [(0, 1), (1, 0)])


def swap_partners(block, mask):
    chips = lax.axis_size("tensor")
    return lax.ppermute(block, "tensor", [(chip, chip ^ mask) for chip in range(chips)])


def trade(blocks):
    chips = lax.axis_size("tensor")
    return [
        lax.ppermute(
            block,
            ("pool", "tensor"),
            [
                (core * chips + chip, core * chips + (chip ^ MASKS[core][index]))
                for core in range(2)
                for chip in range(chips)
            ],
        )
        for index, block in enumerate(blocks)
    ]


def swap_chips(blocks):
    return lax.all_to_all(blocks, "tensor", split_axis=0, concat_axis=0, tiled=True)


def swap_all(blocks):
    return lax.all_to_all(blocks, ("pool", "tensor"), split_axis=0, concat_axis=0, tiled=True)


def spread_kernel(rows, unread, out):
    for chip in range(out.shape[0]):
        out[chip] = rows[...]


def spread(rows, chips, unread):
    return pl.pallas_call(
        spread_kernel,
        out_shape=jax.ShapeDtypeStruct((chips,) + rows.shape, rows.dtype),
        in_specs=[IN_VMEM, IN_HBM],
        out_specs=IN_VMEM,
        compiler_params=pltpu.CompilerParams(vmem_limit_bytes=MIB),
        cost_estimate=cost(8),
        name="spread",
    )(rows, keep_in_hbm(unread))


def gather_half(rows, chips, unread):
    return swap_chips(spread(rows, chips, unread))


def scatter_halves(own_half, other_half, chips):
    added = own_half.astype(jnp.float32) + swap_cores(other_half).astype(jnp.float32)
    blocks = added.astype(jnp.bfloat16).reshape(chips, -1, own_half.shape[1])
    return jnp.sum(swap_chips(blocks).astype(jnp.float32), axis=0)


def dot_rows(left, right):
    return lax.dot_general(
        left, right, (((1,), (0,)), ((), ())), preferred_element_type=jnp.float32
    )


def dot_columns(left, right):
    return lax.dot_general(
        left, right, (((1,), (1,)), ((), ())), preferred_element_type=jnp.float32
    )


def pieces(extent, step):
    return [(start, min(step, extent - start)) for start in range(0, extent, step)]


def keep_in_hbm(array):
    return pltpu.with_memory_space_constraint(array, pltpu.HBM)


def keep_in_vmem(array):
    return pltpu.with_memory_space_constraint(array, pltpu.VMEM)


def split_range(count, shares):
    ends = [count * sum(shares[: index + 1]) // sum(shares) * STEP for index in range(len(shares))]
    starts = [0] + ends[:-1]
    return [(start, end) if start < end else None for start, end in zip(starts, ends)]


def load_kernel(far, near, token, far_rows, near_rows, *refs):
    outs = list(refs[: bool(far) + bool(near)])
    copies, stage = [], None
    if far:
        begin, end = far
        stage, sems = refs[-2:]
        for index, (start, size) in enumerate(pieces(end - begin, STEP)):
            copies.append(
                pltpu.make_async_copy(
                    far_rows.at[:, pl.ds(begin + start, size)],
                    stage.at[:, pl.ds(start, size)],
                    sems.at[index],
                )
            )
            copies[-1].start()
    if near:
        begin, end = near
        for start, size in pieces(end - begin, STEP):
            outs[-1][start : start + size, :] = near_rows[:, begin + start : begin + start + size].T
    for copy, (start, size) in zip(copies, pieces(far[1] - far[0], STEP) if far else []):
        copy.wait()
        outs[0][start : start + size, :] = stage[:, start : start + size].T


def load(far, near, token, far_rows, near_rows):
    units, width = far_rows.shape
    ranges = [span for span in (far, near) if span]
    staged = 2 * units * (far[1] - far[0]) if far else 0
    scratch = []
    if far:
        scratch = [
            pltpu.VMEM((units, far[1] - far[0]), far_rows.dtype),
            pltpu.SemaphoreType.DMA((len(pieces(far[1] - far[0], STEP)),)),
        ]
    return pl.pallas_call(
        functools.partial(load_kernel, far, near),
        out_shape=tuple(pltpu.VMEM((end - begin, units), far_rows.dtype) for begin, end in ranges),
        in_specs=[IN_HBM, IN_HBM, IN_VMEM if near else IN_HBM],
        out_specs=tuple([IN_VMEM] * len(ranges)),
        scratch_shapes=scratch,
        compiler_params=pltpu.CompilerParams(
            vmem_limit_bytes=2 * MIB + staged + (2 * units * width if near else 0)
        ),
        cost_estimate=cost(8),
        name="load",
    )(token, keep_in_hbm(far_rows), near_rows if near else keep_in_hbm(near_rows))


def flat_rows(blocks):
    return jnp.concatenate(
        [blocks[chip].astype(jnp.float32) for chip in range(blocks.shape[0])], axis=0
    )


def one_hot(rows, columns):
    return jnp.where(rows == columns, 1.0, 0.0).astype(jnp.bfloat16)


def differ(mask):
    here = lax.rem(lax.axis_index("tensor"), SIDES)
    low = lax.rem(lax.rem(mask, 2) + lax.rem(here, 2), 2)
    high = lax.rem(mask // 2 + here // 2, 2)
    return 2 * high + low


def mask_of(core, place):
    result = jnp.zeros_like(place)
    for index in range(SIDES - 1):
        mask = jnp.where(core == 0, MASKS[0][index], MASKS[1][index])
        result = jnp.where(place == index + 1, mask, result)
    return result


def place_of(core, mask):
    result = jnp.zeros_like(mask)
    for index in range(SIDES - 1):
        held = jnp.where(core == 0, MASKS[0][index], MASKS[1][index])
        result = jnp.where(mask == held, index + 1, result)
    return result


def slot_matrix(slots, places):
    return one_hot(lax.broadcasted_iota(jnp.int32, (places, slots.shape[1]), 0), slots[...])


def prepare_kernel(
    slot_count,
    slots,
    lengths,
    frequency,
    packing,
    unpacking,
    first,
    last,
    cosine,
    sine,
):
    places, requests = packing.shape
    owners = places // slot_count
    core = lax.axis_index("pool")
    natural = slot_matrix(slots, places)
    row = lax.broadcasted_iota(jnp.int32, (requests, requests), 0)
    column = lax.broadcasted_iota(jnp.int32, (requests, requests), 1)
    half_first = one_hot(lax.rem(column + core * (requests // 2), requests), row)
    packing[...] = dot_rows(natural, half_first).astype(jnp.bfloat16)
    half, block, local = requests // 2, requests // 2 // SIDES, requests // owners
    half_of = lax.rem(row // half + core, 2)
    side = differ(mask_of(half_of, lax.rem(row, half) // block))
    inner = lax.rem(row, local)
    source = half_of * half + (lax.rem(row, block) // local * SIDES + side) * local + inner
    unpacking[...] = dot_columns(one_hot(source, column), natural).astype(jnp.bfloat16)
    start = lax.axis_index(("pool", "tensor")) * slot_count
    place = slots[...] - start
    rows = lax.broadcasted_iota(jnp.int32, (slot_count, requests), 0)
    amounts = lengths[...].astype(jnp.float32)
    length = jnp.sum(jnp.where(place == rows, amounts, 0.0), axis=1, keepdims=True)
    offset = jnp.sum(
        jnp.where((place >= 0) & (place < rows), amounts, 0.0), axis=1, keepdims=True
    )
    angles = length * frequency[...]
    turn = jnp.sin(angles)
    lean = jnp.cos(angles)
    cosine[...] = jnp.concatenate([lean, lean], axis=1)
    sine[...] = jnp.concatenate([-turn, turn], axis=1)
    first[...] = jnp.broadcast_to(offset.astype(jnp.int32), first.shape)
    last[...] = jnp.broadcast_to((offset + length).astype(jnp.int32), last.shape)


def prepare(slot_count, devices, head_dim, slots, lengths):
    requests = slots.shape[0]
    places = devices * slot_count
    frequency = theta ** (-jnp.arange(head_dim // 2, dtype=jnp.float32) * 2.0 / head_dim)
    table = jax.ShapeDtypeStruct((slot_count, head_dim), jnp.float32)
    bound = jax.ShapeDtypeStruct((slot_count, head_dim), jnp.int32)
    return pl.pallas_call(
        functools.partial(prepare_kernel, slot_count),
        out_shape=(
            jax.ShapeDtypeStruct((places, requests), jnp.bfloat16),
            jax.ShapeDtypeStruct((requests, places), jnp.bfloat16),
            bound,
            bound,
            table,
            table,
        ),
        in_specs=[IN_VMEM] * 3,
        out_specs=tuple([IN_VMEM] * 6),
        compiler_params=pltpu.CompilerParams(vmem_limit_bytes=MIB),
        cost_estimate=cost(8),
        name="prepare",
    )(
        slots.reshape(1, -1),
        lengths.reshape(1, -1),
        frequency.reshape(1, -1),
    )


def project_kernel(slot_count, own, other, gain, packing, q_vm, k_vm, v_vm, out, normed):
    half = own.shape[0] * own.shape[1]
    for index, source in enumerate((own, other)):
        rows = flat_rows(source)
        scale = lax.rsqrt(jnp.mean(rows * rows, axis=-1, keepdims=True) + eps)
        normed[pl.ds(index * half, half), :] = (rows * scale * gain[...]).astype(jnp.bfloat16)
    query_part = dot_rows(normed[...], q_vm[...])
    key_part = dot_columns(normed[...], k_vm[...])
    value_part = dot_columns(normed[...], v_vm[...])
    projected = jnp.concatenate([query_part, key_part, value_part], axis=1).astype(jnp.bfloat16)
    packed = dot_rows(packing[...], projected)
    for owner in range(out.shape[0]):
        out[owner] = packed[owner * slot_count : (owner + 1) * slot_count, :].astype(jnp.bfloat16)


def project(slot_count, own, other, gain, packing, weights):
    depth, query_cols = weights[0].shape
    width = query_cols + weights[1].shape[0] + weights[2].shape[0]
    places, requests = packing.shape
    return pl.pallas_call(
        functools.partial(project_kernel, slot_count),
        out_shape=jax.ShapeDtypeStruct((places // slot_count, slot_count, width), jnp.bfloat16),
        in_specs=[IN_VMEM] * 7,
        out_specs=IN_VMEM,
        scratch_shapes=[pltpu.VMEM((requests, depth), jnp.bfloat16)],
        compiler_params=pltpu.CompilerParams(vmem_limit_bytes=8 * MIB),
        cost_estimate=cost(32),
        name="project",
    )(
        own,
        other,
        gain.reshape(1, depth),
        packing,
        *weights,
    )


def attend_kernel(
    query_cols,
    key_cols,
    arrived,
    first,
    last,
    cosine,
    sine,
    query_gain,
    key_gain,
    keys,
    values,
    out,
    queries,
    scores,
):
    devices, slot_count, _ = arrived.shape
    tokens, width = keys.shape
    head_dim = query_gain.shape[1]
    kv_count = devices * key_cols // head_dim
    sharers = devices // kv_count
    heads_here = query_cols // head_dim
    repeats = sharers * heads_here
    count = repeats * slot_count
    parts = pieces(tokens, TOKEN_STEP)
    scale_factor = 1.0 / math.sqrt(head_dim)

    def tile(rows, times):
        return jnp.concatenate([rows] * times, axis=0)

    def prepare(rows, gain, times):
        rows = rows * lax.rsqrt(jnp.mean(rows * rows, axis=-1, keepdims=True) + eps) * gain[...]
        turned = pltpu.roll(rows, head_dim // 2, 1)
        return (rows * tile(cosine[...], times) + turned * tile(sine[...], times)).astype(
            jnp.bfloat16
        )

    blocks = [arrived[device].astype(jnp.float32) for device in range(devices)]
    rows = jnp.concatenate(
        [
            blocks[kv * sharers + place][:, head * head_dim : (head + 1) * head_dim]
            for kv in range(kv_count)
            for head in range(heads_here)
            for place in range(sharers)
        ],
        axis=0,
    )
    query = prepare(rows, query_gain, kv_count * repeats)

    def whole(begin):
        return [
            jnp.concatenate(
                [
                    blocks[kv * sharers + place][:, begin : begin + key_cols]
                    for place in range(sharers)
                ],
                axis=1,
            )
            for kv in range(kv_count)
        ]

    fresh = prepare(jnp.concatenate(whole(query_cols), axis=0), key_gain, kv_count)
    fresh = fresh.astype(jnp.float32)
    key_new = jnp.concatenate(
        [
            tile(fresh[kv * slot_count : (kv + 1) * slot_count, :], repeats)
            for kv in range(kv_count)
        ],
        axis=0,
    )
    value_new = [tile(rows, repeats) for rows in whole(query_cols + key_cols)]
    own_score = (
        jnp.sum(query.astype(jnp.float32) * key_new, axis=-1, keepdims=True) * scale_factor
    )
    queries[...] = jnp.zeros(queries.shape, queries.dtype)
    for kv in range(kv_count):
        queries[kv * count : (kv + 1) * count, kv * head_dim : (kv + 1) * head_dim] = query[
            kv * count : (kv + 1) * count, :
        ]
    start = tile(first[:, :1], kv_count * repeats)
    end = tile(last[:, :1], kv_count * repeats)
    largest = own_score
    for begin, size in parts:
        positions = lax.broadcasted_iota(jnp.int32, (kv_count * count, size), 1) + begin
        inside = (positions >= start) & (positions < end)
        part = dot_columns(queries[...], keys[begin : begin + size, :]) * scale_factor
        part = jnp.where(inside, part, -1e30)
        scores[:, begin : begin + size] = part
        largest = jnp.maximum(largest, jnp.max(part, axis=1, keepdims=True))
    own_weight = jnp.exp(own_score - largest)
    denominator = own_weight
    summed = jnp.zeros((kv_count * count, width), jnp.float32)
    for begin, size in parts:
        weights = jnp.exp(scores[:, begin : begin + size] - largest)
        denominator = denominator + jnp.sum(weights, axis=1, keepdims=True)
        summed = summed + dot_rows(
            weights.astype(jnp.bfloat16), values[begin : begin + size, :]
        )
    own_low = own_weight.astype(jnp.bfloat16).astype(jnp.float32)
    for kv in range(kv_count):
        span = slice(kv * count, (kv + 1) * count)
        mine = summed[span, kv * head_dim : (kv + 1) * head_dim]
        mine = (mine + own_low[span, :] * value_new[kv]) / denominator[span, :]
        for head in range(heads_here):
            for place in range(sharers):
                row = (head * sharers + place) * slot_count
                out[kv * sharers + place, :, head * head_dim : (head + 1) * head_dim] = mine[
                    row : row + slot_count, :
                ].astype(jnp.bfloat16)


def attend(arrived, planned, query_gain, key_gain, key_cache, value_cache, query_cols):
    devices, slot_count, width = arrived.shape
    key_cols = (width - query_cols) // 2
    head_dim = query_gain.shape[0]
    tokens, cache_width = key_cache.shape
    rows = devices * query_cols // head_dim * slot_count
    return pl.pallas_call(
        functools.partial(attend_kernel, query_cols, key_cols),
        out_shape=jax.ShapeDtypeStruct((devices, slot_count, query_cols), jnp.bfloat16),
        in_specs=[IN_VMEM] * 9,
        out_specs=IN_VMEM,
        scratch_shapes=[
            pltpu.VMEM((rows, cache_width), jnp.bfloat16),
            pltpu.VMEM((rows, tokens), jnp.float32),
        ],
        compiler_params=pltpu.CompilerParams(vmem_limit_bytes=16 * MIB),
        name="attend",
    )(
        arrived,
        *planned,
        query_gain.reshape(1, head_dim),
        key_gain.reshape(1, head_dim),
        key_cache,
        value_cache,
    )


def mix_kernel(returned, unpacking, weight, hidden, near_out, far_out, other_out):
    owners = returned.shape[0]
    block, width = near_out.shape
    local = hidden.shape[0]
    group = lax.axis_index("tensor") // SIDES
    by_slot = jnp.concatenate(
        [returned[owner].astype(jnp.float32) for owner in range(owners)], axis=0
    ).astype(jnp.bfloat16)
    rows = dot_rows(unpacking[...], by_slot).astype(jnp.bfloat16)
    for start, size in pieces(width, 1024):
        columns = slice(start, start + size)
        total = dot_rows(rows, weight[:, columns])
        residual = hidden[:, columns].astype(jnp.float32)
        near_out[:, columns] = total[:block] + jnp.concatenate(
            [jnp.where(group == index, residual, 0.0) for index in range(block // local)], axis=0
        )
        for side in range(SIDES):
            row = side * block
            if side:
                far_out[side - 1, :, columns] = total[row : row + block]
            row += SIDES * block
            other_out[side, :, columns] = total[row : row + block].astype(other_out.dtype)


def mix(returned, unpacking, output_weight, hidden):
    block, width = unpacking.shape[0] // 2 // SIDES, output_weight.shape[1]
    return pl.pallas_call(
        mix_kernel,
        out_shape=(
            jax.ShapeDtypeStruct((block, width), jnp.float32),
            jax.ShapeDtypeStruct((SIDES - 1, block, width), jnp.float32),
            jax.ShapeDtypeStruct((SIDES, block, width), jnp.bfloat16),
        ),
        in_specs=[IN_VMEM] * 4,
        out_specs=(IN_VMEM, IN_VMEM, IN_VMEM),
        compiler_params=pltpu.CompilerParams(vmem_limit_bytes=8 * MIB),
        name="mix",
    )(returned, unpacking, output_weight, hidden)


def stack_kernel(*refs):
    out = refs[-1]
    for index, ref in enumerate(refs[:-1]):
        out[index] = ref[...]


def stack(blocks):
    shape = (len(blocks),) + blocks[0].shape
    return pl.pallas_call(
        stack_kernel,
        out_shape=jax.ShapeDtypeStruct(shape, blocks[0].dtype),
        in_specs=[IN_VMEM] * len(blocks),
        out_specs=IN_VMEM,
        compiler_params=pltpu.CompilerParams(vmem_limit_bytes=2 * MIB),
        name="stack",
    )(*blocks)


def renew_kernel(own, partner, gain, mixed, normed):
    local = mixed.shape[0]
    total = own[...].astype(jnp.float32) + partner[...].astype(jnp.float32)
    rows = total.astype(jnp.bfloat16).astype(jnp.float32)
    scale = lax.rsqrt(jnp.mean(rows * rows, axis=-1, keepdims=True) + eps)
    normed[...] = (rows * scale * gain[...]).astype(jnp.bfloat16)
    group = lax.axis_index("tensor") // SIDES
    here = rows[:local]
    for index in range(1, rows.shape[0] // local):
        here = jnp.where(group == index, rows[index * local : (index + 1) * local], here)
    mixed[...] = here.astype(jnp.bfloat16)


def renew(own, partner, gain, local):
    return pl.pallas_call(
        renew_kernel,
        out_shape=(
            pltpu.VMEM((local, own.shape[1]), jnp.bfloat16),
            jax.ShapeDtypeStruct(own.shape, jnp.bfloat16),
        ),
        in_specs=[IN_VMEM] * 3,
        out_specs=(IN_VMEM, IN_VMEM),
        compiler_params=pltpu.CompilerParams(vmem_limit_bytes=4 * MIB),
        name="renew",
    )(own, partner, gain.reshape(1, -1))


def settle_kernel(rows, out):
    out[...] = rows[...]


def settle(rows):
    return pl.pallas_call(
        settle_kernel,
        out_shape=jax.ShapeDtypeStruct(rows.shape, rows.dtype),
        in_specs=[IN_VMEM],
        out_specs=IN_VMEM,
        compiler_params=pltpu.CompilerParams(vmem_limit_bytes=MIB),
        cost_estimate=cost(4),
        name="settle",
    )(keep_in_vmem(rows))


def feed_kernel(spans, local, *refs):
    halves, weights = refs[:2], refs[2 : 2 + len(spans)]
    down, own_out, other_out, rows = refs[2 + len(spans) :]
    half, width = own_out.shape
    block = half // SIDES

    def part(array, start, size):
        for (index, begin, end), ref in zip(spans, weights):
            if index == array and begin <= start and start + size <= end:
                span = slice(start - begin, start - begin + size)
                return ref[span, :]

    for index, blocks in enumerate(halves):
        rows[index * half : (index + 1) * half, :] = flat_rows(blocks).astype(jnp.bfloat16)
    gate_part = up_part = 0.0
    for start, size in pieces(width, FEED_STEP):
        some = rows[:, start : start + size]
        gate_part = gate_part + dot_rows(some, part(0, start, size))
        up_part = up_part + dot_rows(some, part(1, start, size))
    active = (gate_part / (1.0 + jnp.exp(-gate_part)) * up_part).astype(jnp.bfloat16)
    row = lax.broadcasted_iota(jnp.int32, (2 * half, 2 * half), 0)
    chip = lax.rem(row, half) // local
    inner = lax.rem(row, local)
    core = lax.rem(row // half + lax.axis_index("pool"), 2)
    place = place_of(core, differ(lax.rem(chip, SIDES)))
    source = row // half * half + place * block + chip // SIDES * local + inner
    order = one_hot(source, lax.broadcasted_iota(jnp.int32, (2 * half, 2 * half), 1))
    active = dot_rows(order, active).astype(jnp.bfloat16)
    for start, size in pieces(width, FEED_STEP):
        total = dot_rows(active, down[:, start : start + size])
        own_out[:, start : start + size] = total[:half]
        other_out[:, start : start + size] = total[half:].astype(other_out.dtype)


def feed(halves, spans, weights, down_weight, local):
    _, block, width = halves[0].shape
    half = SIDES * block
    return pl.pallas_call(
        functools.partial(feed_kernel, spans, local),
        out_shape=(
            jax.ShapeDtypeStruct((half, width), jnp.float32),
            jax.ShapeDtypeStruct((half, width), jnp.bfloat16),
        ),
        in_specs=[IN_VMEM] * (3 + len(spans)),
        out_specs=(IN_VMEM, IN_VMEM),
        scratch_shapes=[pltpu.VMEM((2 * half, width), jnp.bfloat16)],
        compiler_params=pltpu.CompilerParams(vmem_limit_bytes=16 * MIB),
        name="feed",
    )(*halves, *[keep_in_vmem(weight) for weight in weights], down_weight)


def on_device_kernels(
    hidden,
    input_gain,
    query_weight,
    key_weight,
    value_weight,
    query_gain,
    key_gain,
    output_weight,
    post_gain,
    gate_weight,
    up_weight,
    down_weight,
    key_cache,
    value_cache,
    lengths,
    request_slot,
):
    devices = lax.axis_size(("pool", "tensor"))
    chips = lax.axis_size("tensor")
    local, width = hidden.shape
    slot_count = SLOTS
    query_cols = query_weight.shape[1]
    head_dim = query_gain.shape[0]
    own = gather_half(hidden, chips, gate_weight.T)
    packing, unpacking, *planned = prepare(
        slot_count, devices, head_dim, request_slot, lengths
    )
    other = swap_cores(own)
    weights = (query_weight, key_weight.T, value_weight.T)
    outgoing = project(slot_count, own, other, input_gain, packing, weights)
    head_out = attend(
        swap_all(outgoing), planned, query_gain, key_gain, key_cache, value_cache, query_cols
    )
    returned = swap_all(head_out)
    near_sum, far_sum, other_sum = mix(returned, unpacking, output_weight, hidden)

    gate_rows, up_rows = gate_weight.T, up_weight.T
    columns = width // STEP
    steps = chips.bit_length() - 3
    far = split_range(columns, [4] + [6] * steps + [0, 0])
    near = split_range(columns, [0] + [0] * steps + [6, 4])
    spans, fetched = [], []

    def beside_load(exchange, blocks):
        group = len(fetched)
        token = jax.tree.leaves(blocks)[0]
        parts = load(far[group], near[group], token, gate_rows, up_rows)
        blocks, parts = lax.optimization_barrier((exchange(blocks), parts))
        for array, span in enumerate((far[group], near[group])):
            if span:
                spans.append((array,) + span)
        fetched.append(parts)
        return blocks

    def plus(left, right):
        return left.astype(jnp.float32) + right.astype(jnp.float32)

    from_core = swap_cores(other_sum)
    far_sums = plus(far_sum, from_core[1:]).astype(jnp.bfloat16)
    from_sides = beside_load(trade, [far_sums[index] for index in range(SIDES - 1)])
    total = plus(near_sum, from_core[0])
    for block in from_sides:
        total = plus(total, block)
    total = total.astype(jnp.bfloat16)
    mask = SIDES
    while 2 * mask < chips:
        partner = beside_load(lambda block: swap_partners(block, mask), total)
        total = plus(total, partner).astype(jnp.bfloat16)
        mask *= 2
    partner = beside_load(lambda block: swap_partners(block, mask), total)
    mixed_rows, normed = renew(total, partner, post_gain, local)
    held = settle(mixed_rows)
    sides, held = lax.optimization_barrier((beside_load(trade, [normed] * (SIDES - 1)), held))
    own = stack([normed] + sides)
    halves = (own, beside_load(swap_cores, own))
    own_sum, other_sum = feed(
        halves, spans, [array for parts in fetched for array in parts], down_weight, local
    )
    lowered = scatter_halves(own_sum, other_sum, chips)
    final_rows = (mixed_rows.astype(jnp.float32) + lowered).astype(jnp.bfloat16)
    return (held, final_rows)


def gather_rows(rows, devices):
    copies = jnp.broadcast_to(rows[None], (devices,) + rows.shape)
    arrived = lax.all_to_all(copies, ("pool", "tensor"), split_axis=0, concat_axis=0, tiled=True)
    return arrived.reshape(devices * rows.shape[0], rows.shape[1])


def scatter_sum(partial, devices):
    blocks = partial.astype(jnp.bfloat16).reshape(devices, -1, partial.shape[1])
    arrived = lax.all_to_all(blocks, ("pool", "tensor"), split_axis=0, concat_axis=0, tiled=True)
    return jnp.sum(arrived.astype(jnp.float32), axis=0)


def on_device_general(
    hidden,
    input_gain,
    query_weight,
    key_weight,
    value_weight,
    query_gain,
    key_gain,
    output_weight,
    post_gain,
    gate_weight,
    up_weight,
    down_weight,
    key_cache,
    value_cache,
    lengths,
    request_slot,
):
    devices = lax.axis_size(("pool", "tensor"))
    device_index = lax.axis_index(("pool", "tensor"))
    local_rows = hidden.shape[0]
    query_cols = query_weight.shape[1]
    key_cols = key_weight.shape[1]
    width_sent = query_cols + 2 * key_cols
    head_dim = query_gain.shape[0]
    slot_count = SLOTS
    head_count = devices * query_cols // head_dim
    kv_count = devices * key_cols // head_dim
    group_size = head_count // kv_count
    normed = rms_scale(hidden, input_gain).astype(jnp.bfloat16)
    shard_rows = gather_rows(normed, devices)
    query_part = jnp.dot(shard_rows, query_weight, preferred_element_type=jnp.float32)
    key_part = jnp.dot(shard_rows, key_weight, preferred_element_type=jnp.float32)
    value_part = jnp.dot(shard_rows, value_weight, preferred_element_type=jnp.float32)
    projected = jnp.concatenate([query_part, key_part, value_part], axis=1).astype(jnp.bfloat16)
    outgoing = (
        jnp.zeros((devices * slot_count, width_sent), jnp.bfloat16).at[request_slot].set(projected)
    )
    outgoing = outgoing.reshape(devices, slot_count, width_sent)
    arrived = lax.all_to_all(
        outgoing, ("pool", "tensor"), split_axis=0, concat_axis=2, tiled=True
    ).reshape(slot_count, devices, width_sent)
    query_full = arrived[:, :, :query_cols].reshape(slot_count, head_count, head_dim)
    key_full = arrived[:, :, query_cols : query_cols + key_cols].reshape(
        slot_count, kv_count, head_dim
    )
    value_new = arrived[:, :, query_cols + key_cols :].reshape(slot_count, kv_count, head_dim)
    slot_ids = device_index * slot_count + jnp.arange(slot_count, dtype=jnp.int32)
    matches = request_slot[None, :] == slot_ids[:, None]
    slot_length = jnp.sum(jnp.where(matches, lengths[None, :], 0), axis=1)
    owner_of = request_slot // slot_count
    within = request_slot % slot_count
    earlier = (owner_of[None, :] == device_index) & (
        within[None, :] < jnp.arange(slot_count, dtype=jnp.int32)[:, None]
    )
    slot_offset = jnp.sum(jnp.where(earlier, lengths[None, :], 0), axis=1)
    position = slot_length.astype(jnp.float32)[:, None, None]
    query_heads = rotate(rms_scale(query_full, query_gain), position).astype(jnp.bfloat16)
    query_heads = query_heads.reshape(slot_count, kv_count, group_size, head_dim)
    key_new = rotate(rms_scale(key_full, key_gain), position).astype(jnp.bfloat16)
    pool_tokens = key_cache.shape[0]
    scale_factor = 1.0 / math.sqrt(head_dim)
    scores = jnp.stack(
        [
            jnp.einsum(
                "sgd,td->sgt",
                query_heads[:, kv],
                key_cache[:, kv * head_dim : (kv + 1) * head_dim],
                preferred_element_type=jnp.float32,
            )
            for kv in range(kv_count)
        ],
        axis=1,
    ) * scale_factor
    own_score = (
        jnp.einsum("skgd,skd->skg", query_heads, key_new, preferred_element_type=jnp.float32)
        * scale_factor
    )
    token_pos = jnp.arange(pool_tokens, dtype=jnp.int32)
    inside = (token_pos[None, :] >= slot_offset[:, None]) & (
        token_pos[None, :] < (slot_offset + slot_length)[:, None]
    )
    inside = inside[:, None, None, :]
    largest = jnp.maximum(jnp.max(jnp.where(inside, scores, -1e30), axis=3), own_score)
    weights = jnp.where(inside, jnp.exp(scores - largest[..., None]), 0.0)
    own_weight = jnp.exp(own_score - largest)
    denominator = jnp.sum(weights, axis=3) + own_weight
    weights_low = weights.astype(jnp.bfloat16)
    summed = jnp.stack(
        [
            jnp.einsum(
                "sgt,td->sgd",
                weights_low[:, kv],
                value_cache[:, kv * head_dim : (kv + 1) * head_dim],
                preferred_element_type=jnp.float32,
            )
            for kv in range(kv_count)
        ],
        axis=1,
    )
    own_low = own_weight.astype(jnp.bfloat16).astype(jnp.float32)
    summed = summed + own_low[..., None] * value_new.astype(jnp.float32)[:, :, None, :]
    head_out = (
        (summed / denominator[..., None])
        .astype(jnp.bfloat16)
        .reshape(slot_count, devices, query_cols)
    )
    returned = lax.all_to_all(head_out, ("pool", "tensor"), split_axis=1, concat_axis=0, tiled=True)
    head_rows = returned.reshape(devices * slot_count, query_cols)[request_slot]
    partial_value = jnp.dot(head_rows, output_weight, preferred_element_type=jnp.float32)
    mixed_rows = (hidden.astype(jnp.float32) + scatter_sum(partial_value, devices)).astype(jnp.bfloat16)
    post_normed = gather_rows(rms_scale(mixed_rows, post_gain).astype(jnp.bfloat16), devices)
    gate_part = jnp.dot(post_normed, gate_weight, preferred_element_type=jnp.float32)
    up_part = jnp.dot(post_normed, up_weight, preferred_element_type=jnp.float32)
    activated = (jax.nn.silu(gate_part) * up_part).astype(jnp.bfloat16)
    lowered = scatter_sum(
        jnp.dot(activated, down_weight, preferred_element_type=jnp.float32), devices
    )
    final_rows = (mixed_rows.astype(jnp.float32) + lowered).astype(jnp.bfloat16)
    return (mixed_rows, final_rows)


def on_device(*arrays):
    query_cols, key_cols = arrays[2].shape[1], arrays[3].shape[1]
    head_dim = arrays[5].shape[0]
    devices = lax.axis_size(("pool", "tensor"))
    kv_count = devices * key_cols // head_dim
    whole_heads = query_cols % head_dim == 0 and head_dim % LANES == 0
    shared = kv_count > 0 and devices % kv_count == 0
    chips = lax.axis_size("tensor")
    pairs = lax.axis_size("pool") == 2 and chips >= 2 * SIDES and chips & (chips - 1) == 0
    pairs = pairs and arrays[14].shape[0] % 32 == 0
    if whole_heads and shared and pairs:
        return on_device_kernels(*arrays)
    return on_device_general(*arrays)


def solution(mesh):
    placed = (
        P(("groups", "pool", "tensor"), None),
        P(),
        P(None, ("pool", "tensor")),
        P(None, ("pool", "tensor")),
        P(None, ("pool", "tensor")),
        P(),
        P(),
        P(("pool", "tensor"), None),
        P(),
        P(None, ("pool", "tensor")),
        P(None, ("pool", "tensor")),
        P(("pool", "tensor"), None),
        P(("groups", "pool", "tensor"), None),
        P(("groups", "pool", "tensor"), None),
        P("groups"),
        P("groups"),
    )
    return jax.shard_map(
        on_device,
        mesh=mesh,
        in_specs=placed,
        out_specs=(P(("groups", "pool", "tensor"), None), P(("groups", "pool", "tensor"), None)),
        check_vma=False,
    )
```

```python
import functools
import math

import jax
import jax.numpy as jnp
from jax import lax
from jax.experimental import pallas as pl
from jax.experimental.pallas import tpu as pltpu
from jax.sharding import PartitionSpec as P

SLOTS = 4
SIDES = 4
MASKS = ((2, 3, 1), (1, 2, 3))
LANES = 128
MIB = 2**20
TOKEN_STEP = 256
IN_VMEM = pl.BlockSpec(memory_space=pltpu.VMEM)
IN_HBM = pl.BlockSpec(memory_space=pl.ANY)


def cost(mib):
    return pl.CostEstimate(flops=0, bytes_accessed=mib * MIB, transcendentals=0)

STEP = 512
FEED_STEP = 256


eps = 1e-06
theta = 1000000.0


def rms_scale(values, scales):
    values = values.astype(jnp.float32)
    return values * lax.rsqrt(jnp.mean(values * values, axis=-1, keepdims=True) + eps) * scales


def rotate(values, position):
    half_width = values.shape[-1] // 2
    frequency = theta ** (-jnp.arange(half_width, dtype=jnp.float32) * 2.0 / values.shape[-1])
    angles = position * frequency
    cosine = jnp.cos(angles)
    sine_part = jnp.sin(angles)
    front_half = values[..., :half_width]
    back_half = values[..., half_width:]
    return jnp.concatenate(
        [front_half * cosine - back_half * sine_part, back_half * cosine + front_half * sine_part],
        axis=-1,
    )


def swap_cores(block):
    return lax.ppermute(block, "pool", [(0, 1), (1, 0)])


def swap_partners(block, mask):
    chips = lax.axis_size("tensor")
    return lax.ppermute(block, "tensor", [(chip, chip ^ mask) for chip in range(chips)])


def trade(blocks):
    chips = lax.axis_size("tensor")
    return [
        lax.ppermute(
            block,
            ("pool", "tensor"),
            [
                (core * chips + chip, core * chips + (chip ^ MASKS[core][index]))
                for core in range(2)
                for chip in range(chips)
            ],
        )
        for index, block in enumerate(blocks)
    ]


def swap_chips(blocks):
    return lax.all_to_all(blocks, "tensor", split_axis=0, concat_axis=0, tiled=True)


def swap_all(blocks):
    return lax.all_to_all(blocks, ("pool", "tensor"), split_axis=0, concat_axis=0, tiled=True)


def spread_kernel(rows, unread, out):
    for chip in range(out.shape[0]):
        out[chip] = rows[...]


def spread(rows, chips, unread):
    return pl.pallas_call(
        spread_kernel,
        out_shape=jax.ShapeDtypeStruct((chips,) + rows.shape, rows.dtype),
        in_specs=[IN_VMEM, IN_HBM],
        out_specs=IN_VMEM,
        compiler_params=pltpu.CompilerParams(vmem_limit_bytes=MIB),
        cost_estimate=cost(8),
        name="spread",
    )(rows, keep_in_hbm(unread))


def gather_half(rows, chips, unread):
    return swap_chips(spread(rows, chips, unread))


def scatter_halves(own_half, other_half, chips):
    added = own_half.astype(jnp.float32) + swap_cores(other_half).astype(jnp.float32)
    blocks = added.astype(jnp.bfloat16).reshape(chips, -1, own_half.shape[1])
    return jnp.sum(swap_chips(blocks).astype(jnp.float32), axis=0)


def dot_rows(left, right):
    return lax.dot_general(
        left, right, (((1,), (0,)), ((), ())), preferred_element_type=jnp.float32
    )


def dot_columns(left, right):
    return lax.dot_general(
        left, right, (((1,), (1,)), ((), ())), preferred_element_type=jnp.float32
    )


def pieces(extent, step):
    return [(start, min(step, extent - start)) for start in range(0, extent, step)]


def keep_in_hbm(array):
    return pltpu.with_memory_space_constraint(array, pltpu.HBM)


def keep_in_vmem(array):
    return pltpu.with_memory_space_constraint(array, pltpu.VMEM)


def split_range(count, shares):
    ends = [count * sum(shares[: index + 1]) // sum(shares) * STEP for index in range(len(shares))]
    starts = [0] + ends[:-1]
    return [(start, end) if start < end else None for start, end in zip(starts, ends)]


def load_kernel(far, near, token, far_rows, near_rows, *refs):
    outs = list(refs[: bool(far) + bool(near)])
    copies, stage = [], None
    if far:
        begin, end = far
        stage, sems = refs[-2:]
        for index, (start, size) in enumerate(pieces(end - begin, STEP)):
            copies.append(
                pltpu.make_async_copy(
                    far_rows.at[:, pl.ds(begin + start, size)],
                    stage.at[:, pl.ds(start, size)],
                    sems.at[index],
                )
            )
            copies[-1].start()
    if near:
        begin, end = near
        for start, size in pieces(end - begin, STEP):
            outs[-1][start : start + size, :] = near_rows[:, begin + start : begin + start + size].T
    for copy, (start, size) in zip(copies, pieces(far[1] - far[0], STEP) if far else []):
        copy.wait()
        outs[0][start : start + size, :] = stage[:, start : start + size].T


def load(far, near, token, far_rows, near_rows):
    units, width = far_rows.shape
    ranges = [span for span in (far, near) if span]
    staged = 2 * units * (far[1] - far[0]) if far else 0
    scratch = []
    if far:
        scratch = [
            pltpu.VMEM((units, far[1] - far[0]), far_rows.dtype),
            pltpu.SemaphoreType.DMA((len(pieces(far[1] - far[0], STEP)),)),
        ]
    return pl.pallas_call(
        functools.partial(load_kernel, far, near),
        out_shape=tuple(pltpu.VMEM((end - begin, units), far_rows.dtype) for begin, end in ranges),
        in_specs=[IN_HBM, IN_HBM, IN_VMEM if near else IN_HBM],
        out_specs=tuple([IN_VMEM] * len(ranges)),
        scratch_shapes=scratch,
        compiler_params=pltpu.CompilerParams(
            vmem_limit_bytes=2 * MIB + staged + (2 * units * width if near else 0)
        ),
        cost_estimate=cost(8),
        name="load",
    )(token, keep_in_hbm(far_rows), near_rows if near else keep_in_hbm(near_rows))


def flat_rows(blocks):
    return jnp.concatenate(
        [blocks[chip].astype(jnp.float32) for chip in range(blocks.shape[0])], axis=0
    )


def one_hot(rows, columns):
    return jnp.where(rows == columns, 1.0, 0.0).astype(jnp.bfloat16)


def differ(mask):
    here = lax.rem(lax.axis_index("tensor"), SIDES)
    low = lax.rem(lax.rem(mask, 2) + lax.rem(here, 2), 2)
    high = lax.rem(mask // 2 + here // 2, 2)
    return 2 * high + low


def mask_of(core, place):
    result = jnp.zeros_like(place)
    for index in range(SIDES - 1):
        mask = jnp.where(core == 0, MASKS[0][index], MASKS[1][index])
        result = jnp.where(place == index + 1, mask, result)
    return result


def place_of(core, mask):
    result = jnp.zeros_like(mask)
    for index in range(SIDES - 1):
        held = jnp.where(core == 0, MASKS[0][index], MASKS[1][index])
        result = jnp.where(mask == held, index + 1, result)
    return result


def slot_matrix(slots, places):
    return one_hot(lax.broadcasted_iota(jnp.int32, (places, slots.shape[1]), 0), slots[...])


def prepare_kernel(
    slot_count,
    slots,
    lengths,
    frequency,
    packing,
    unpacking,
    first,
    last,
    cosine,
    sine,
):
    places, requests = packing.shape
    owners = places // slot_count
    core = lax.axis_index("pool")
    natural = slot_matrix(slots, places)
    row = lax.broadcasted_iota(jnp.int32, (requests, requests), 0)
    column = lax.broadcasted_iota(jnp.int32, (requests, requests), 1)
    half_first = one_hot(lax.rem(column + core * (requests // 2), requests), row)
    packing[...] = dot_rows(natural, half_first).astype(jnp.bfloat16)
    half, block, local = requests // 2, requests // 2 // SIDES, requests // owners
    half_of = lax.rem(row // half + core, 2)
    side = differ(mask_of(half_of, lax.rem(row, half) // block))
    inner = lax.rem(row, local)
    source = half_of * half + (lax.rem(row, block) // local * SIDES + side) * local + inner
    unpacking[...] = dot_columns(one_hot(source, column), natural).astype(jnp.bfloat16)
    start = lax.axis_index(("pool", "tensor")) * slot_count
    place = slots[...] - start
    rows = lax.broadcasted_iota(jnp.int32, (slot_count, requests), 0)
    amounts = lengths[...].astype(jnp.float32)
    length = jnp.sum(jnp.where(place == rows, amounts, 0.0), axis=1, keepdims=True)
    offset = jnp.sum(
        jnp.where((place >= 0) & (place < rows), amounts, 0.0), axis=1, keepdims=True
    )
    angles = length * frequency[...]
    turn = jnp.sin(angles)
    lean = jnp.cos(angles)
    cosine[...] = jnp.concatenate([lean, lean], axis=1)
    sine[...] = jnp.concatenate([-turn, turn], axis=1)
    first[...] = jnp.broadcast_to(offset.astype(jnp.int32), first.shape)
    last[...] = jnp.broadcast_to((offset + length).astype(jnp.int32), last.shape)


def prepare(slot_count, devices, head_dim, slots, lengths):
    requests = slots.shape[0]
    places = devices * slot_count
    frequency = theta ** (-jnp.arange(head_dim // 2, dtype=jnp.float32) * 2.0 / head_dim)
    table = jax.ShapeDtypeStruct((slot_count, head_dim), jnp.float32)
    bound = jax.ShapeDtypeStruct((slot_count, head_dim), jnp.int32)
    return pl.pallas_call(
        functools.partial(prepare_kernel, slot_count),
        out_shape=(
            jax.ShapeDtypeStruct((places, requests), jnp.bfloat16),
            jax.ShapeDtypeStruct((requests, places), jnp.bfloat16),
            bound,
            bound,
            table,
            table,
        ),
        in_specs=[IN_VMEM] * 3,
        out_specs=tuple([IN_VMEM] * 6),
        compiler_params=pltpu.CompilerParams(vmem_limit_bytes=MIB),
        cost_estimate=cost(8),
        name="prepare",
    )(
        slots.reshape(1, -1),
        lengths.reshape(1, -1),
        frequency.reshape(1, -1),
    )


def project_kernel(slot_count, own, other, gain, packing, q_vm, k_vm, v_vm, out, normed):
    half = own.shape[0] * own.shape[1]
    for index, source in enumerate((own, other)):
        rows = flat_rows(source)
        scale = lax.rsqrt(jnp.mean(rows * rows, axis=-1, keepdims=True) + eps)
        normed[pl.ds(index * half, half), :] = (rows * scale * gain[...]).astype(jnp.bfloat16)
    query_part = dot_rows(normed[...], q_vm[...])
    key_part = dot_columns(normed[...], k_vm[...])
    value_part = dot_columns(normed[...], v_vm[...])
    projected = jnp.concatenate([query_part, key_part, value_part], axis=1).astype(jnp.bfloat16)
    packed = dot_rows(packing[...], projected)
    for owner in range(out.shape[0]):
        out[owner] = packed[owner * slot_count : (owner + 1) * slot_count, :].astype(jnp.bfloat16)


def project(slot_count, own, other, gain, packing, weights):
    depth, query_cols = weights[0].shape
    width = query_cols + weights[1].shape[0] + weights[2].shape[0]
    places, requests = packing.shape
    return pl.pallas_call(
        functools.partial(project_kernel, slot_count),
        out_shape=jax.ShapeDtypeStruct((places // slot_count, slot_count, width), jnp.bfloat16),
        in_specs=[IN_VMEM] * 7,
        out_specs=IN_VMEM,
        scratch_shapes=[pltpu.VMEM((requests, depth), jnp.bfloat16)],
        compiler_params=pltpu.CompilerParams(vmem_limit_bytes=8 * MIB),
        cost_estimate=cost(32),
        name="project",
    )(
        own,
        other,
        gain.reshape(1, depth),
        packing,
        *weights,
    )


def attend_kernel(
    query_cols,
    key_cols,
    arrived,
    first,
    last,
    cosine,
    sine,
    query_gain,
    key_gain,
    keys,
    values,
    out,
    queries,
    scores,
):
    devices, slot_count, _ = arrived.shape
    tokens, width = keys.shape
    head_dim = query_gain.shape[1]
    kv_count = devices * key_cols // head_dim
    sharers = devices // kv_count
    heads_here = query_cols // head_dim
    repeats = sharers * heads_here
    count = repeats * slot_count
    parts = pieces(tokens, TOKEN_STEP)
    scale_factor = 1.0 / math.sqrt(head_dim)

    def tile(rows, times):
        return jnp.concatenate([rows] * times, axis=0)

    def prepare(rows, gain, times):
        rows = rows * lax.rsqrt(jnp.mean(rows * rows, axis=-1, keepdims=True) + eps) * gain[...]
        turned = pltpu.roll(rows, head_dim // 2, 1)
        return (rows * tile(cosine[...], times) + turned * tile(sine[...], times)).astype(
            jnp.bfloat16
        )

    blocks = [arrived[device].astype(jnp.float32) for device in range(devices)]
    rows = jnp.concatenate(
        [
            blocks[kv * sharers + place][:, head * head_dim : (head + 1) * head_dim]
            for kv in range(kv_count)
            for head in range(heads_here)
            for place in range(sharers)
        ],
        axis=0,
    )
    query = prepare(rows, query_gain, kv_count * repeats)

    def whole(begin):
        return [
            jnp.concatenate(
                [
                    blocks[kv * sharers + place][:, begin : begin + key_cols]
                    for place in range(sharers)
                ],
                axis=1,
            )
            for kv in range(kv_count)
        ]

    fresh = prepare(jnp.concatenate(whole(query_cols), axis=0), key_gain, kv_count)
    fresh = fresh.astype(jnp.float32)
    key_new = jnp.concatenate(
        [
            tile(fresh[kv * slot_count : (kv + 1) * slot_count, :], repeats)
            for kv in range(kv_count)
        ],
        axis=0,
    )
    value_new = [tile(rows, repeats) for rows in whole(query_cols + key_cols)]
    own_score = (
        jnp.sum(query.astype(jnp.float32) * key_new, axis=-1, keepdims=True) * scale_factor
    )
    queries[...] = jnp.zeros(queries.shape, queries.dtype)
    for kv in range(kv_count):
        queries[kv * count : (kv + 1) * count, kv * head_dim : (kv + 1) * head_dim] = query[
            kv * count : (kv + 1) * count, :
        ]
    start = tile(first[:, :1], kv_count * repeats)
    end = tile(last[:, :1], kv_count * repeats)
    largest = own_score
    for begin, size in parts:
        positions = lax.broadcasted_iota(jnp.int32, (kv_count * count, size), 1) + begin
        inside = (positions >= start) & (positions < end)
        part = dot_columns(queries[...], keys[begin : begin + size, :]) * scale_factor
        part = jnp.where(inside, part, -1e30)
        scores[:, begin : begin + size] = part
        largest = jnp.maximum(largest, jnp.max(part, axis=1, keepdims=True))
    own_weight = jnp.exp(own_score - largest)
    denominator = own_weight
    summed = jnp.zeros((kv_count * count, width), jnp.float32)
    for begin, size in parts:
        weights = jnp.exp(scores[:, begin : begin + size] - largest)
        denominator = denominator + jnp.sum(weights, axis=1, keepdims=True)
        summed = summed + dot_rows(
            weights.astype(jnp.bfloat16), values[begin : begin + size, :]
        )
    own_low = own_weight.astype(jnp.bfloat16).astype(jnp.float32)
    for kv in range(kv_count):
        span = slice(kv * count, (kv + 1) * count)
        mine = summed[span, kv * head_dim : (kv + 1) * head_dim]
        mine = (mine + own_low[span, :] * value_new[kv]) / denominator[span, :]
        for head in range(heads_here):
            for place in range(sharers):
                row = (head * sharers + place) * slot_count
                out[kv * sharers + place, :, head * head_dim : (head + 1) * head_dim] = mine[
                    row : row + slot_count, :
                ].astype(jnp.bfloat16)


def attend(arrived, planned, query_gain, key_gain, key_cache, value_cache, query_cols):
    devices, slot_count, width = arrived.shape
    key_cols = (width - query_cols) // 2
    head_dim = query_gain.shape[0]
    tokens, cache_width = key_cache.shape
    rows = devices * query_cols // head_dim * slot_count
    return pl.pallas_call(
        functools.partial(attend_kernel, query_cols, key_cols),
        out_shape=jax.ShapeDtypeStruct((devices, slot_count, query_cols), jnp.bfloat16),
        in_specs=[IN_VMEM] * 9,
        out_specs=IN_VMEM,
        scratch_shapes=[
            pltpu.VMEM((rows, cache_width), jnp.bfloat16),
            pltpu.VMEM((rows, tokens), jnp.float32),
        ],
        compiler_params=pltpu.CompilerParams(vmem_limit_bytes=16 * MIB),
        name="attend",
    )(
        arrived,
        *planned,
        query_gain.reshape(1, head_dim),
        key_gain.reshape(1, head_dim),
        key_cache,
        value_cache,
    )


def mix_kernel(returned, unpacking, weight, hidden, near_out, far_out, other_out):
    owners = returned.shape[0]
    block, width = near_out.shape
    local = hidden.shape[0]
    group = lax.axis_index("tensor") // SIDES
    by_slot = jnp.concatenate(
        [returned[owner].astype(jnp.float32) for owner in range(owners)], axis=0
    ).astype(jnp.bfloat16)
    rows = dot_rows(unpacking[...], by_slot).astype(jnp.bfloat16)
    for start, size in pieces(width, 1024):
        columns = slice(start, start + size)
        total = dot_rows(rows, weight[:, columns])
        residual = hidden[:, columns].astype(jnp.float32)
        near_out[:, columns] = total[:block] + jnp.concatenate(
            [jnp.where(group == index, residual, 0.0) for index in range(block // local)], axis=0
        )
        for side in range(SIDES):
            row = side * block
            if side:
                far_out[side - 1, :, columns] = total[row : row + block]
            row += SIDES * block
            other_out[side, :, columns] = total[row : row + block].astype(other_out.dtype)


def mix(returned, unpacking, output_weight, hidden):
    block, width = unpacking.shape[0] // 2 // SIDES, output_weight.shape[1]
    return pl.pallas_call(
        mix_kernel,
        out_shape=(
            jax.ShapeDtypeStruct((block, width), jnp.float32),
            jax.ShapeDtypeStruct((SIDES - 1, block, width), jnp.float32),
            jax.ShapeDtypeStruct((SIDES, block, width), jnp.bfloat16),
        ),
        in_specs=[IN_VMEM] * 4,
        out_specs=(IN_VMEM, IN_VMEM, IN_VMEM),
        compiler_params=pltpu.CompilerParams(vmem_limit_bytes=8 * MIB),
        name="mix",
    )(returned, unpacking, output_weight, hidden)


def stack_kernel(*refs):
    out = refs[-1]
    for index, ref in enumerate(refs[:-1]):
        out[index] = ref[...]


def stack(blocks):
    shape = (len(blocks),) + blocks[0].shape
    return pl.pallas_call(
        stack_kernel,
        out_shape=jax.ShapeDtypeStruct(shape, blocks[0].dtype),
        in_specs=[IN_VMEM] * len(blocks),
        out_specs=IN_VMEM,
        compiler_params=pltpu.CompilerParams(vmem_limit_bytes=2 * MIB),
        name="stack",
    )(*blocks)


def renew_kernel(own, partner, gain, mixed, normed):
    local = mixed.shape[0]
    total = own[...].astype(jnp.float32) + partner[...].astype(jnp.float32)
    rows = total.astype(jnp.bfloat16).astype(jnp.float32)
    scale = lax.rsqrt(jnp.mean(rows * rows, axis=-1, keepdims=True) + eps)
    normed[...] = (rows * scale * gain[...]).astype(jnp.bfloat16)
    group = lax.axis_index("tensor") // SIDES
    here = rows[:local]
    for index in range(1, rows.shape[0] // local):
        here = jnp.where(group == index, rows[index * local : (index + 1) * local], here)
    mixed[...] = here.astype(jnp.bfloat16)


def renew(own, partner, gain, local):
    return pl.pallas_call(
        renew_kernel,
        out_shape=(
            pltpu.VMEM((local, own.shape[1]), jnp.bfloat16),
            jax.ShapeDtypeStruct(own.shape, jnp.bfloat16),
        ),
        in_specs=[IN_VMEM] * 3,
        out_specs=(IN_VMEM, IN_VMEM),
        compiler_params=pltpu.CompilerParams(vmem_limit_bytes=4 * MIB),
        name="renew",
    )(own, partner, gain.reshape(1, -1))


def settle_kernel(rows, out):
    out[...] = rows[...]


def settle(rows):
    return pl.pallas_call(
        settle_kernel,
        out_shape=jax.ShapeDtypeStruct(rows.shape, rows.dtype),
        in_specs=[IN_VMEM],
        out_specs=IN_VMEM,
        compiler_params=pltpu.CompilerParams(vmem_limit_bytes=MIB),
        cost_estimate=cost(4),
        name="settle",
    )(keep_in_vmem(rows))


def feed_kernel(spans, local, *refs):
    halves, weights = refs[:2], refs[2 : 2 + len(spans)]
    down, own_out, other_out, rows = refs[2 + len(spans) :]
    half, width = own_out.shape
    block = half // SIDES

    def part(array, start, size):
        for (index, begin, end), ref in zip(spans, weights):
            if index == array and begin <= start and start + size <= end:
                span = slice(start - begin, start - begin + size)
                return ref[span, :]

    for index, blocks in enumerate(halves):
        rows[index * half : (index + 1) * half, :] = flat_rows(blocks).astype(jnp.bfloat16)
    gate_part = up_part = 0.0
    for start, size in pieces(width, FEED_STEP):
        some = rows[:, start : start + size]
        gate_part = gate_part + dot_rows(some, part(0, start, size))
        up_part = up_part + dot_rows(some, part(1, start, size))
    active = (gate_part / (1.0 + jnp.exp(-gate_part)) * up_part).astype(jnp.bfloat16)
    row = lax.broadcasted_iota(jnp.int32, (2 * half, 2 * half), 0)
    chip = lax.rem(row, half) // local
    inner = lax.rem(row, local)
    core = lax.rem(row // half + lax.axis_index("pool"), 2)
    place = place_of(core, differ(lax.rem(chip, SIDES)))
    source = row // half * half + place * block + chip // SIDES * local + inner
    order = one_hot(source, lax.broadcasted_iota(jnp.int32, (2 * half, 2 * half), 1))
    active = dot_rows(order, active).astype(jnp.bfloat16)
    for start, size in pieces(width, FEED_STEP):
        total = dot_rows(active, down[:, start : start + size])
        own_out[:, start : start + size] = total[:half]
        other_out[:, start : start + size] = total[half:].astype(other_out.dtype)


def feed(halves, spans, weights, down_weight, local):
    _, block, width = halves[0].shape
    half = SIDES * block
    return pl.pallas_call(
        functools.partial(feed_kernel, spans, local),
        out_shape=(
            jax.ShapeDtypeStruct((half, width), jnp.float32),
            jax.ShapeDtypeStruct((half, width), jnp.bfloat16),
        ),
        in_specs=[IN_VMEM] * (3 + len(spans)),
        out_specs=(IN_VMEM, IN_VMEM),
        scratch_shapes=[pltpu.VMEM((2 * half, width), jnp.bfloat16)],
        compiler_params=pltpu.CompilerParams(vmem_limit_bytes=16 * MIB),
        name="feed",
    )(*halves, *[keep_in_vmem(weight) for weight in weights], down_weight)


def on_device_kernels(
    hidden,
    input_gain,
    query_weight,
    key_weight,
    value_weight,
    query_gain,
    key_gain,
    output_weight,
    post_gain,
    gate_weight,
    up_weight,
    down_weight,
    key_cache,
    value_cache,
    lengths,
    request_slot,
):
    devices = lax.axis_size(("pool", "tensor"))
    chips = lax.axis_size("tensor")
    local, width = hidden.shape
    slot_count = SLOTS
    query_cols = query_weight.shape[1]
    head_dim = query_gain.shape[0]
    own = gather_half(hidden, chips, gate_weight.T)
    packing, unpacking, *planned = prepare(
        slot_count, devices, head_dim, request_slot, lengths
    )
    other = swap_cores(own)
    weights = (query_weight, key_weight.T, value_weight.T)
    outgoing = project(slot_count, own, other, input_gain, packing, weights)
    head_out = attend(
        swap_all(outgoing), planned, query_gain, key_gain, key_cache, value_cache, query_cols
    )
    returned = swap_all(head_out)
    near_sum, far_sum, other_sum = mix(returned, unpacking, output_weight, hidden)

    gate_rows, up_rows = gate_weight.T, up_weight.T
    columns = width // STEP
    steps = chips.bit_length() - 3
    far = split_range(columns, [4] + [6] * steps + [0, 0])
    near = split_range(columns, [0] + [0] * steps + [6, 4])
    spans, fetched = [], []

    def beside_load(exchange, blocks):
        group = len(fetched)
        token = jax.tree.leaves(blocks)[0]
        parts = load(far[group], near[group], token, gate_rows, up_rows)
        blocks, parts = lax.optimization_barrier((exchange(blocks), parts))
        for array, span in enumerate((far[group], near[group])):
            if span:
                spans.append((array,) + span)
        fetched.append(parts)
        return blocks

    def plus(left, right):
        return left.astype(jnp.float32) + right.astype(jnp.float32)

    from_core = swap_cores(other_sum)
    far_sums = plus(far_sum, from_core[1:]).astype(jnp.bfloat16)
    from_sides = beside_load(trade, [far_sums[index] for index in range(SIDES - 1)])
    total = plus(near_sum, from_core[0])
    for block in from_sides:
        total = plus(total, block)
    total = total.astype(jnp.bfloat16)
    mask = SIDES
    while 2 * mask < chips:
        partner = beside_load(lambda block: swap_partners(block, mask), total)
        total = plus(total, partner).astype(jnp.bfloat16)
        mask *= 2
    partner = beside_load(lambda block: swap_partners(block, mask), total)
    mixed_rows, normed = renew(total, partner, post_gain, local)
    held = settle(mixed_rows)
    sides, held = lax.optimization_barrier((beside_load(trade, [normed] * (SIDES - 1)), held))
    own = stack([normed] + sides)
    halves = (own, beside_load(swap_cores, own))
    own_sum, other_sum = feed(
        halves, spans, [array for parts in fetched for array in parts], down_weight, local
    )
    lowered = scatter_halves(own_sum, other_sum, chips)
    final_rows = (mixed_rows.astype(jnp.float32) + lowered).astype(jnp.bfloat16)
    return (held, final_rows)


def gather_rows(rows, devices):
    copies = jnp.broadcast_to(rows[None], (devices,) + rows.shape)
    arrived = lax.all_to_all(copies, ("pool", "tensor"), split_axis=0, concat_axis=0, tiled=True)
    return arrived.reshape(devices * rows.shape[0], rows.shape[1])


def scatter_sum(partial, devices):
    blocks = partial.astype(jnp.bfloat16).reshape(devices, -1, partial.shape[1])
    arrived = lax.all_to_all(blocks, ("pool", "tensor"), split_axis=0, concat_axis=0, tiled=True)
    return jnp.sum(arrived.astype(jnp.float32), axis=0)


def on_device_general(
    hidden,
    input_gain,
    query_weight,
    key_weight,
    value_weight,
    query_gain,
    key_gain,
    output_weight,
    post_gain,
    gate_weight,
    up_weight,
    down_weight,
    key_cache,
    value_cache,
    lengths,
    request_slot,
):
    devices = lax.axis_size(("pool", "tensor"))
    device_index = lax.axis_index(("pool", "tensor"))
    local_rows = hidden.shape[0]
    query_cols = query_weight.shape[1]
    key_cols = key_weight.shape[1]
    width_sent = query_cols + 2 * key_cols
    head_dim = query_gain.shape[0]
    slot_count = SLOTS
    head_count = devices * query_cols // head_dim
    kv_count = devices * key_cols // head_dim
    group_size = head_count // kv_count
    normed = rms_scale(hidden, input_gain).astype(jnp.bfloat16)
    shard_rows = gather_rows(normed, devices)
    query_part = jnp.dot(shard_rows, query_weight, preferred_element_type=jnp.float32)
    key_part = jnp.dot(shard_rows, key_weight, preferred_element_type=jnp.float32)
    value_part = jnp.dot(shard_rows, value_weight, preferred_element_type=jnp.float32)
    projected = jnp.concatenate([query_part, key_part, value_part], axis=1).astype(jnp.bfloat16)
    outgoing = (
        jnp.zeros((devices * slot_count, width_sent), jnp.bfloat16).at[request_slot].set(projected)
    )
    outgoing = outgoing.reshape(devices, slot_count, width_sent)
    arrived = lax.all_to_all(
        outgoing, ("pool", "tensor"), split_axis=0, concat_axis=2, tiled=True
    ).reshape(slot_count, devices, width_sent)
    query_full = arrived[:, :, :query_cols].reshape(slot_count, head_count, head_dim)
    key_full = arrived[:, :, query_cols : query_cols + key_cols].reshape(
        slot_count, kv_count, head_dim
    )
    value_new = arrived[:, :, query_cols + key_cols :].reshape(slot_count, kv_count, head_dim)
    slot_ids = device_index * slot_count + jnp.arange(slot_count, dtype=jnp.int32)
    matches = request_slot[None, :] == slot_ids[:, None]
    slot_length = jnp.sum(jnp.where(matches, lengths[None, :], 0), axis=1)
    owner_of = request_slot // slot_count
    within = request_slot % slot_count
    earlier = (owner_of[None, :] == device_index) & (
        within[None, :] < jnp.arange(slot_count, dtype=jnp.int32)[:, None]
    )
    slot_offset = jnp.sum(jnp.where(earlier, lengths[None, :], 0), axis=1)
    position = slot_length.astype(jnp.float32)[:, None, None]
    query_heads = rotate(rms_scale(query_full, query_gain), position).astype(jnp.bfloat16)
    query_heads = query_heads.reshape(slot_count, kv_count, group_size, head_dim)
    key_new = rotate(rms_scale(key_full, key_gain), position).astype(jnp.bfloat16)
    pool_tokens = key_cache.shape[0]
    scale_factor = 1.0 / math.sqrt(head_dim)
    scores = jnp.stack(
        [
            jnp.einsum(
                "sgd,td->sgt",
                query_heads[:, kv],
                key_cache[:, kv * head_dim : (kv + 1) * head_dim],
                preferred_element_type=jnp.float32,
            )
            for kv in range(kv_count)
        ],
        axis=1,
    ) * scale_factor
    own_score = (
        jnp.einsum("skgd,skd->skg", query_heads, key_new, preferred_element_type=jnp.float32)
        * scale_factor
    )
    token_pos = jnp.arange(pool_tokens, dtype=jnp.int32)
    inside = (token_pos[None, :] >= slot_offset[:, None]) & (
        token_pos[None, :] < (slot_offset + slot_length)[:, None]
    )
    inside = inside[:, None, None, :]
    largest = jnp.maximum(jnp.max(jnp.where(inside, scores, -1e30), axis=3), own_score)
    weights = jnp.where(inside, jnp.exp(scores - largest[..., None]), 0.0)
    own_weight = jnp.exp(own_score - largest)
    denominator = jnp.sum(weights, axis=3) + own_weight
    weights_low = weights.astype(jnp.bfloat16)
    summed = jnp.stack(
        [
            jnp.einsum(
                "sgt,td->sgd",
                weights_low[:, kv],
                value_cache[:, kv * head_dim : (kv + 1) * head_dim],
                preferred_element_type=jnp.float32,
            )
            for kv in range(kv_count)
        ],
        axis=1,
    )
    own_low = own_weight.astype(jnp.bfloat16).astype(jnp.float32)
    summed = summed + own_low[..., None] * value_new.astype(jnp.float32)[:, :, None, :]
    head_out = (
        (summed / denominator[..., None])
        .astype(jnp.bfloat16)
        .reshape(slot_count, devices, query_cols)
    )
    returned = lax.all_to_all(head_out, ("pool", "tensor"), split_axis=1, concat_axis=0, tiled=True)
    head_rows = returned.reshape(devices * slot_count, query_cols)[request_slot]
    partial_value = jnp.dot(head_rows, output_weight, preferred_element_type=jnp.float32)
    mixed_rows = (hidden.astype(jnp.float32) + scatter_sum(partial_value, devices)).astype(jnp.bfloat16)
    post_normed = gather_rows(rms_scale(mixed_rows, post_gain).astype(jnp.bfloat16), devices)
    gate_part = jnp.dot(post_normed, gate_weight, preferred_element_type=jnp.float32)
    up_part = jnp.dot(post_normed, up_weight, preferred_element_type=jnp.float32)
    activated = (jax.nn.silu(gate_part) * up_part).astype(jnp.bfloat16)
    lowered = scatter_sum(
        jnp.dot(activated, down_weight, preferred_element_type=jnp.float32), devices
    )
    final_rows = (mixed_rows.astype(jnp.float32) + lowered).astype(jnp.bfloat16)
    return (mixed_rows, final_rows)


def on_device(*arrays):
    query_cols, key_cols = arrays[2].shape[1], arrays[3].shape[1]
    head_dim = arrays[5].shape[0]
    devices = lax.axis_size(("pool", "tensor"))
    kv_count = devices * key_cols // head_dim
    whole_heads = query_cols % head_dim == 0 and head_dim % LANES == 0
    shared = kv_count > 0 and devices % kv_count == 0
    chips = lax.axis_size("tensor")
    pairs = lax.axis_size("pool") == 2 and chips >= 2 * SIDES and chips & (chips - 1) == 0
    pairs = pairs and arrays[14].shape[0] % 32 == 0
    if whole_heads and shared and pairs:
        return on_device_kernels(*arrays)
    return on_device_general(*arrays)


def solution(mesh):
    placed = (
        P(("groups", "pool", "tensor"), None),
        P(),
        P(None, ("pool", "tensor")),
        P(None, ("pool", "tensor")),
        P(None, ("pool", "tensor")),
        P(),
        P(),
        P(("pool", "tensor"), None),
        P(),
        P(None, ("pool", "tensor")),
        P(None, ("pool", "tensor")),
        P(("pool", "tensor"), None),
        P(("groups", "pool", "tensor"), None),
        P(("groups", "pool", "tensor"), None),
        P("groups"),
        P("groups"),
    )
    return jax.shard_map(
        on_device,
        mesh=mesh,
        in_specs=placed,
        out_specs=(P(("groups", "pool", "tensor"), None), P(("groups", "pool", "tensor"), None)),
        check_vma=False,
    )
```

```python
import functools
import math

import jax
import jax.numpy as jnp
from jax import lax
from jax.experimental import pallas as pl
from jax.experimental.pallas import tpu as pltpu
from jax.sharding import PartitionSpec as P

SLOTS = 4
SIDES = 4
MASKS = ((2, 3, 1), (1, 2, 3))
LANES = 128
MIB = 2**20
TOKEN_STEP = 256
IN_VMEM = pl.BlockSpec(memory_space=pltpu.VMEM)
IN_HBM = pl.BlockSpec(memory_space=pl.ANY)


def cost(mib):
    return pl.CostEstimate(flops=0, bytes_accessed=mib * MIB, transcendentals=0)

STEP = 512
FEED_STEP = 256


eps = 1e-06
theta = 1000000.0


def rms_scale(values, scales):
    values = values.astype(jnp.float32)
    return values * lax.rsqrt(jnp.mean(values * values, axis=-1, keepdims=True) + eps) * scales


def rotate(values, position):
    half_width = values.shape[-1] // 2
    frequency = theta ** (-jnp.arange(half_width, dtype=jnp.float32) * 2.0 / values.shape[-1])
    angles = position * frequency
    cosine = jnp.cos(angles)
    sine_part = jnp.sin(angles)
    front_half = values[..., :half_width]
    back_half = values[..., half_width:]
    return jnp.concatenate(
        [front_half * cosine - back_half * sine_part, back_half * cosine + front_half * sine_part],
        axis=-1,
    )


def swap_cores(block):
    return lax.ppermute(block, "pool", [(0, 1), (1, 0)])


def swap_partners(block, mask):
    chips = lax.axis_size("tensor")
    return lax.ppermute(block, "tensor", [(chip, chip ^ mask) for chip in range(chips)])


def trade(blocks):
    chips = lax.axis_size("tensor")
    return [
        lax.ppermute(
            block,
            ("pool", "tensor"),
            [
                (core * chips + chip, core * chips + (chip ^ MASKS[core][index]))
                for core in range(2)
                for chip in range(chips)
            ],
        )
        for index, block in enumerate(blocks)
    ]


def swap_chips(blocks):
    return lax.all_to_all(blocks, "tensor", split_axis=0, concat_axis=0, tiled=True)


def swap_all(blocks):
    return lax.all_to_all(blocks, ("pool", "tensor"), split_axis=0, concat_axis=0, tiled=True)


def spread_kernel(rows, unread, out):
    for chip in range(out.shape[0]):
        out[chip] = rows[...]


def spread(rows, chips, unread):
    return pl.pallas_call(
        spread_kernel,
        out_shape=jax.ShapeDtypeStruct((chips,) + rows.shape, rows.dtype),
        in_specs=[IN_VMEM, IN_HBM],
        out_specs=IN_VMEM,
        compiler_params=pltpu.CompilerParams(vmem_limit_bytes=MIB),
        cost_estimate=cost(8),
        name="spread",
    )(rows, keep_in_hbm(unread))


def gather_half(rows, chips, unread):
    return swap_chips(spread(rows, chips, unread))


def scatter_halves(own_half, other_half, chips):
    added = own_half.astype(jnp.float32) + swap_cores(other_half).astype(jnp.float32)
    blocks = added.astype(jnp.bfloat16).reshape(chips, -1, own_half.shape[1])
    return jnp.sum(swap_chips(blocks).astype(jnp.float32), axis=0)


def dot_rows(left, right):
    return lax.dot_general(
        left, right, (((1,), (0,)), ((), ())), preferred_element_type=jnp.float32
    )


def dot_columns(left, right):
    return lax.dot_general(
        left, right, (((1,), (1,)), ((), ())), preferred_element_type=jnp.float32
    )


def pieces(extent, step):
    return [(start, min(step, extent - start)) for start in range(0, extent, step)]


def keep_in_hbm(array):
    return pltpu.with_memory_space_constraint(array, pltpu.HBM)


def keep_in_vmem(array):
    return pltpu.with_memory_space_constraint(array, pltpu.VMEM)


def split_range(count, shares):
    ends = [count * sum(shares[: index + 1]) // sum(shares) * STEP for index in range(len(shares))]
    starts = [0] + ends[:-1]
    return [(start, end) if start < end else None for start, end in zip(starts, ends)]


def load_kernel(far, near, token, far_rows, near_rows, *refs):
    outs = list(refs[: bool(far) + bool(near)])
    copies, stage = [], None
    if far:
        begin, end = far
        stage, sems = refs[-2:]
        for index, (start, size) in enumerate(pieces(end - begin, STEP)):
            copies.append(
                pltpu.make_async_copy(
                    far_rows.at[:, pl.ds(begin + start, size)],
                    stage.at[:, pl.ds(start, size)],
                    sems.at[index],
                )
            )
            copies[-1].start()
    if near:
        begin, end = near
        for start, size in pieces(end - begin, STEP):
            outs[-1][start : start + size, :] = near_rows[:, begin + start : begin + start + size].T
    for copy, (start, size) in zip(copies, pieces(far[1] - far[0], STEP) if far else []):
        copy.wait()
        outs[0][start : start + size, :] = stage[:, start : start + size].T


def load(far, near, token, far_rows, near_rows):
    units, width = far_rows.shape
    ranges = [span for span in (far, near) if span]
    staged = 2 * units * (far[1] - far[0]) if far else 0
    scratch = []
    if far:
        scratch = [
            pltpu.VMEM((units, far[1] - far[0]), far_rows.dtype),
            pltpu.SemaphoreType.DMA((len(pieces(far[1] - far[0], STEP)),)),
        ]
    return pl.pallas_call(
        functools.partial(load_kernel, far, near),
        out_shape=tuple(pltpu.VMEM((end - begin, units), far_rows.dtype) for begin, end in ranges),
        in_specs=[IN_HBM, IN_HBM, IN_VMEM if near else IN_HBM],
        out_specs=tuple([IN_VMEM] * len(ranges)),
        scratch_shapes=scratch,
        compiler_params=pltpu.CompilerParams(
            vmem_limit_bytes=2 * MIB + staged + (2 * units * width if near else 0)
        ),
        cost_estimate=cost(8),
        name="load",
    )(token, keep_in_hbm(far_rows), near_rows if near else keep_in_hbm(near_rows))


def flat_rows(blocks):
    return jnp.concatenate(
        [blocks[chip].astype(jnp.float32) for chip in range(blocks.shape[0])], axis=0
    )


def one_hot(rows, columns):
    return jnp.where(rows == columns, 1.0, 0.0).astype(jnp.bfloat16)


def differ(mask):
    here = lax.rem(lax.axis_index("tensor"), SIDES)
    low = lax.rem(lax.rem(mask, 2) + lax.rem(here, 2), 2)
    high = lax.rem(mask // 2 + here // 2, 2)
    return 2 * high + low


def mask_of(core, place):
    result = jnp.zeros_like(place)
    for index in range(SIDES - 1):
        mask = jnp.where(core == 0, MASKS[0][index], MASKS[1][index])
        result = jnp.where(place == index + 1, mask, result)
    return result


def place_of(core, mask):
    result = jnp.zeros_like(mask)
    for index in range(SIDES - 1):
        held = jnp.where(core == 0, MASKS[0][index], MASKS[1][index])
        result = jnp.where(mask == held, index + 1, result)
    return result


def slot_matrix(slots, places):
    return one_hot(lax.broadcasted_iota(jnp.int32, (places, slots.shape[1]), 0), slots[...])


def prepare_kernel(
    slot_count,
    slots,
    lengths,
    frequency,
    packing,
    unpacking,
    first,
    last,
    cosine,
    sine,
):
    places, requests = packing.shape
    owners = places // slot_count
    core = lax.axis_index("pool")
    natural = slot_matrix(slots, places)
    row = lax.broadcasted_iota(jnp.int32, (requests, requests), 0)
    column = lax.broadcasted_iota(jnp.int32, (requests, requests), 1)
    half_first = one_hot(lax.rem(column + core * (requests // 2), requests), row)
    packing[...] = dot_rows(natural, half_first).astype(jnp.bfloat16)
    half, block, local = requests // 2, requests // 2 // SIDES, requests // owners
    half_of = lax.rem(row // half + core, 2)
    side = differ(mask_of(half_of, lax.rem(row, half) // block))
    inner = lax.rem(row, local)
    source = half_of * half + (lax.rem(row, block) // local * SIDES + side) * local + inner
    unpacking[...] = dot_columns(one_hot(source, column), natural).astype(jnp.bfloat16)
    start = lax.axis_index(("pool", "tensor")) * slot_count
    place = slots[...] - start
    rows = lax.broadcasted_iota(jnp.int32, (slot_count, requests), 0)
    amounts = lengths[...].astype(jnp.float32)
    length = jnp.sum(jnp.where(place == rows, amounts, 0.0), axis=1, keepdims=True)
    offset = jnp.sum(
        jnp.where((place >= 0) & (place < rows), amounts, 0.0), axis=1, keepdims=True
    )
    angles = length * frequency[...]
    turn = jnp.sin(angles)
    lean = jnp.cos(angles)
    cosine[...] = jnp.concatenate([lean, lean], axis=1)
    sine[...] = jnp.concatenate([-turn, turn], axis=1)
    first[...] = jnp.broadcast_to(offset.astype(jnp.int32), first.shape)
    last[...] = jnp.broadcast_to((offset + length).astype(jnp.int32), last.shape)


def prepare(slot_count, devices, head_dim, slots, lengths):
    requests = slots.shape[0]
    places = devices * slot_count
    frequency = theta ** (-jnp.arange(head_dim // 2, dtype=jnp.float32) * 2.0 / head_dim)
    table = jax.ShapeDtypeStruct((slot_count, head_dim), jnp.float32)
    bound = jax.ShapeDtypeStruct((slot_count, head_dim), jnp.int32)
    return pl.pallas_call(
        functools.partial(prepare_kernel, slot_count),
        out_shape=(
            jax.ShapeDtypeStruct((places, requests), jnp.bfloat16),
            jax.ShapeDtypeStruct((requests, places), jnp.bfloat16),
            bound,
            bound,
            table,
            table,
        ),
        in_specs=[IN_VMEM] * 3,
        out_specs=tuple([IN_VMEM] * 6),
        compiler_params=pltpu.CompilerParams(vmem_limit_bytes=MIB),
        cost_estimate=cost(8),
        name="prepare",
    )(
        slots.reshape(1, -1),
        lengths.reshape(1, -1),
        frequency.reshape(1, -1),
    )


def project_kernel(slot_count, own, other, gain, packing, q_vm, k_vm, v_vm, out, normed):
    half = own.shape[0] * own.shape[1]
    for index, source in enumerate((own, other)):
        rows = flat_rows(source)
        scale = lax.rsqrt(jnp.mean(rows * rows, axis=-1, keepdims=True) + eps)
        normed[pl.ds(index * half, half), :] = (rows * scale * gain[...]).astype(jnp.bfloat16)
    query_part = dot_rows(normed[...], q_vm[...])
    key_part = dot_columns(normed[...], k_vm[...])
    value_part = dot_columns(normed[...], v_vm[...])
    projected = jnp.concatenate([query_part, key_part, value_part], axis=1).astype(jnp.bfloat16)
    packed = dot_rows(packing[...], projected)
    for owner in range(out.shape[0]):
        out[owner] = packed[owner * slot_count : (owner + 1) * slot_count, :].astype(jnp.bfloat16)


def project(slot_count, own, other, gain, packing, weights):
    depth, query_cols = weights[0].shape
    width = query_cols + weights[1].shape[0] + weights[2].shape[0]
    places, requests = packing.shape
    return pl.pallas_call(
        functools.partial(project_kernel, slot_count),
        out_shape=jax.ShapeDtypeStruct((places // slot_count, slot_count, width), jnp.bfloat16),
        in_specs=[IN_VMEM] * 7,
        out_specs=IN_VMEM,
        scratch_shapes=[pltpu.VMEM((requests, depth), jnp.bfloat16)],
        compiler_params=pltpu.CompilerParams(vmem_limit_bytes=8 * MIB),
        cost_estimate=cost(32),
        name="project",
    )(
        own,
        other,
        gain.reshape(1, depth),
        packing,
        *weights,
    )


def attend_kernel(
    query_cols,
    key_cols,
    arrived,
    first,
    last,
    cosine,
    sine,
    query_gain,
    key_gain,
    keys,
    values,
    out,
    queries,
    scores,
):
    devices, slot_count, _ = arrived.shape
    tokens, width = keys.shape
    head_dim = query_gain.shape[1]
    kv_count = devices * key_cols // head_dim
    sharers = devices // kv_count
    heads_here = query_cols // head_dim
    repeats = sharers * heads_here
    count = repeats * slot_count
    parts = pieces(tokens, TOKEN_STEP)
    scale_factor = 1.0 / math.sqrt(head_dim)

    def tile(rows, times):
        return jnp.concatenate([rows] * times, axis=0)

    def prepare(rows, gain, times):
        rows = rows * lax.rsqrt(jnp.mean(rows * rows, axis=-1, keepdims=True) + eps) * gain[...]
        turned = pltpu.roll(rows, head_dim // 2, 1)
        return (rows * tile(cosine[...], times) + turned * tile(sine[...], times)).astype(
            jnp.bfloat16
        )

    blocks = [arrived[device].astype(jnp.float32) for device in range(devices)]
    rows = jnp.concatenate(
        [
            blocks[kv * sharers + place][:, head * head_dim : (head + 1) * head_dim]
            for kv in range(kv_count)
            for head in range(heads_here)
            for place in range(sharers)
        ],
        axis=0,
    )
    query = prepare(rows, query_gain, kv_count * repeats)

    def whole(begin):
        return [
            jnp.concatenate(
                [
                    blocks[kv * sharers + place][:, begin : begin + key_cols]
                    for place in range(sharers)
                ],
                axis=1,
            )
            for kv in range(kv_count)
        ]

    fresh = prepare(jnp.concatenate(whole(query_cols), axis=0), key_gain, kv_count)
    fresh = fresh.astype(jnp.float32)
    key_new = jnp.concatenate(
        [
            tile(fresh[kv * slot_count : (kv + 1) * slot_count, :], repeats)
            for kv in range(kv_count)
        ],
        axis=0,
    )
    value_new = [tile(rows, repeats) for rows in whole(query_cols + key_cols)]
    own_score = (
        jnp.sum(query.astype(jnp.float32) * key_new, axis=-1, keepdims=True) * scale_factor
    )
    queries[...] = jnp.zeros(queries.shape, queries.dtype)
    for kv in range(kv_count):
        queries[kv * count : (kv + 1) * count, kv * head_dim : (kv + 1) * head_dim] = query[
            kv * count : (kv + 1) * count, :
        ]
    start = tile(first[:, :1], kv_count * repeats)
    end = tile(last[:, :1], kv_count * repeats)
    largest = own_score
    for begin, size in parts:
        positions = lax.broadcasted_iota(jnp.int32, (kv_count * count, size), 1) + begin
        inside = (positions >= start) & (positions < end)
        part = dot_columns(queries[...], keys[begin : begin + size, :]) * scale_factor
        part = jnp.where(inside, part, -1e30)
        scores[:, begin : begin + size] = part
        largest = jnp.maximum(largest, jnp.max(part, axis=1, keepdims=True))
    own_weight = jnp.exp(own_score - largest)
    denominator = own_weight
    summed = jnp.zeros((kv_count * count, width), jnp.float32)
    for begin, size in parts:
        weights = jnp.exp(scores[:, begin : begin + size] - largest)
        denominator = denominator + jnp.sum(weights, axis=1, keepdims=True)
        summed = summed + dot_rows(
            weights.astype(jnp.bfloat16), values[begin : begin + size, :]
        )
    own_low = own_weight.astype(jnp.bfloat16).astype(jnp.float32)
    for kv in range(kv_count):
        span = slice(kv * count, (kv + 1) * count)
        mine = summed[span, kv * head_dim : (kv + 1) * head_dim]
        mine = (mine + own_low[span, :] * value_new[kv]) / denominator[span, :]
        for head in range(heads_here):
            for place in range(sharers):
                row = (head * sharers + place) * slot_count
                out[kv * sharers + place, :, head * head_dim : (head + 1) * head_dim] = mine[
                    row : row + slot_count, :
                ].astype(jnp.bfloat16)


def attend(arrived, planned, query_gain, key_gain, key_cache, value_cache, query_cols):
    devices, slot_count, width = arrived.shape
    key_cols = (width - query_cols) // 2
    head_dim = query_gain.shape[0]
    tokens, cache_width = key_cache.shape
    rows = devices * query_cols // head_dim * slot_count
    return pl.pallas_call(
        functools.partial(attend_kernel, query_cols, key_cols),
        out_shape=jax.ShapeDtypeStruct((devices, slot_count, query_cols), jnp.bfloat16),
        in_specs=[IN_VMEM] * 9,
        out_specs=IN_VMEM,
        scratch_shapes=[
            pltpu.VMEM((rows, cache_width), jnp.bfloat16),
            pltpu.VMEM((rows, tokens), jnp.float32),
        ],
        compiler_params=pltpu.CompilerParams(vmem_limit_bytes=16 * MIB),
        name="attend",
    )(
        arrived,
        *planned,
        query_gain.reshape(1, head_dim),
        key_gain.reshape(1, head_dim),
        key_cache,
        value_cache,
    )


def mix_kernel(returned, unpacking, weight, hidden, near_out, far_out, other_out):
    owners = returned.shape[0]
    block, width = near_out.shape
    local = hidden.shape[0]
    group = lax.axis_index("tensor") // SIDES
    by_slot = jnp.concatenate(
        [returned[owner].astype(jnp.float32) for owner in range(owners)], axis=0
    ).astype(jnp.bfloat16)
    rows = dot_rows(unpacking[...], by_slot).astype(jnp.bfloat16)
    for start, size in pieces(width, 1024):
        columns = slice(start, start + size)
        total = dot_rows(rows, weight[:, columns])
        residual = hidden[:, columns].astype(jnp.float32)
        near_out[:, columns] = total[:block] + jnp.concatenate(
            [jnp.where(group == index, residual, 0.0) for index in range(block // local)], axis=0
        )
        for side in range(SIDES):
            row = side * block
            if side:
                far_out[side - 1, :, columns] = total[row : row + block]
            row += SIDES * block
            other_out[side, :, columns] = total[row : row + block].astype(other_out.dtype)


def mix(returned, unpacking, output_weight, hidden):
    block, width = unpacking.shape[0] // 2 // SIDES, output_weight.shape[1]
    return pl.pallas_call(
        mix_kernel,
        out_shape=(
            jax.ShapeDtypeStruct((block, width), jnp.float32),
            jax.ShapeDtypeStruct((SIDES - 1, block, width), jnp.float32),
            jax.ShapeDtypeStruct((SIDES, block, width), jnp.bfloat16),
        ),
        in_specs=[IN_VMEM] * 4,
        out_specs=(IN_VMEM, IN_VMEM, IN_VMEM),
        compiler_params=pltpu.CompilerParams(vmem_limit_bytes=8 * MIB),
        name="mix",
    )(returned, unpacking, output_weight, hidden)


def stack_kernel(*refs):
    out = refs[-1]
    for index, ref in enumerate(refs[:-1]):
        out[index] = ref[...]


def stack(blocks):
    shape = (len(blocks),) + blocks[0].shape
    return pl.pallas_call(
        stack_kernel,
        out_shape=jax.ShapeDtypeStruct(shape, blocks[0].dtype),
        in_specs=[IN_VMEM] * len(blocks),
        out_specs=IN_VMEM,
        compiler_params=pltpu.CompilerParams(vmem_limit_bytes=2 * MIB),
        name="stack",
    )(*blocks)


def renew_kernel(own, partner, gain, mixed, normed):
    local = mixed.shape[0]
    total = own[...].astype(jnp.float32) + partner[...].astype(jnp.float32)
    rows = total.astype(jnp.bfloat16).astype(jnp.float32)
    scale = lax.rsqrt(jnp.mean(rows * rows, axis=-1, keepdims=True) + eps)
    normed[...] = (rows * scale * gain[...]).astype(jnp.bfloat16)
    group = lax.axis_index("tensor") // SIDES
    here = rows[:local]
    for index in range(1, rows.shape[0] // local):
        here = jnp.where(group == index, rows[index * local : (index + 1) * local], here)
    mixed[...] = here.astype(jnp.bfloat16)


def renew(own, partner, gain, local):
    return pl.pallas_call(
        renew_kernel,
        out_shape=(
            pltpu.VMEM((local, own.shape[1]), jnp.bfloat16),
            jax.ShapeDtypeStruct(own.shape, jnp.bfloat16),
        ),
        in_specs=[IN_VMEM] * 3,
        out_specs=(IN_VMEM, IN_VMEM),
        compiler_params=pltpu.CompilerParams(vmem_limit_bytes=4 * MIB),
        name="renew",
    )(own, partner, gain.reshape(1, -1))


def settle_kernel(rows, out):
    out[...] = rows[...]


def settle(rows):
    return pl.pallas_call(
        settle_kernel,
        out_shape=jax.ShapeDtypeStruct(rows.shape, rows.dtype),
        in_specs=[IN_VMEM],
        out_specs=IN_VMEM,
        compiler_params=pltpu.CompilerParams(vmem_limit_bytes=MIB),
        cost_estimate=cost(4),
        name="settle",
    )(keep_in_vmem(rows))


def feed_kernel(spans, local, *refs):
    halves, weights = refs[:2], refs[2 : 2 + len(spans)]
    down, own_out, other_out, rows = refs[2 + len(spans) :]
    half, width = own_out.shape
    block = half // SIDES

    def part(array, start, size):
        for (index, begin, end), ref in zip(spans, weights):
            if index == array and begin <= start and start + size <= end:
                span = slice(start - begin, start - begin + size)
                return ref[span, :]

    for index, blocks in enumerate(halves):
        rows[index * half : (index + 1) * half, :] = flat_rows(blocks).astype(jnp.bfloat16)
    gate_part = up_part = 0.0
    for start, size in pieces(width, FEED_STEP):
        some = rows[:, start : start + size]
        gate_part = gate_part + dot_rows(some, part(0, start, size))
        up_part = up_part + dot_rows(some, part(1, start, size))
    active = (gate_part / (1.0 + jnp.exp(-gate_part)) * up_part).astype(jnp.bfloat16)
    row = lax.broadcasted_iota(jnp.int32, (2 * half, 2 * half), 0)
    chip = lax.rem(row, half) // local
    inner = lax.rem(row, local)
    core = lax.rem(row // half + lax.axis_index("pool"), 2)
    place = place_of(core, differ(lax.rem(chip, SIDES)))
    source = row // half * half + place * block + chip // SIDES * local + inner
    order = one_hot(source, lax.broadcasted_iota(jnp.int32, (2 * half, 2 * half), 1))
    active = dot_rows(order, active).astype(jnp.bfloat16)
    for start, size in pieces(width, FEED_STEP):
        total = dot_rows(active, down[:, start : start + size])
        own_out[:, start : start + size] = total[:half]
        other_out[:, start : start + size] = total[half:].astype(other_out.dtype)


def feed(halves, spans, weights, down_weight, local):
    _, block, width = halves[0].shape
    half = SIDES * block
    return pl.pallas_call(
        functools.partial(feed_kernel, spans, local),
        out_shape=(
            jax.ShapeDtypeStruct((half, width), jnp.float32),
            jax.ShapeDtypeStruct((half, width), jnp.bfloat16),
        ),
        in_specs=[IN_VMEM] * (3 + len(spans)),
        out_specs=(IN_VMEM, IN_VMEM),
        scratch_shapes=[pltpu.VMEM((2 * half, width), jnp.bfloat16)],
        compiler_params=pltpu.CompilerParams(vmem_limit_bytes=16 * MIB),
        name="feed",
    )(*halves, *[keep_in_vmem(weight) for weight in weights], down_weight)


def on_device_kernels(
    hidden,
    input_gain,
    query_weight,
    key_weight,
    value_weight,
    query_gain,
    key_gain,
    output_weight,
    post_gain,
    gate_weight,
    up_weight,
    down_weight,
    key_cache,
    value_cache,
    lengths,
    request_slot,
):
    devices = lax.axis_size(("pool", "tensor"))
    chips = lax.axis_size("tensor")
    local, width = hidden.shape
    slot_count = SLOTS
    query_cols = query_weight.shape[1]
    head_dim = query_gain.shape[0]
    own = gather_half(hidden, chips, gate_weight.T)
    packing, unpacking, *planned = prepare(
        slot_count, devices, head_dim, request_slot, lengths
    )
    other = swap_cores(own)
    weights = (query_weight, key_weight.T, value_weight.T)
    outgoing = project(slot_count, own, other, input_gain, packing, weights)
    head_out = attend(
        swap_all(outgoing), planned, query_gain, key_gain, key_cache, value_cache, query_cols
    )
    returned = swap_all(head_out)
    near_sum, far_sum, other_sum = mix(returned, unpacking, output_weight, hidden)

    gate_rows, up_rows = gate_weight.T, up_weight.T
    columns = width // STEP
    steps = chips.bit_length() - 3
    far = split_range(columns, [4] + [6] * steps + [0, 0])
    near = split_range(columns, [0] + [0] * steps + [7, 3])
    spans, fetched = [], []

    def beside_load(exchange, blocks):
        group = len(fetched)
        token = jax.tree.leaves(blocks)[0]
        parts = load(far[group], near[group], token, gate_rows, up_rows)
        blocks, parts = lax.optimization_barrier((exchange(blocks), parts))
        for array, span in enumerate((far[group], near[group])):
            if span:
                spans.append((array,) + span)
        fetched.append(parts)
        return blocks

    def plus(left, right):
        return left.astype(jnp.float32) + right.astype(jnp.float32)

    from_core = swap_cores(other_sum)
    far_sums = plus(far_sum, from_core[1:]).astype(jnp.bfloat16)
    from_sides = beside_load(trade, [far_sums[index] for index in range(SIDES - 1)])
    total = plus(near_sum, from_core[0])
    for block in from_sides:
        total = plus(total, block)
    total = total.astype(jnp.bfloat16)
    mask = SIDES
    while 2 * mask < chips:
        partner = beside_load(lambda block: swap_partners(block, mask), total)
        total = plus(total, partner).astype(jnp.bfloat16)
        mask *= 2
    partner = beside_load(lambda block: swap_partners(block, mask), total)
    mixed_rows, normed = renew(total, partner, post_gain, local)
    held = settle(mixed_rows)
    sides, held = lax.optimization_barrier((beside_load(trade, [normed] * (SIDES - 1)), held))
    own = stack([normed] + sides)
    halves = (own, beside_load(swap_cores, own))
    own_sum, other_sum = feed(
        halves, spans, [array for parts in fetched for array in parts], down_weight, local
    )
    lowered = scatter_halves(own_sum, other_sum, chips)
    final_rows = (mixed_rows.astype(jnp.float32) + lowered).astype(jnp.bfloat16)
    return (held, final_rows)


def gather_rows(rows, devices):
    copies = jnp.broadcast_to(rows[None], (devices,) + rows.shape)
    arrived = lax.all_to_all(copies, ("pool", "tensor"), split_axis=0, concat_axis=0, tiled=True)
    return arrived.reshape(devices * rows.shape[0], rows.shape[1])


def scatter_sum(partial, devices):
    blocks = partial.astype(jnp.bfloat16).reshape(devices, -1, partial.shape[1])
    arrived = lax.all_to_all(blocks, ("pool", "tensor"), split_axis=0, concat_axis=0, tiled=True)
    return jnp.sum(arrived.astype(jnp.float32), axis=0)


def on_device_general(
    hidden,
    input_gain,
    query_weight,
    key_weight,
    value_weight,
    query_gain,
    key_gain,
    output_weight,
    post_gain,
    gate_weight,
    up_weight,
    down_weight,
    key_cache,
    value_cache,
    lengths,
    request_slot,
):
    devices = lax.axis_size(("pool", "tensor"))
    device_index = lax.axis_index(("pool", "tensor"))
    local_rows = hidden.shape[0]
    query_cols = query_weight.shape[1]
    key_cols = key_weight.shape[1]
    width_sent = query_cols + 2 * key_cols
    head_dim = query_gain.shape[0]
    slot_count = SLOTS
    head_count = devices * query_cols // head_dim
    kv_count = devices * key_cols // head_dim
    group_size = head_count // kv_count
    normed = rms_scale(hidden, input_gain).astype(jnp.bfloat16)
    shard_rows = gather_rows(normed, devices)
    query_part = jnp.dot(shard_rows, query_weight, preferred_element_type=jnp.float32)
    key_part = jnp.dot(shard_rows, key_weight, preferred_element_type=jnp.float32)
    value_part = jnp.dot(shard_rows, value_weight, preferred_element_type=jnp.float32)
    projected = jnp.concatenate([query_part, key_part, value_part], axis=1).astype(jnp.bfloat16)
    outgoing = (
        jnp.zeros((devices * slot_count, width_sent), jnp.bfloat16).at[request_slot].set(projected)
    )
    outgoing = outgoing.reshape(devices, slot_count, width_sent)
    arrived = lax.all_to_all(
        outgoing, ("pool", "tensor"), split_axis=0, concat_axis=2, tiled=True
    ).reshape(slot_count, devices, width_sent)
    query_full = arrived[:, :, :query_cols].reshape(slot_count, head_count, head_dim)
    key_full = arrived[:, :, query_cols : query_cols + key_cols].reshape(
        slot_count, kv_count, head_dim
    )
    value_new = arrived[:, :, query_cols + key_cols :].reshape(slot_count, kv_count, head_dim)
    slot_ids = device_index * slot_count + jnp.arange(slot_count, dtype=jnp.int32)
    matches = request_slot[None, :] == slot_ids[:, None]
    slot_length = jnp.sum(jnp.where(matches, lengths[None, :], 0), axis=1)
    owner_of = request_slot // slot_count
    within = request_slot % slot_count
    earlier = (owner_of[None, :] == device_index) & (
        within[None, :] < jnp.arange(slot_count, dtype=jnp.int32)[:, None]
    )
    slot_offset = jnp.sum(jnp.where(earlier, lengths[None, :], 0), axis=1)
    position = slot_length.astype(jnp.float32)[:, None, None]
    query_heads = rotate(rms_scale(query_full, query_gain), position).astype(jnp.bfloat16)
    query_heads = query_heads.reshape(slot_count, kv_count, group_size, head_dim)
    key_new = rotate(rms_scale(key_full, key_gain), position).astype(jnp.bfloat16)
    pool_tokens = key_cache.shape[0]
    scale_factor = 1.0 / math.sqrt(head_dim)
    scores = jnp.stack(
        [
            jnp.einsum(
                "sgd,td->sgt",
                query_heads[:, kv],
                key_cache[:, kv * head_dim : (kv + 1) * head_dim],
                preferred_element_type=jnp.float32,
            )
            for kv in range(kv_count)
        ],
        axis=1,
    ) * scale_factor
    own_score = (
        jnp.einsum("skgd,skd->skg", query_heads, key_new, preferred_element_type=jnp.float32)
        * scale_factor
    )
    token_pos = jnp.arange(pool_tokens, dtype=jnp.int32)
    inside = (token_pos[None, :] >= slot_offset[:, None]) & (
        token_pos[None, :] < (slot_offset + slot_length)[:, None]
    )
    inside = inside[:, None, None, :]
    largest = jnp.maximum(jnp.max(jnp.where(inside, scores, -1e30), axis=3), own_score)
    weights = jnp.where(inside, jnp.exp(scores - largest[..., None]), 0.0)
    own_weight = jnp.exp(own_score - largest)
    denominator = jnp.sum(weights, axis=3) + own_weight
    weights_low = weights.astype(jnp.bfloat16)
    summed = jnp.stack(
        [
            jnp.einsum(
                "sgt,td->sgd",
                weights_low[:, kv],
                value_cache[:, kv * head_dim : (kv + 1) * head_dim],
                preferred_element_type=jnp.float32,
            )
            for kv in range(kv_count)
        ],
        axis=1,
    )
    own_low = own_weight.astype(jnp.bfloat16).astype(jnp.float32)
    summed = summed + own_low[..., None] * value_new.astype(jnp.float32)[:, :, None, :]
    head_out = (
        (summed / denominator[..., None])
        .astype(jnp.bfloat16)
        .reshape(slot_count, devices, query_cols)
    )
    returned = lax.all_to_all(head_out, ("pool", "tensor"), split_axis=1, concat_axis=0, tiled=True)
    head_rows = returned.reshape(devices * slot_count, query_cols)[request_slot]
    partial_value = jnp.dot(head_rows, output_weight, preferred_element_type=jnp.float32)
    mixed_rows = (hidden.astype(jnp.float32) + scatter_sum(partial_value, devices)).astype(jnp.bfloat16)
    post_normed = gather_rows(rms_scale(mixed_rows, post_gain).astype(jnp.bfloat16), devices)
    gate_part = jnp.dot(post_normed, gate_weight, preferred_element_type=jnp.float32)
    up_part = jnp.dot(post_normed, up_weight, preferred_element_type=jnp.float32)
    activated = (jax.nn.silu(gate_part) * up_part).astype(jnp.bfloat16)
    lowered = scatter_sum(
        jnp.dot(activated, down_weight, preferred_element_type=jnp.float32), devices
    )
    final_rows = (mixed_rows.astype(jnp.float32) + lowered).astype(jnp.bfloat16)
    return (mixed_rows, final_rows)


def on_device(*arrays):
    query_cols, key_cols = arrays[2].shape[1], arrays[3].shape[1]
    head_dim = arrays[5].shape[0]
    devices = lax.axis_size(("pool", "tensor"))
    kv_count = devices * key_cols // head_dim
    whole_heads = query_cols % head_dim == 0 and head_dim % LANES == 0
    shared = kv_count > 0 and devices % kv_count == 0
    chips = lax.axis_size("tensor")
    pairs = lax.axis_size("pool") == 2 and chips >= 2 * SIDES and chips & (chips - 1) == 0
    pairs = pairs and arrays[14].shape[0] % 32 == 0
    if whole_heads and shared and pairs:
        return on_device_kernels(*arrays)
    return on_device_general(*arrays)


def solution(mesh):
    placed = (
        P(("groups", "pool", "tensor"), None),
        P(),
        P(None, ("pool", "tensor")),
        P(None, ("pool", "tensor")),
        P(None, ("pool", "tensor")),
        P(),
        P(),
        P(("pool", "tensor"), None),
        P(),
        P(None, ("pool", "tensor")),
        P(None, ("pool", "tensor")),
        P(("pool", "tensor"), None),
        P(("groups", "pool", "tensor"), None),
        P(("groups", "pool", "tensor"), None),
        P("groups"),
        P("groups"),
    )
    return jax.shard_map(
        on_device,
        mesh=mesh,
        in_specs=placed,
        out_specs=(P(("groups", "pool", "tensor"), None), P(("groups", "pool", "tensor"), None)),
        check_vma=False,
    )
```
